256 devices in a mesh: dp: 16 (over x, z_hi), frame: 16 (over y, z_lo, core).
Axes of the slice: x: 4, y: 4, z: 8 (z_hi: 4, z_lo: 2; z = z_hi * 2 + z_lo), core: 2. Of those that a mesh axis runs over, the one named last changes fastest.
Arguments:
- video: bfloat16 [32, 16, 256, 1024], P('dp', 'frame'), may hold values from -96 to 96
- cotangent: bfloat16 [32, 16, 256, 1024], P('dp', 'frame'), may hold values from -6 to 6
- norm_gain: float32 [1024], replicated, may hold values from 0.1 to 1.9
- norm_bias: float32 [1024], replicated, may hold values from -3 to 3
- qkv_weight: bfloat16 [1024, 3072], replicated, may hold values from -1 to 1
- out_weight: bfloat16 [1024, 1024], replicated, may hold values from -0.1875 to 0.1875
Outputs:
- grad_video: bfloat16 [32, 16, 256, 1024], P('dp', 'frame')
- grad_qkv: float32 [1024, 3072], P('frame')
- grad_out: float32 [1024, 1024], P('frame')
- grad_gain: float32 [1024], P('frame')
- grad_bias: float32 [1024], P('frame')
The draws below stay inside these ranges and needn't reach their ends.
All inputs are finite; a program needn't handle non-finite values.
Results may differ from the reference program's by a relative error of at most 0.004.
The reference program's roundings to bfloat16 on the way count: a program that leaves them out, or rounds other values in their place, can miss the bound.
Values may be sent and summed in bfloat16 or wider, within the bound.
No kernel may reach another device: no remote copies, remote signals or barrier semaphores. Data moves between devices by JAX's collectives and lax.ppermute only.
A program may use at most 128 MiB of HBM per device.

```python
import math
import jax
import jax.numpy as jnp
from jax import lax

D = 1024
HEADS = 16
HEAD_DIM = 64
P_SIZE = 256
FRAMES = 16
CLIPS = 32
TOKENS = 131072


def draw_video(key, part):
    key = jax.random.fold_in(key, 11)
    key_noise, key_rows, key_cols = jax.random.split(key, 3)
    shape = (CLIPS, FRAMES, P_SIZE, D)
    col_scale = jnp.exp(jax.random.uniform(key_cols, (D,), jnp.float32, math.log(0.3), math.log(3.0)))
    row_scale = jnp.exp(jax.random.uniform(key_rows, (CLIPS, FRAMES, P_SIZE, 1), jnp.float32, 0.0, math.log(10.0)))
    values = jax.random.normal(key_noise, shape, jnp.float32) * col_scale * row_scale
    return jnp.clip(values, -96.0, 96.0).astype(jnp.bfloat16)


def draw_qkv_weight(key, part):
    key = jax.random.fold_in(key, 23)
    key_base = jax.random.fold_in(key, 0)
    values = jax.random.normal(key_base, (D, 3 * D), jnp.float32) * D ** (-0.5)
    return jnp.clip(values, -1.0, 1.0).astype(jnp.bfloat16)


def shard_levels(rng, extent, cuts, smallest, top_value):
    level = 1.0
    for dim, blocks in cuts:
        steps = jax.random.uniform(jax.random.fold_in(jax.random.fold_in(rng, 6), dim), (blocks,), jnp.float32, smallest / len(cuts), top_value / len(cuts))
        level = level * jnp.repeat(jnp.exp(steps), extent[dim] // blocks).reshape((-1,) + (1,) * (len(extent) - 1 - dim))
    return level


def centred(stream_key, shape, width, limit, pieces=(), held_as=jnp.bfloat16):
    gain = shard_levels(stream_key, shape, pieces, -0.22, 0.18) if pieces else 1.0
    values = jax.random.normal(stream_key, shape, jnp.float32) * width * gain
    return jnp.minimum(jnp.maximum(values, -limit), limit).astype(held_as)


def setup_inputs(seed: int = 0) -> dict:
    streams_of = jax.random.split(jax.random.key(seed), 7)
    return {
        "video": draw_video(jax.random.fold_in(streams_of[6], 71), 0),
        "cotangent": centred(streams_of[1], (CLIPS, FRAMES, P_SIZE, D), 1.0, 6.0, ((0, 16), (1, 16))),
        "norm_gain": jnp.clip(1.0 + 0.18 * jax.random.normal(streams_of[2], (D,), jnp.float32), 0.1, 1.9),
        "norm_bias": centred(streams_of[3], (D,), 0.5, 3.0, (), jnp.float32),
        "qkv_weight": draw_qkv_weight(jax.random.fold_in(streams_of[6], 71), 0),
        "out_weight": centred(streams_of[5], (D, D), D ** -0.5, 0.1875),
    }


def normalize(token_rows, norm_gain, norm_bias):
    values = token_rows.astype(jnp.float32)
    centered = values - lax.optimization_barrier(jnp.mean(values, axis=-1, keepdims=True))
    inv_std = lax.rsqrt(lax.optimization_barrier(jnp.mean(centered * centered, axis=-1, keepdims=True)) + 1e-05)
    whitened = centered * inv_std
    normed = (whitened * norm_gain + norm_bias).astype(jnp.bfloat16)
    return (normed, whitened, inv_std)

def head_block(packed, offset):
    column_block = packed[..., offset * D:(offset + 1) * D]
    return column_block.reshape(column_block.shape[:-1] + (HEADS, HEAD_DIM)).astype(jnp.float32)

def widen(low_value):
    return lax.optimization_barrier(low_value).astype(jnp.float32)

def attend_clip(packed):
    query_part = head_block(packed, 0)
    key_part = head_block(packed, 1)
    value_part = head_block(packed, 2)
    scores = jnp.einsum('flhd,glhd->lhfg', query_part, key_part) * HEAD_DIM ** (-0.5)
    attn_probs = jax.nn.softmax(scores, axis=-1)
    probs_low = widen(attn_probs.astype(jnp.bfloat16))
    mixed = jnp.einsum('lhfg,glhd->flhd', probs_low, value_part)
    attended = mixed.astype(jnp.bfloat16).reshape(packed.shape[:-1] + (D,))
    return (attended, attn_probs)

def back_clip(inputs):
    packed, attn_probs, d_attended = inputs
    query_part = head_block(packed, 0)
    key_part = head_block(packed, 1)
    value_part = head_block(packed, 2)
    grad_heads = d_attended.reshape(d_attended.shape[:-1] + (HEADS, HEAD_DIM)).astype(jnp.float32)
    probs_low = widen(attn_probs.astype(jnp.bfloat16))
    d_value = jnp.einsum('lhfg,flhd->glhd', probs_low, grad_heads).astype(jnp.bfloat16)
    d_probs = jnp.einsum('flhd,glhd->lhfg', grad_heads, value_part)
    inner = lax.optimization_barrier(jnp.sum(d_probs * attn_probs, axis=-1, keepdims=True))
    d_scores = widen((attn_probs * (d_probs - inner) * HEAD_DIM ** (-0.5)).astype(jnp.bfloat16))
    d_query = jnp.einsum('lhfg,glhd->flhd', d_scores, key_part).astype(jnp.bfloat16)
    d_key = jnp.einsum('lhfg,flhd->glhd', d_scores, query_part).astype(jnp.bfloat16)
    flat_shape = packed.shape[:-1] + (D,)
    return jnp.concatenate([d_query.reshape(flat_shape), d_key.reshape(flat_shape), d_value.reshape(flat_shape)], axis=-1)

def norm_back(d_normed, whitened, inv_std, norm_gain):
    scaled = d_normed * norm_gain
    first = lax.optimization_barrier(jnp.mean(scaled, axis=-1, keepdims=True))
    second = lax.optimization_barrier(jnp.mean(scaled * whitened, axis=-1, keepdims=True))
    return inv_std * (scaled - first - whitened * second)

def reference(video, cotangent, norm_gain, norm_bias, qkv_weight, out_weight):
    token_rows = video.reshape(-1, D)
    grad_rows = cotangent.reshape(-1, D)
    normed, whitened, inv_std = normalize(token_rows, norm_gain, norm_bias)
    packed = jnp.dot(normed, qkv_weight, preferred_element_type=jnp.float32).astype(jnp.bfloat16)
    packed = packed.reshape(CLIPS, FRAMES, P_SIZE, 3 * D)
    attended, attn_probs = lax.map(attend_clip, packed)
    attended_rows = attended.reshape(-1, D)
    grad_scale = 1.0 / math.sqrt(TOKENS)
    grad_out = jnp.dot(attended_rows.T, grad_rows, preferred_element_type=jnp.float32) * grad_scale
    d_attended = jnp.dot(grad_rows, out_weight.T, preferred_element_type=jnp.float32).astype(jnp.bfloat16)
    d_attended = d_attended.reshape(CLIPS, FRAMES, P_SIZE, D)
    d_packed = lax.map(back_clip, (packed, attn_probs, d_attended)).reshape(-1, 3 * D)
    grad_qkv = jnp.dot(normed.T, d_packed, preferred_element_type=jnp.float32) * grad_scale
    d_normed = jnp.dot(d_packed, qkv_weight.T, preferred_element_type=jnp.float32)
    grad_gain = lax.optimization_barrier(jnp.sum(d_normed * whitened, axis=0)) * grad_scale
    grad_bias = lax.optimization_barrier(jnp.sum(d_normed, axis=0)) * grad_scale
    grad_video = (grad_rows.astype(jnp.float32) + norm_back(d_normed, whitened, inv_std, norm_gain)).astype(jnp.bfloat16)
    return (grad_video.reshape(video.shape), grad_qkv, grad_out, grad_gain, grad_bias)
```

```python
import math

import jax
import jax.numpy as jnp
from jax import lax
from jax.experimental import pallas as pl
from jax.experimental.pallas import tpu as pltpu
from jax.sharding import PartitionSpec as P

F32 = jnp.float32
BF16 = jnp.bfloat16
MIB = 1024 * 1024


def dot_nn(a, b):
    return lax.dot_general(a, b, (((1,), (0,)), ((), ())), preferred_element_type=F32)


def dot_nt(a, b):
    return lax.dot_general(a, b, (((1,), (1,)), ((), ())), preferred_element_type=F32)


def dot_tn(a, b):
    return lax.dot_general(a, b, (((0,), (0,)), ((), ())), preferred_element_type=F32)


def main_kernel(
    tokens_ref, gain_ref, bias_ref, wqkv_ref, wout_ref,
    left_ref, right_ref, gv_ref, dgb_ref,
    normed_s, packed_s, datt_s, wh_s, inv_s, dn_s,
):
    clips, frames, positions, width = gv_ref.shape
    halves = positions // 8
    part = frames * 8
    rows = clips * frames * positions
    gain = gain_ref[...]
    bias = bias_ref[...]

    def norm_step(i, carry):
        c = i // (frames // 2)
        q = i % (frames // 2)
        x = tokens_ref[c, pl.ds(2 * q, 2)].astype(F32).reshape(2, halves, 8, width)
        g = tokens_ref[clips + c, pl.ds(2 * q, 2)].astype(F32).reshape(2, halves, 8, width)
        for h in range(halves):
            at = pl.multiple_of((c * halves + h) * part + q * 16, 16)
            xh = x[:, h].reshape(16, width)
            centred = xh - jnp.mean(xh, axis=-1, keepdims=True)
            inv = lax.rsqrt(jnp.mean(centred * centred, axis=-1, keepdims=True) + 1e-05)
            wh = centred * inv
            wh_s[pl.ds(at, 16), :] = wh
            inv_s[pl.ds(at, 16), :] = jnp.broadcast_to(inv, (16, 128))
            normed_s[pl.ds(at, 16), :] = (wh * gain + bias).astype(BF16)
            right_ref[pl.ds(at, 16), pl.ds(3 * width, width)] = g[:, h].reshape(16, width).astype(BF16)
        return carry

    lax.fori_loop(0, clips * frames // 2, norm_step, 0)

    def qkv_step(n, carry):
        cols = pl.ds(pl.multiple_of(n * 256, 256), 256)
        packed_s[:, cols] = dot_nn(normed_s[...], wqkv_ref[:, cols]).astype(BF16)
        return carry

    lax.fori_loop(0, 3 * width // 256, qkv_step, 0)

    def datt_step(n, carry):
        cols = pl.ds(pl.multiple_of(n * 256, 256), 256)
        datt_s[:, cols] = dot_nt(right_ref[:, pl.ds(3 * width, width)], wout_ref[cols, :]).astype(BF16)
        left_ref[0, cols, :] = normed_s[:, cols].T
        return carry

    lax.fori_loop(0, width // 256, datt_step, 0)

    lane = lax.broadcasted_iota(jnp.int32, (part, 128), 1)
    first = lane < 64
    same = lax.broadcasted_iota(jnp.int32, (1, 8, part), 1) == (
        lax.broadcasted_iota(jnp.int32, (1, 8, part), 2) % 8
    )
    zero = jnp.zeros((part, 128), BF16)

    def split(a):
        return jnp.concatenate([jnp.where(first, a, zero), jnp.where(first, zero, a)], axis=0)

    def attend_step(i, carry):
        t = i // (width // 128)
        hp = i % (width // 128)
        tok = pl.ds(pl.multiple_of(t * part, part), part)
        col = pl.multiple_of(hp * 128, 128)
        q = packed_s[tok, pl.ds(col, 128)]
        k = packed_s[tok, pl.ds(width + col, 128)]
        v = packed_s[tok, pl.ds(2 * width + col, 128)]
        da = datt_s[tok, pl.ds(col, 128)]
        k2 = split(k)
        v2 = split(v)
        scores = (dot_nt(k2, q) * 0.125).reshape(2, frames, 8, part)
        e = jnp.exp(scores - jnp.max(scores, axis=1, keepdims=True))
        probs = e * (1.0 / jnp.sum(e, axis=1, keepdims=True))
        probs = jnp.where(same[None], probs, 0.0)
        low = probs.astype(BF16).reshape(2, part, part)
        dp = dot_nt(v2, da).reshape(2, frames, 8, part)
        inner = jnp.sum(dp * probs, axis=1, keepdims=True)
        ds = (probs * (dp - inner) * 0.125).astype(BF16).reshape(2, part, part)
        left_ref[1, pl.ds(col, 128), tok] = dot_tn(v2, low.reshape(2 * part, part)).astype(BF16)
        right_ref[tok, pl.ds(col, 128)] = dot_tn(ds.reshape(2 * part, part), k2).astype(BF16)
        right_ref[tok, pl.ds(width + col, 128)] = dot_nn(
            jnp.concatenate([ds[0], ds[1]], axis=1), split(q)
        ).astype(BF16)
        right_ref[tok, pl.ds(2 * width + col, 128)] = dot_nn(
            jnp.concatenate([low[0], low[1]], axis=1), split(da)
        ).astype(BF16)
        return carry

    lax.fori_loop(0, clips * halves * (width // 128), attend_step, 0)

    def dn_step(n, carry):
        cols = pl.ds(pl.multiple_of(n * 256, 256), 256)
        dn_s[:, cols] = dot_nt(right_ref[:, pl.ds(0, 3 * width)], wqkv_ref[cols, :])
        return carry

    lax.fori_loop(0, width // 256, dn_step, 0)

    def back_step(i, carry):
        dgain, dbias = carry
        c = i // (frames // 2)
        q = i % (frames // 2)
        outs = []
        for h in range(halves):
            at = pl.multiple_of((c * halves + h) * part + q * 16, 16)
            dn = dn_s[pl.ds(at, 16), :]
            wh = wh_s[pl.ds(at, 16), :]
            inv = inv_s[pl.ds(at, 16), :][:, :1]
            dw = dn * wh
            dgain = dgain + dw[:8] + dw[8:]
            dbias = dbias + dn[:8] + dn[8:]
            scaled = dn * gain
            m1 = jnp.mean(scaled, axis=-1, keepdims=True)
            m2 = jnp.mean(scaled * wh, axis=-1, keepdims=True)
            gr = right_ref[pl.ds(at, 16), pl.ds(3 * width, width)].astype(F32)
            outs.append((gr + inv * (scaled - m1 - wh * m2)).reshape(2, 8, width))
        gv_ref[c, pl.ds(2 * q, 2)] = jnp.concatenate(outs, axis=1).astype(BF16)
        return dgain, dbias

    zeros = jnp.zeros((8, width), F32)
    dgain, dbias = lax.fori_loop(0, clips * frames // 2, back_step, (zeros, zeros))
    dgb_ref[0:1, :] = jnp.sum(dgain, axis=0, keepdims=True)
    dgb_ref[1:2, :] = jnp.sum(dbias, axis=0, keepdims=True)


def run_main(tokens, gain, bias, wqkv, wout):
    clips, frames, positions, width = tokens.shape
    clips = clips // 2
    rows = clips * frames * positions
    vm = pl.BlockSpec(memory_space=pltpu.VMEM)
    return pl.pallas_call(
        main_kernel,
        out_shape=(
            jax.ShapeDtypeStruct((2, width, rows), BF16),
            jax.ShapeDtypeStruct((rows, 4 * width), BF16),
            jax.ShapeDtypeStruct((clips, frames, positions, width), BF16),
            jax.ShapeDtypeStruct((2, width), F32),
        ),
        in_specs=[vm] * 5,
        out_specs=(vm,) * 4,
        scratch_shapes=[
            pltpu.VMEM((rows, width), BF16),
            pltpu.VMEM((rows, 3 * width), BF16),
            pltpu.VMEM((rows, width), BF16),
            pltpu.VMEM((rows, width), F32),
            pltpu.VMEM((rows, 128), F32),
            pltpu.VMEM((rows, width), F32),
        ],
        compiler_params=pltpu.CompilerParams(vmem_limit_bytes=40 * MIB),
        name="sublayer",
    )(tokens, gain.reshape(1, -1), bias.reshape(1, -1), wqkv, wout)


def grads_kernel(core_ref, left_ref, right_ref, send_ref, keep_ref):
    width, rows = left_ref.shape[1:]
    blocks, shard, cols = send_ref.shape
    core = core_ref[0]
    for b in range(4):
        per = width // 4
        g = dot_nn(left_ref[0, b * per:(b + 1) * per, :], right_ref[...])
        g = g.reshape(blocks // 4, 2, shard, cols)
        at = pl.ds(b * (blocks // 4), blocks // 4)
        mine = jnp.where(core == 0, g[:, 0], g[:, 1])
        other = jnp.where(core == 0, g[:, 1], g[:, 0])
        keep_ref[at] = mine
        send_ref[at] = other.astype(BF16)


def run_grads(core, left, right):
    _, width, rows = left.shape
    total = right.shape[1]
    n = 512
    blocks = width // 128
    return pl.pallas_call(
        grads_kernel,
        grid=(total // n,),
        out_shape=(
            jax.ShapeDtypeStruct((blocks, 64, total), BF16),
            jax.ShapeDtypeStruct((blocks, 64, total), F32),
        ),
        in_specs=[
            pl.BlockSpec(memory_space=pltpu.SMEM),
            pl.BlockSpec((1, width, rows), lambda i: (i // (3 * width // n), 0, 0)),
            pl.BlockSpec((rows, n), lambda i: (0, i)),
        ],
        out_specs=(
            pl.BlockSpec((blocks, 64, n), lambda i: (0, 0, i)),
            pl.BlockSpec((blocks, 64, n), lambda i: (0, 0, i)),
        ),
        compiler_params=pltpu.CompilerParams(vmem_limit_bytes=40 * MIB),
        name="weight_grads",
    )(core, left, right)


def frame_pairs(move):
    pairs = []
    for i in range(16):
        y, z, core = move(i // 4, i // 2 % 2, i % 2)
        pairs.append((i, y % 4 * 4 + z % 2 * 2 + core % 2))
    return pairs


def dp_pairs(move):
    pairs = []
    for i in range(16):
        x, h = move(i // 4, i % 4)
        pairs.append((i, x % 4 * 4 + h % 4))
    return pairs


def pick(array, index, axis):
    return lax.dynamic_index_in_dim(array, index, axis, keepdims=False)


def reduce_pieces(array, me, count, axis, name, pairs_of, dtype):
    total = pick(array, me, axis)
    got = []
    for k in range(1, count):
        piece = pick(array, (me + k) % count, axis).astype(dtype)
        got.append(lax.ppermute(piece, name, pairs_of(k)))
    for piece in got:
        total = total + piece.astype(F32)
    return total


def gather_pieces(piece, me, count, name, pairs_of):
    got = [piece]
    for k in range(1, count):
        got.append(lax.ppermute(piece, name, pairs_of(k)))
    stacked = jnp.stack(got)
    order = (me - jnp.arange(count)) % count
    return jnp.take(stacked, order, axis=0)


def step_y(k):
    return frame_pairs(lambda y, z, c: (y + k, z, c))


def step_z(k):
    return frame_pairs(lambda y, z, c: (y, z + k, c))


def step_x(k):
    return dp_pairs(lambda x, h: (x + k, h))


def step_h(k):
    return dp_pairs(lambda x, h: (x, h + k))


def reduce_grads(send, keep):
    frame = lax.axis_index("frame")
    dp = lax.axis_index("dp")
    y, z = frame // 4, frame // 2 % 2
    x, h = dp // 4, dp % 4
    cols = keep.shape[-1]
    half, part = cols // 2, cols // 8
    other = lax.ppermute(send, "frame", frame_pairs(lambda y, z, c: (y, z, 1 - c)))
    own = keep + other.astype(F32)
    own = own.reshape(4, 2, 64, cols)
    a = reduce_pieces(own[..., :half], y, 4, 0, "frame", step_y, BF16)
    b = reduce_pieces(own[..., half:].reshape(4, 2, 64, 4, part), x, 4, 3, "dp", step_x, BF16)
    a = reduce_pieces(a.reshape(2, 64, 4, part), x, 4, 2, "dp", step_x, F32)
    b = reduce_pieces(b, y, 4, 0, "frame", step_y, F32)
    both = jnp.concatenate([a, b], axis=-1)
    both = reduce_pieces(both, z, 2, 0, "frame", step_z, F32)
    both = reduce_pieces(both.reshape(4, 16, 2 * part), h, 4, 0, "dp", step_h, F32)
    both = gather_pieces(both, h, 4, "dp", step_h).reshape(64, 2 * part)
    both = gather_pieces(both, x, 4, "dp", step_x)
    both = both.reshape(4, 64, 2, part).transpose(1, 2, 0, 3)
    return both.reshape(64, cols)


def reduce_small(dgb):
    share = dgb.reshape(2, 16, 64).transpose(1, 0, 2).reshape(16, 1, 128)
    share = lax.all_to_all(share, "frame", 0, 0, tiled=True)
    share = jnp.sum(share, axis=0, keepdims=True)
    share = lax.all_to_all(jnp.broadcast_to(share, (16, 1, 128)), "dp", 0, 0, tiled=True)
    return jnp.sum(share, axis=0).reshape(2, 64)


def local(video, cotangent, norm_gain, norm_bias, qkv_weight, out_weight):
    clips, frames_here, positions, width = video.shape
    token_count = clips * positions * 256
    grad_scale = 1.0 / math.sqrt(token_count)
    tokens = jnp.concatenate([video, cotangent], axis=0)
    tokens = lax.all_to_all(tokens, "frame", split_axis=2, concat_axis=1, tiled=True)
    left, right, grad_video, dgb = run_main(tokens, norm_gain, norm_bias, qkv_weight, out_weight)
    grad_video = lax.all_to_all(grad_video, "frame", split_axis=1, concat_axis=2, tiled=True)
    core = (lax.axis_index("frame") % 2).reshape(1)
    send, keep = run_grads(core, left, right)
    total = reduce_grads(send, keep) * grad_scale
    small = reduce_small(dgb) * grad_scale
    return grad_video, total[:, : 3 * width], total[:, 3 * width :], small[0], small[1]


def solution(mesh):
    in_specs = (P("dp", "frame", None, None), P("dp", "frame", None, None), P(), P(), P(), P())
    out_specs = (
        P("dp", "frame", None, None),
        P("frame", None),
        P("frame", None),
        P("frame"),
        P("frame"),
    )
    return jax.shard_map(local, mesh=mesh, in_specs=in_specs, out_specs=out_specs, check_vma=False)
```

```python
import functools
import math

import jax
import jax.numpy as jnp
from jax import lax
from jax.experimental import pallas as pl
from jax.experimental.pallas import tpu as pltpu
from jax.sharding import PartitionSpec as P

F32 = jnp.float32
BF16 = jnp.bfloat16
MIB = 1024 * 1024
CHUNK = 512


def dot_nn(a, b):
    return lax.dot_general(a, b, (((1,), (0,)), ((), ())), preferred_element_type=F32)


def dot_nt(a, b):
    return lax.dot_general(a, b, (((1,), (1,)), ((), ())), preferred_element_type=F32)


def dot_tn(a, b):
    return lax.dot_general(a, b, (((0,), (0,)), ((), ())), preferred_element_type=F32)


def chunk(n):
    return pl.ds(pl.multiple_of(n * CHUNK, CHUNK), CHUNK)


def block_row(block, place):
    x, h, y, z, core = place
    dh = (block % 4 - h) % 4
    dcore = (block // 4 % 2 - core) % 2
    dz = (block // 8 % 2 - z) % 2
    dy = (block // 16 - y) % 4
    return pl.multiple_of((((dcore * 4 + dy) * 2 + dz) * 4 + dh) * 16, 16)


def read_place(place_ref):
    return tuple(place_ref[i] for i in range(5))


def whiten(xh):
    centred = xh - jnp.mean(xh, axis=-1, keepdims=True)
    inv = lax.rsqrt(jnp.mean(centred * centred, axis=-1, keepdims=True) + 1e-05)
    return centred * inv, inv


def main_kernel(
    place_ref, tokens_ref, gain_ref, bias_ref, wqkv_ref, wout_ref,
    send_hbm, keep_hbm, left_hbm, right_hbm,
    left_s, right_s, normed_s, packed_s, datt_s, send_s, keep_s, sems,
):
    place = read_place(place_ref)
    frames, clips, positions, width = tokens_ref.shape
    clips = clips // 2
    halves = positions // 8
    part = frames * 8
    gain = gain_ref[...]
    bias = bias_ref[...]

    def norm_step(i, carry):
        c = i // (frames // 2)
        q = i % (frames // 2)
        x = tokens_ref[pl.ds(2 * q, 2), c].astype(F32).reshape(2, halves, 8, width)
        g = tokens_ref[pl.ds(2 * q, 2), clips + c].astype(F32).reshape(2, halves, 8, width)
        for hf in range(halves):
            at = pl.multiple_of((c * halves + hf) * part + q * 16, 16)
            wh, _ = whiten(x[:, hf].reshape(16, width))
            normed_s[pl.ds(at, 16), :] = (wh * gain + bias).astype(BF16)
            right_s[pl.ds(at, 16), pl.ds(3 * width, width)] = g[:, hf].reshape(16, width).astype(BF16)
        return carry

    lax.fori_loop(0, clips * frames // 2, norm_step, 0)

    def qkv_step(n, carry):
        packed_s[:, chunk(n)] = dot_nn(normed_s[...], wqkv_ref[:, chunk(n)]).astype(BF16)
        return carry

    lax.fori_loop(0, 3 * width // CHUNK, qkv_step, 0, unroll=2)

    for n in range(width // CHUNK):
        cols = slice(n * CHUNK, (n + 1) * CHUNK)
        datt_s[:, cols] = dot_nt(right_s[:, 3 * width:], wout_ref[cols, :]).astype(BF16)
        turned = normed_s[:, cols].T
        for b in range(CHUNK // 16):
            at = block_row(n * (CHUNK // 16) + b, place)
            left_s[0, pl.ds(at, 16), :] = turned[b * 16:(b + 1) * 16]

    lane = lax.broadcasted_iota(jnp.int32, (part, 128), 1)
    first = lane < 64
    same = lax.broadcasted_iota(jnp.int32, (1, 8, part), 1) == (
        lax.broadcasted_iota(jnp.int32, (1, 8, part), 2) % 8
    )
    zero = jnp.zeros((part, 128), BF16)

    def split(a):
        return jnp.concatenate([jnp.where(first, a, zero), jnp.where(first, zero, a)], axis=0)

    def attend_step(i, carry):
        t = i // (width // 128)
        hp = i % (width // 128)
        tok = pl.ds(pl.multiple_of(t * part, part), part)
        col = pl.multiple_of(hp * 128, 128)
        q = packed_s[tok, pl.ds(col, 128)]
        k = packed_s[tok, pl.ds(width + col, 128)]
        v = packed_s[tok, pl.ds(2 * width + col, 128)]
        da = datt_s[tok, pl.ds(col, 128)]
        k2 = split(k)
        v2 = split(v)
        scores = (dot_nt(k2, q) * 0.125).reshape(2, frames, 8, part)
        e = jnp.exp(scores - jnp.max(scores, axis=1, keepdims=True))
        probs = e * (1.0 / jnp.sum(e, axis=1, keepdims=True))
        probs = jnp.where(same[None], probs, 0.0)
        low = probs.astype(BF16).reshape(2, part, part)
        dp = dot_nt(v2, da).reshape(2, frames, 8, part)
        inner = jnp.sum(dp * probs, axis=1, keepdims=True)
        ds = (probs * (dp - inner) * 0.125).astype(BF16).reshape(2, part, part)
        attended = dot_tn(v2, low.reshape(2 * part, part)).astype(BF16)
        for b in range(8):
            left_s[1, pl.ds(block_row(hp * 8 + b, place), 16), tok] = attended[b * 16:(b + 1) * 16]
        right_s[tok, pl.ds(col, 128)] = dot_tn(ds.reshape(2 * part, part), k2).astype(BF16)
        right_s[tok, pl.ds(width + col, 128)] = dot_nn(
            jnp.concatenate([ds[0], ds[1]], axis=1), split(q)
        ).astype(BF16)
        right_s[tok, pl.ds(2 * width + col, 128)] = dot_nn(
            jnp.concatenate([low[0], low[1]], axis=1), split(da)
        ).astype(BF16)
        return carry

    lax.fori_loop(0, clips * halves * (width // 128), attend_step, 0, unroll=4)

    copies = [
        pltpu.make_async_copy(left_s, left_hbm, sems.at[0]),
        pltpu.make_async_copy(right_s, right_hbm, sems.at[1]),
    ]
    for copy in copies:
        copy.start()
    half = width // 2
    for k in range(4):
        rhs = right_s[:, chunk((place[0] + k) % 4)]
        g = dot_nn(left_s[0, half:, :], rhs)
        send_s[:, k] = g.reshape(4, 128, CHUNK).astype(BF16)
        copies.append(pltpu.make_async_copy(send_s.at[:, k], send_hbm.at[:, k], sems.at[2 + k]))
        copies[-1].start()
        g = dot_nn(left_s[0, :half, :], rhs)
        keep_s[:, k] = g.reshape(4, 128, CHUNK)
        copies.append(pltpu.make_async_copy(keep_s.at[:, k], keep_hbm.at[:, k], sems.at[6 + k]))
        copies[-1].start()
    for copy in copies:
        copy.wait()


def run_main(place, tokens, gain, bias, wqkv, wout):
    frames, clips, positions, width = tokens.shape
    rows = clips // 2 * frames * positions
    vm = pl.BlockSpec(memory_space=pltpu.VMEM)
    hbm = pl.BlockSpec(memory_space=pl.ANY)
    piece = (4, 4, 128, CHUNK)
    return pl.pallas_call(
        main_kernel,
        out_shape=(
            jax.ShapeDtypeStruct(piece, BF16),
            jax.ShapeDtypeStruct(piece, F32),
            jax.ShapeDtypeStruct((2, width, rows), BF16),
            jax.ShapeDtypeStruct((rows, 4 * width), BF16),
        ),
        in_specs=[pl.BlockSpec(memory_space=pltpu.SMEM)] + [vm] * 5,
        out_specs=(hbm,) * 4,
        scratch_shapes=[
            pltpu.VMEM((2, width, rows), BF16),
            pltpu.VMEM((rows, 4 * width), BF16),
            pltpu.VMEM((rows, width), BF16),
            pltpu.VMEM((rows, 3 * width), BF16),
            pltpu.VMEM((rows, width), BF16),
            pltpu.VMEM(piece, BF16),
            pltpu.VMEM(piece, F32),
            pltpu.SemaphoreType.DMA((10,)),
        ],
        compiler_params=pltpu.CompilerParams(vmem_limit_bytes=36 * MIB),
        cost_estimate=pl.CostEstimate(flops=12 * 1024**3, bytes_accessed=20 * MIB, transcendentals=MIB),
        name="sublayer",
    )(place, tokens, gain, bias, wqkv, wout)


def grads_kernel(place_ref, left_ref, right_ref, send_ref, keep_ref):
    half = left_ref.shape[1] // 2
    rhs = right_ref[...]
    send_ref[0] = dot_nn(left_ref[0, half:, :], rhs).reshape(4, 128, CHUNK).astype(BF16)
    keep_ref[0] = dot_nn(left_ref[0, :half, :], rhs).reshape(4, 128, CHUNK)


def run_grads(place, left, right):
    _, width, rows = left.shape
    piece = (4, 4, 128, CHUNK)
    out = pl.BlockSpec((1, 4, 128, CHUNK), lambda k, place: (k, 0, 0, 0))
    return pl.pallas_call(
        grads_kernel,
        grid_spec=pltpu.PrefetchScalarGridSpec(
            num_scalar_prefetch=1,
            grid=(4,),
            in_specs=[
                pl.BlockSpec((1, width, rows), lambda k, place: ((place[0] + k) % 4 // 2, 0, 0)),
                pl.BlockSpec((rows, CHUNK), lambda k, place: (0, 4 + (place[0] + k) % 4)),
            ],
            out_specs=(out, out),
        ),
        out_shape=(
            jax.ShapeDtypeStruct(piece, BF16),
            jax.ShapeDtypeStruct(piece, F32),
        ),
        compiler_params=pltpu.CompilerParams(vmem_limit_bytes=24 * MIB),
        cost_estimate=pl.CostEstimate(flops=2 * 1024**3, bytes_accessed=12 * MIB, transcendentals=0),
        name="weight_grads",
    )(place, left, right)


def back_kernel(tokens_ref, gain_ref, dpk_ref, wqkv_ref, gv_ref, dn_s):
    frames, clips, positions, width = tokens_ref.shape
    clips = clips // 2
    halves = positions // 8
    part = frames * 8
    gain = gain_ref[...]
    for n in range(width // CHUNK):
        cols = slice(n * CHUNK, (n + 1) * CHUNK)
        dn_s[:, cols] = dot_nt(dpk_ref[...], wqkv_ref[cols, :])

    def back_step(i, carry):
        dgain, dbias = carry
        c = i // (frames // 2)
        q = i % (frames // 2)
        x = tokens_ref[pl.ds(2 * q, 2), c].astype(F32).reshape(2, halves, 8, width)
        g = tokens_ref[pl.ds(2 * q, 2), clips + c].astype(F32).reshape(2, halves, 8, width)
        outs = []
        for hf in range(halves):
            at = pl.multiple_of((c * halves + hf) * part + q * 16, 16)
            dn = dn_s[pl.ds(at, 16), :]
            wh, inv = whiten(x[:, hf].reshape(16, width))
            dw = dn * wh
            dgain = dgain + dw[:8] + dw[8:]
            dbias = dbias + dn[:8] + dn[8:]
            scaled = dn * gain
            m1 = jnp.mean(scaled, axis=-1, keepdims=True)
            m2 = jnp.mean(scaled * wh, axis=-1, keepdims=True)
            grad = g[:, hf].reshape(16, width) + inv * (scaled - m1 - wh * m2)
            outs.append(grad.reshape(2, 8, width))
        cols = pl.ds(pl.multiple_of(c * width, width), width)
        gv_ref[pl.ds(2 * q, 2), :, cols] = jnp.concatenate(outs, axis=1).astype(BF16)
        return dgain, dbias

    zeros = jnp.zeros((8, width), F32)
    dgain, dbias = lax.fori_loop(0, clips * frames // 2, back_step, (zeros, zeros))
    dgain = jnp.sum(dgain, axis=0, keepdims=True)
    dbias = jnp.sum(dbias, axis=0, keepdims=True)
    lane = lax.broadcasted_iota(jnp.int32, (1, 128), 1)
    row = lax.broadcasted_iota(jnp.int32, (16, 128), 0)
    for f in range(frames):
        at = f // 2 * 128
        a = dgain[:, at:at + 128]
        b = dbias[:, at:at + 128]
        if f % 2 == 0:
            b = jnp.concatenate([b[:, 64:], b[:, :64]], axis=1)
        else:
            a = jnp.concatenate([a[:, 64:], a[:, :64]], axis=1)
        both = jnp.where(lane < 64, a, b)
        hi = both.astype(BF16).astype(F32)
        mid = (both - hi).astype(BF16).astype(F32)
        low = both - hi - mid
        terms = jnp.where(row == 0, hi, jnp.where(row == 1, mid, jnp.where(row == 2, low, 0.0)))
        gv_ref[f, :, clips * width:] = terms.astype(BF16)


def run_back(tokens, gain, right, wqkv):
    frames, clips, positions, width = tokens.shape
    clips = clips // 2
    rows = clips * frames * positions
    whole = lambda *shape: pl.BlockSpec(shape, lambda i: (0,) * len(shape))
    message = (frames, positions, clips * width + 128)
    return pl.pallas_call(
        back_kernel,
        grid=(1,),
        out_shape=jax.ShapeDtypeStruct(message, BF16),
        in_specs=[
            whole(*tokens.shape),
            whole(1, width),
            whole(rows, 3 * width),
            whole(width, 3 * width),
        ],
        out_specs=whole(*message),
        scratch_shapes=[pltpu.VMEM((rows, width), F32)],
        compiler_params=pltpu.CompilerParams(vmem_limit_bytes=40 * MIB),
        cost_estimate=pl.CostEstimate(flops=4 * 1024**3, bytes_accessed=12 * MIB, transcendentals=0),
        name="video_grads",
    )(tokens, gain, right, wqkv)


def place_kernel(scale, place_ref, d0, d1, d2, d3, qkv_ref, out_ref, small_ref):
    x, h = place_ref[0], place_ref[1]
    small = jnp.zeros((8, 128), F32)
    for j, d in enumerate((d0, d1, d2, d3)):
        block = (x - j) % 4
        for k in range(4):
            rows = pl.ds(pl.multiple_of((h - k) % 4 * 16, 16), 16)
            qkv_ref[rows, chunk(block)] = d[k * 32:k * 32 + 16, :] * scale
            b = d[k * 32 + 16:k * 32 + 32, :] * scale

            @pl.when(block < 2)
            def _():
                qkv_ref[rows, chunk(4 + block)] = b

            @pl.when(block >= 2)
            def _():
                out_ref[rows, chunk(block - 2)] = b

        small = small + d[128:136, :128] * scale
    small_ref[...] = small


def run_place(place, scale, pieces):
    vm = pl.BlockSpec(memory_space=pltpu.VMEM)
    return pl.pallas_call(
        functools.partial(place_kernel, scale),
        out_shape=(
            jax.ShapeDtypeStruct((64, 6 * CHUNK), F32),
            jax.ShapeDtypeStruct((64, 2 * CHUNK), F32),
            jax.ShapeDtypeStruct((8, 128), F32),
        ),
        in_specs=[pl.BlockSpec(memory_space=pltpu.SMEM)] + [vm] * 4,
        out_specs=(vm,) * 3,
        name="place_grads",
    )(place, *pieces)


def frame_pairs(move):
    pairs = []
    for i in range(16):
        y, z, core = move(i // 4, i // 2 % 2, i % 2)
        pairs.append((i, y % 4 * 4 + z % 2 * 2 + core % 2))
    return pairs


def dp_pairs(move):
    pairs = []
    for i in range(16):
        x, h = move(i // 4, i % 4)
        pairs.append((i, x % 4 * 4 + h % 4))
    return pairs


def go_core(a):
    return lax.ppermute(a, "frame", frame_pairs(lambda y, z, c: (y, z, c + 1)))


def go_y(a, k):
    return lax.ppermute(a, "frame", frame_pairs(lambda y, z, c: (y + k, z, c)))


def go_z(a):
    return lax.ppermute(a, "frame", frame_pairs(lambda y, z, c: (y, z + 1, c)))


def go_x(a, k):
    return lax.ppermute(a, "dp", dp_pairs(lambda x, h: (x + k, h)))


def go_h(a, k):
    return lax.ppermute(a, "dp", dp_pairs(lambda x, h: (x, h + k)))


def reduce_ring(piece, go, dtype):
    got = [go(piece(k).astype(dtype), k) for k in range(1, 4)]
    total = piece(0)
    for part in got:
        total = total + part.astype(F32)
    return total


def reduce_grads(send_a, keep_a, send_b, keep_b, small):
    got_a = go_core(send_a)
    got_b = go_core(send_b)
    a = reduce_ring(lambda k: keep_a[k] + got_a[k].astype(F32), go_y, BF16)
    b = reduce_ring(lambda k: keep_b[k] + got_b[k].astype(F32), go_x, BF16)
    a = reduce_second(a, go_x)
    b = reduce_second(b, go_y)
    away = jnp.stack([a[64:], b[64:]])
    both = jnp.stack([a[:64], b[:64]]) + go_z(away)
    both = both.reshape(2, 4, 16, CHUNK)
    both = reduce_ring(lambda k: both[:, k], go_h, F32)
    message = jnp.concatenate([both.reshape(32, CHUNK), small], axis=0)
    got = [message] + [go_h(message, k) for k in range(1, 4)]
    small = got[0][32:] + got[1][32:] + got[2][32:] + got[3][32:]
    message = jnp.concatenate([g[:32] for g in got] + [small], axis=0)
    return [message] + [go_x(message, k) for k in range(1, 4)]


def reduce_second(total, go):
    return reduce_ring(lambda k: total[k], go, F32)


def local(video, cotangent, norm_gain, norm_bias, qkv_weight, out_weight):
    clips, frames_here, positions, width = video.shape
    grad_scale = 1.0 / math.sqrt(clips * positions * 256)
    frame = lax.axis_index("frame")
    dp = lax.axis_index("dp")
    place = jnp.stack([dp // 4, dp % 4, frame // 4, frame // 2 % 2, frame % 2]).astype(jnp.int32)
    gain = norm_gain.reshape(1, width)
    bias = norm_bias.reshape(1, width)
    tokens = jnp.concatenate([video, cotangent], axis=0).reshape(2 * clips, 16, positions // 16, width)
    tokens = lax.all_to_all(tokens.transpose(1, 0, 2, 3), "frame", 0, 0, tiled=True)
    send_a, keep_a, left, right = run_main(place, tokens, gain, bias, qkv_weight, out_weight)
    send_b, keep_b = run_grads(place, left, right)
    back = run_back(tokens, gain, right, qkv_weight)
    back = lax.all_to_all(back, "frame", 0, 0, tiled=True)
    grad_video = back[:, :, : clips * width].reshape(positions, clips, width)
    grad_video = grad_video.transpose(1, 0, 2).reshape(video.shape)
    small = jnp.sum(back[:, :3, clips * width :].astype(F32), axis=(0, 1))
    small = jnp.pad(small.reshape(1, 128), ((0, 7), (0, CHUNK - 128)))
    pieces = reduce_grads(send_a, keep_a, send_b, keep_b, small)
    grad_qkv, grad_out, small = run_place(place, grad_scale, pieces)
    return grad_video, grad_qkv, grad_out, small[0, :64], small[0, 64:]


def solution(mesh):
    in_specs = (P("dp", "frame", None, None), P("dp", "frame", None, None), P(), P(), P(), P())
    out_specs = (
        P("dp", "frame", None, None),
        P("frame", None),
        P("frame", None),
        P("frame"),
        P("frame"),
    )
    return jax.shard_map(local, mesh=mesh, in_specs=in_specs, out_specs=out_specs, check_vma=False)
```

```python
import functools
import math

import jax
import jax.numpy as jnp
from jax import lax
from jax.experimental import pallas as pl
from jax.experimental.pallas import tpu as pltpu
from jax.sharding import PartitionSpec as P

F32 = jnp.float32
BF16 = jnp.bfloat16
MIB = 1024 * 1024
CHUNK = 512


def dot_nn(a, b):
    return lax.dot_general(a, b, (((1,), (0,)), ((), ())), preferred_element_type=F32)


def dot_nt(a, b):
    return lax.dot_general(a, b, (((1,), (1,)), ((), ())), preferred_element_type=F32)


def dot_tn(a, b):
    return lax.dot_general(a, b, (((0,), (0,)), ((), ())), preferred_element_type=F32)


def chunk(n):
    return pl.ds(pl.multiple_of(n * CHUNK, CHUNK), CHUNK)


def block_row(block, place):
    x, y, z, core = place
    dcore = (block % 2 - core) % 2
    dz = (block // 2 % 2 - z) % 2
    dy = (block // 4 - y) % 4
    return pl.multiple_of(((dcore * 4 + dy) * 2 + dz) * 64, 64)


def read_place(place_ref):
    return tuple(place_ref[i] for i in range(4))


def whiten(xh):
    centred = xh - jnp.mean(xh, axis=-1, keepdims=True)
    inv = lax.rsqrt(jnp.mean(centred * centred, axis=-1, keepdims=True) + 1e-05)
    return centred * inv, inv


def main_kernel(
    place_ref, tokens_ref, gain_ref, bias_ref, wqkv_ref, wout_ref,
    send_hbm, keep_hbm, left_hbm, right_hbm,
    left_s, right_s, normed_s, packed_s, datt_s, send_s, keep_s, sems,
):
    place = read_place(place_ref)
    frames, clips, positions, width = tokens_ref.shape
    clips = clips // 2
    halves = positions // 8
    part = frames * 8
    gain = gain_ref[...]
    bias = bias_ref[...]

    def norm_step(i, carry):
        c = i // (frames // 2)
        q = i % (frames // 2)
        x = tokens_ref[pl.ds(2 * q, 2), c].astype(F32).reshape(2, halves, 8, width)
        g = tokens_ref[pl.ds(2 * q, 2), clips + c].astype(F32).reshape(2, halves, 8, width)
        for hf in range(halves):
            at = pl.multiple_of((c * halves + hf) * part + q * 16, 16)
            wh, _ = whiten(x[:, hf].reshape(16, width))
            normed_s[pl.ds(at, 16), :] = (wh * gain + bias).astype(BF16)
            right_s[pl.ds(at, 16), pl.ds(3 * width, width)] = g[:, hf].reshape(16, width).astype(BF16)
        return carry

    lax.fori_loop(0, clips * frames // 2, norm_step, 0)

    def qkv_step(n, carry):
        packed_s[:, chunk(n)] = dot_nn(normed_s[...], wqkv_ref[:, chunk(n)]).astype(BF16)
        return carry

    lax.fori_loop(0, 3 * width // CHUNK, qkv_step, 0, unroll=2)

    for n in range(width // CHUNK):
        cols = slice(n * CHUNK, (n + 1) * CHUNK)
        datt_s[:, cols] = dot_nt(right_s[:, 3 * width:], wout_ref[cols, :]).astype(BF16)
        turned = normed_s[:, cols].T
        for b in range(CHUNK // 64):
            at = block_row(n * (CHUNK // 64) + b, place)
            left_s[0, pl.ds(at, 64), :] = turned[b * 64:(b + 1) * 64]

    lane = lax.broadcasted_iota(jnp.int32, (part, 128), 1)
    first = lane < 64
    same = lax.broadcasted_iota(jnp.int32, (1, 8, part), 1) == (
        lax.broadcasted_iota(jnp.int32, (1, 8, part), 2) % 8
    )
    zero = jnp.zeros((part, 128), BF16)

    def split(a):
        return jnp.concatenate([jnp.where(first, a, zero), jnp.where(first, zero, a)], axis=0)

    def attend_step(i, carry):
        t = i // (width // 128)
        hp = i % (width // 128)
        tok = pl.ds(pl.multiple_of(t * part, part), part)
        col = pl.multiple_of(hp * 128, 128)
        q = packed_s[tok, pl.ds(col, 128)]
        k = packed_s[tok, pl.ds(width + col, 128)]
        v = packed_s[tok, pl.ds(2 * width + col, 128)]
        da = datt_s[tok, pl.ds(col, 128)]
        k2 = split(k)
        v2 = split(v)
        scores = (dot_nt(k2, q) * 0.125).reshape(2, frames, 8, part)
        e = jnp.exp(scores - jnp.max(scores, axis=1, keepdims=True))
        probs = e * (1.0 / jnp.sum(e, axis=1, keepdims=True))
        probs = jnp.where(same[None], probs, 0.0)
        low = probs.astype(BF16).reshape(2, part, part)
        dp = dot_nt(v2, da).reshape(2, frames, 8, part)
        inner = jnp.sum(dp * probs, axis=1, keepdims=True)
        ds = (probs * (dp - inner) * 0.125).astype(BF16).reshape(2, part, part)
        attended = dot_tn(v2, low.reshape(2 * part, part)).astype(BF16)
        for b in range(2):
            left_s[1, pl.ds(block_row(hp * 2 + b, place), 64), tok] = attended[b * 64:(b + 1) * 64]
        right_s[tok, pl.ds(col, 128)] = dot_tn(ds.reshape(2 * part, part), k2).astype(BF16)
        right_s[tok, pl.ds(width + col, 128)] = dot_nn(
            jnp.concatenate([ds[0], ds[1]], axis=1), split(q)
        ).astype(BF16)
        right_s[tok, pl.ds(2 * width + col, 128)] = dot_nn(
            jnp.concatenate([low[0], low[1]], axis=1), split(da)
        ).astype(BF16)
        return carry

    lax.fori_loop(0, clips * halves * (width // 128), attend_step, 0, unroll=4)

    copies = [
        pltpu.make_async_copy(left_s, left_hbm, sems.at[0]),
        pltpu.make_async_copy(right_s, right_hbm, sems.at[1]),
    ]
    for copy in copies:
        copy.start()
    half = width // 2
    for k in range(4):
        rhs = right_s[:, chunk((place[0] + k) % 4)]
        g = dot_nn(left_s[0, half:, :], rhs)
        send_s[:, k] = g.reshape(4, 128, CHUNK).astype(BF16)
        copies.append(pltpu.make_async_copy(send_s.at[:, k], send_hbm.at[:, k], sems.at[2 + k]))
        copies[-1].start()
        g = dot_nn(left_s[0, :half, :], rhs)
        keep_s[:, k] = g.reshape(4, 128, CHUNK)
        copies.append(pltpu.make_async_copy(keep_s.at[:, k], keep_hbm.at[:, k], sems.at[6 + k]))
        copies[-1].start()
    for copy in copies:
        copy.wait()


def run_main(place, tokens, gain, bias, wqkv, wout):
    frames, clips, positions, width = tokens.shape
    rows = clips // 2 * frames * positions
    vm = pl.BlockSpec(memory_space=pltpu.VMEM)
    hbm = pl.BlockSpec(memory_space=pl.ANY)
    piece = (4, 4, 128, CHUNK)
    return pl.pallas_call(
        main_kernel,
        out_shape=(
            jax.ShapeDtypeStruct(piece, BF16),
            jax.ShapeDtypeStruct(piece, F32),
            jax.ShapeDtypeStruct((2, width, rows), BF16),
            jax.ShapeDtypeStruct((rows, 4 * width), BF16),
        ),
        in_specs=[pl.BlockSpec(memory_space=pltpu.SMEM)] + [vm] * 5,
        out_specs=(hbm,) * 4,
        scratch_shapes=[
            pltpu.VMEM((2, width, rows), BF16),
            pltpu.VMEM((rows, 4 * width), BF16),
            pltpu.VMEM((rows, width), BF16),
            pltpu.VMEM((rows, 3 * width), BF16),
            pltpu.VMEM((rows, width), BF16),
            pltpu.VMEM(piece, BF16),
            pltpu.VMEM(piece, F32),
            pltpu.SemaphoreType.DMA((10,)),
        ],
        compiler_params=pltpu.CompilerParams(vmem_limit_bytes=36 * MIB),
        cost_estimate=pl.CostEstimate(flops=12 * 1024**3, bytes_accessed=20 * MIB, transcendentals=MIB),
        name="sublayer",
    )(place, tokens, gain, bias, wqkv, wout)


def grads_kernel(place_ref, left_ref, right_ref, send_ref, keep_ref):
    half = left_ref.shape[1] // 2
    rhs = right_ref[...]
    send_ref[0] = dot_nn(left_ref[0, half:, :], rhs).reshape(4, 128, CHUNK).astype(BF16)
    keep_ref[0] = dot_nn(left_ref[0, :half, :], rhs).reshape(4, 128, CHUNK)


def run_grads(place, left, right):
    _, width, rows = left.shape
    piece = (4, 4, 128, CHUNK)
    out = pl.BlockSpec((1, 4, 128, CHUNK), lambda k, place: (k, 0, 0, 0))
    return pl.pallas_call(
        grads_kernel,
        grid_spec=pltpu.PrefetchScalarGridSpec(
            num_scalar_prefetch=1,
            grid=(4,),
            in_specs=[
                pl.BlockSpec((1, width, rows), lambda k, place: ((place[0] + k) % 4 // 2, 0, 0)),
                pl.BlockSpec((rows, CHUNK), lambda k, place: (0, 4 + (place[0] + k) % 4)),
            ],
            out_specs=(out, out),
        ),
        out_shape=(
            jax.ShapeDtypeStruct(piece, BF16),
            jax.ShapeDtypeStruct(piece, F32),
        ),
        compiler_params=pltpu.CompilerParams(vmem_limit_bytes=24 * MIB),
        cost_estimate=pl.CostEstimate(flops=2 * 1024**3, bytes_accessed=12 * MIB, transcendentals=0),
        name="weight_grads",
    )(place, left, right)


def back_kernel(tokens_ref, gain_ref, dpk_ref, wqkv_ref, gv_ref, dn_s):
    frames, clips, positions, width = tokens_ref.shape
    clips = clips // 2
    halves = positions // 8
    part = frames * 8
    gain = gain_ref[...]
    for n in range(width // CHUNK):
        cols = slice(n * CHUNK, (n + 1) * CHUNK)
        dn_s[:, cols] = dot_nt(dpk_ref[...], wqkv_ref[cols, :])

    def back_step(i, carry):
        dgain, dbias = carry
        c = i // (frames // 2)
        q = i % (frames // 2)
        x = tokens_ref[pl.ds(2 * q, 2), c].astype(F32).reshape(2, halves, 8, width)
        g = tokens_ref[pl.ds(2 * q, 2), clips + c].astype(F32).reshape(2, halves, 8, width)
        outs = []
        for hf in range(halves):
            at = pl.multiple_of((c * halves + hf) * part + q * 16, 16)
            dn = dn_s[pl.ds(at, 16), :]
            wh, inv = whiten(x[:, hf].reshape(16, width))
            dw = dn * wh
            dgain = dgain + dw[:8] + dw[8:]
            dbias = dbias + dn[:8] + dn[8:]
            scaled = dn * gain
            m1 = jnp.mean(scaled, axis=-1, keepdims=True)
            m2 = jnp.mean(scaled * wh, axis=-1, keepdims=True)
            grad = g[:, hf].reshape(16, width) + inv * (scaled - m1 - wh * m2)
            outs.append(grad.reshape(2, 8, width))
        cols = pl.ds(pl.multiple_of(c * width, width), width)
        gv_ref[pl.ds(2 * q, 2), :, cols] = jnp.concatenate(outs, axis=1).astype(BF16)
        return dgain, dbias

    zeros = jnp.zeros((8, width), F32)
    dgain, dbias = lax.fori_loop(0, clips * frames // 2, back_step, (zeros, zeros))
    dgain = jnp.sum(dgain, axis=0, keepdims=True)
    dbias = jnp.sum(dbias, axis=0, keepdims=True)
    lane = lax.broadcasted_iota(jnp.int32, (1, 128), 1)
    row = lax.broadcasted_iota(jnp.int32, (16, 128), 0)
    for f in range(frames):
        at = f // 2 * 128
        a = dgain[:, at:at + 128]
        b = dbias[:, at:at + 128]
        if f % 2 == 0:
            b = jnp.concatenate([b[:, 64:], b[:, :64]], axis=1)
        else:
            a = jnp.concatenate([a[:, 64:], a[:, :64]], axis=1)
        both = jnp.where(lane < 64, a, b)
        hi = both.astype(BF16).astype(F32)
        mid = (both - hi).astype(BF16).astype(F32)
        low = both - hi - mid
        terms = jnp.where(row == 0, hi, jnp.where(row == 1, mid, jnp.where(row == 2, low, 0.0)))
        gv_ref[f, :, clips * width:] = terms.astype(BF16)


def run_back(tokens, gain, right, wqkv):
    frames, clips, positions, width = tokens.shape
    clips = clips // 2
    rows = clips * frames * positions
    whole = lambda *shape: pl.BlockSpec(shape, lambda i: (0,) * len(shape))
    message = (frames, positions, clips * width + 128)
    return pl.pallas_call(
        back_kernel,
        grid=(1,),
        out_shape=jax.ShapeDtypeStruct(message, BF16),
        in_specs=[
            whole(*tokens.shape),
            whole(1, width),
            whole(rows, 3 * width),
            whole(width, 3 * width),
        ],
        out_specs=whole(*message),
        scratch_shapes=[pltpu.VMEM((rows, width), F32)],
        compiler_params=pltpu.CompilerParams(vmem_limit_bytes=40 * MIB),
        cost_estimate=pl.CostEstimate(flops=4 * 1024**3, bytes_accessed=12 * MIB, transcendentals=0),
        name="video_grads",
    )(tokens, gain, right, wqkv)


def place_kernel(scale, place_ref, d0, d1, d2, d3, qkv_ref, out_ref, gain_ref, bias_ref):
    x = place_ref[0]
    small = jnp.zeros((8, 128), F32)
    for j, d in enumerate((d0, d1, d2, d3)):
        block = (x - j) % 4
        qkv_ref[:, chunk(block)] = d[:64, :] * scale

        @pl.when(block < 2)
        def _():
            qkv_ref[:, chunk(4 + block)] = d[64:128, :] * scale

        @pl.when(block >= 2)
        def _():
            out_ref[:, chunk(block - 2)] = d[64:128, :] * scale

        small = small + d[128:136, :128] * scale
    gain_ref[...] = small[:1, :64]
    bias_ref[...] = small[:1, 64:]


def run_place(place, scale, pieces):
    vm = pl.BlockSpec(memory_space=pltpu.VMEM)
    return pl.pallas_call(
        functools.partial(place_kernel, scale),
        out_shape=(
            jax.ShapeDtypeStruct((64, 6 * CHUNK), F32),
            jax.ShapeDtypeStruct((64, 2 * CHUNK), F32),
            jax.ShapeDtypeStruct((1, 64), F32),
            jax.ShapeDtypeStruct((1, 64), F32),
        ),
        in_specs=[pl.BlockSpec(memory_space=pltpu.SMEM)] + [vm] * 4,
        out_specs=(vm,) * 4,
        name="place_grads",
    )(place, *pieces)


def frame_pairs(move):
    pairs = []
    for i in range(16):
        y, z, core = move(i // 4, i // 2 % 2, i % 2)
        pairs.append((i, y % 4 * 4 + z % 2 * 2 + core % 2))
    return pairs


def dp_pairs(move):
    pairs = []
    for i in range(16):
        x, h = move(i // 4, i % 4)
        pairs.append((i, x % 4 * 4 + h % 4))
    return pairs


def go_core(a):
    return lax.ppermute(a, "frame", frame_pairs(lambda y, z, c: (y, z, c + 1)))


def go_y(a, k):
    return lax.ppermute(a, "frame", frame_pairs(lambda y, z, c: (y + k, z, c)))


def go_z(a):
    return lax.ppermute(a, "frame", frame_pairs(lambda y, z, c: (y, z + 1, c)))


def go_x(a, k):
    return lax.ppermute(a, "dp", dp_pairs(lambda x, h: (x + k, h)))


def go_h(a, k):
    return lax.ppermute(a, "dp", dp_pairs(lambda x, h: (x, h + k)))


def combine(own, got):
    for part in got:
        own = own + part.astype(F32)
    return own


def exchange(pieces, go):
    return [go(pieces[k], k) for k in range(1, 4)]


def first_pieces(keep, got):
    own = keep[0] + got[0].astype(F32)
    return [own] + [(keep[k] + got[k].astype(F32)).astype(BF16) for k in range(1, 4)]


def second_pieces(total):
    return [total[0]] + [total[k].astype(BF16) for k in range(1, 4)]


def three_terms(value):
    hi = lax.reduce_precision(value, 8, 7)
    mid = lax.reduce_precision(value - hi, 8, 7)
    return jnp.concatenate([hi, mid, value - hi - mid], axis=0)


def local(video, cotangent, norm_gain, norm_bias, qkv_weight, out_weight):
    clips, frames_here, positions, width = video.shape
    grad_scale = 1.0 / math.sqrt(clips * positions * 256)
    frame = lax.axis_index("frame")
    dp = lax.axis_index("dp")
    place = jnp.stack([dp // 4, frame // 4, frame // 2 % 2, frame % 2]).astype(jnp.int32)
    gain = norm_gain.reshape(1, width)
    bias = norm_bias.reshape(1, width)
    tokens = jnp.concatenate([video, cotangent], axis=0).reshape(2 * clips, 16, positions // 16, width)
    tokens = lax.all_to_all(tokens.transpose(1, 0, 2, 3), "frame", 0, 0, tiled=True)

    send_a, keep_a, left, right = run_main(place, tokens, gain, bias, qkv_weight, out_weight)
    send_b, keep_b = run_grads(place, left, right)
    pieces_a = first_pieces(keep_a, go_core(send_a))
    pieces_b = first_pieces(keep_b, go_core(send_b))
    got_a = exchange(pieces_a, go_y)
    right, pieces_b = lax.optimization_barrier((right, pieces_b))
    got_b = exchange(pieces_b, go_x)

    back = run_back(tokens, gain, right, qkv_weight)
    back = lax.all_to_all(back, "frame", 0, 0, tiled=True)
    grad_video = back[:, :, : clips * width].reshape(positions, clips, width)
    grad_video = grad_video.transpose(1, 0, 2).reshape(video.shape)
    small = jnp.sum(back[:, :3, clips * width :].astype(F32), axis=(0, 1)).reshape(1, 128)

    got_a, got_b[0], got_b[2] = lax.optimization_barrier((got_a, got_b[0], got_b[2]))
    pieces_a = second_pieces(combine(pieces_a[0], got_a))
    pieces_b = second_pieces(combine(pieces_b[0], got_b))
    got_a = exchange(pieces_a, go_x)
    got_b = exchange(pieces_b, go_y)
    a = combine(pieces_a[0], got_a)
    b = combine(pieces_b[0], got_b)
    own = jnp.concatenate([a[:64], b[:64]], axis=0) + go_z(jnp.concatenate([a[64:], b[64:]], axis=0))
    own = jnp.concatenate([own, jnp.pad(three_terms(small), ((0, 13), (0, CHUNK - 128)))], axis=0)
    own = combine(own, exchange([own.astype(BF16)] * 4, go_h))
    small = jnp.sum(own[128:131], axis=0, keepdims=True)
    own = jnp.concatenate([own[:128], jnp.pad(small, ((0, 7), (0, 0)))], axis=0)
    pieces = [own] + exchange([own] * 4, go_x)
    grad_qkv, grad_out, total_gain, total_bias = run_place(place, grad_scale, pieces)
    return grad_video, grad_qkv, grad_out, total_gain.reshape(64), total_bias.reshape(64)


def solution(mesh):
    in_specs = (P("dp", "frame", None, None), P("dp", "frame", None, None), P(), P(), P(), P())
    out_specs = (
        P("dp", "frame", None, None),
        P("frame", None),
        P("frame", None),
        P("frame"),
        P("frame"),
    )
    return jax.shard_map(local, mesh=mesh, in_specs=in_specs, out_specs=out_specs, check_vma=False)
```

```python
import functools
import math

import jax
import jax.numpy as jnp
from jax import lax
from jax.experimental import pallas as pl
from jax.experimental.pallas import tpu as pltpu
from jax.sharding import PartitionSpec as P

F32 = jnp.float32
BF16 = jnp.bfloat16
MIB = 1024 * 1024
CHUNK = 512


def dot_nn(a, b):
    return lax.dot_general(a, b, (((1,), (0,)), ((), ())), preferred_element_type=F32)


def dot_nt(a, b):
    return lax.dot_general(a, b, (((1,), (1,)), ((), ())), preferred_element_type=F32)


def dot_tn(a, b):
    return lax.dot_general(a, b, (((0,), (0,)), ((), ())), preferred_element_type=F32)


def chunk(n):
    return pl.ds(pl.multiple_of(n * CHUNK, CHUNK), CHUNK)


def block_row(block, place):
    return pl.multiple_of(((block % 2 - place[1]) % 2 * 8 + block // 2) * 64, 64)


def read_place(place_ref):
    return tuple(place_ref[i] for i in range(2))


def whiten(xh):
    centred = xh - jnp.mean(xh, axis=-1, keepdims=True)
    inv = lax.rsqrt(jnp.mean(centred * centred, axis=-1, keepdims=True) + 1e-05)
    return centred * inv, inv


def main_kernel(
    place_ref, tokens_ref, gain_ref, bias_ref, wqkv_ref, wout_ref,
    send_hbm, keep_hbm, left_hbm, right_hbm,
    left_s, right_s, normed_s, packed_s, datt_s, send_s, keep_s, sems,
):
    place = read_place(place_ref)
    frames, clips, positions, width = tokens_ref.shape
    clips = clips // 2
    halves = positions // 8
    part = frames * 8
    gain = gain_ref[...]
    bias = bias_ref[...]

    def norm_step(i, carry):
        c = i // (frames // 2)
        q = i % (frames // 2)
        x = tokens_ref[pl.ds(2 * q, 2), c].astype(F32).reshape(2, halves, 8, width)
        g = tokens_ref[pl.ds(2 * q, 2), clips + c].astype(F32).reshape(2, halves, 8, width)
        for hf in range(halves):
            at = pl.multiple_of((c * halves + hf) * part + q * 16, 16)
            wh, _ = whiten(x[:, hf].reshape(16, width))
            normed_s[pl.ds(at, 16), :] = (wh * gain + bias).astype(BF16)
            right_s[pl.ds(at, 16), pl.ds(3 * width, width)] = g[:, hf].reshape(16, width).astype(BF16)
        return carry

    lax.fori_loop(0, clips * frames // 2, norm_step, 0)

    def qkv_step(n, carry):
        packed_s[:, chunk(n)] = dot_nn(normed_s[...], wqkv_ref[:, chunk(n)]).astype(BF16)
        return carry

    lax.fori_loop(0, 3 * width // CHUNK, qkv_step, 0, unroll=2)

    for n in range(width // CHUNK):
        cols = slice(n * CHUNK, (n + 1) * CHUNK)
        datt_s[:, cols] = dot_nt(right_s[:, 3 * width:], wout_ref[cols, :]).astype(BF16)
        turned = normed_s[:, cols].T
        for b in range(CHUNK // 64):
            at = block_row(n * (CHUNK // 64) + b, place)
            left_s[0, pl.ds(at, 64), :] = turned[b * 64:(b + 1) * 64]

    lane = lax.broadcasted_iota(jnp.int32, (part, 128), 1)
    first = lane < 64
    same = lax.broadcasted_iota(jnp.int32, (1, 8, part), 1) == (
        lax.broadcasted_iota(jnp.int32, (1, 8, part), 2) % 8
    )
    zero = jnp.zeros((part, 128), BF16)

    def split(a):
        return jnp.concatenate([jnp.where(first, a, zero), jnp.where(first, zero, a)], axis=0)

    def attend_step(i, carry):
        t = i // (width // 128)
        hp = i % (width // 128)
        tok = pl.ds(pl.multiple_of(t * part, part), part)
        col = pl.multiple_of(hp * 128, 128)
        q = packed_s[tok, pl.ds(col, 128)]
        k = packed_s[tok, pl.ds(width + col, 128)]
        v = packed_s[tok, pl.ds(2 * width + col, 128)]
        da = datt_s[tok, pl.ds(col, 128)]
        k2 = split(k)
        v2 = split(v)
        scores = (dot_nt(k2, q) * 0.125).reshape(2, frames, 8, part)
        e = jnp.exp(scores - jnp.max(scores, axis=1, keepdims=True))
        probs = e * (1.0 / jnp.sum(e, axis=1, keepdims=True))
        probs = jnp.where(same[None], probs, 0.0)
        low = probs.astype(BF16).reshape(2, part, part)
        dp = dot_nt(v2, da).reshape(2, frames, 8, part)
        inner = jnp.sum(dp * probs, axis=1, keepdims=True)
        ds = (probs * (dp - inner) * 0.125).astype(BF16).reshape(2, part, part)
        attended = dot_tn(v2, low.reshape(2 * part, part)).astype(BF16)
        for b in range(2):
            left_s[1, pl.ds(block_row(hp * 2 + b, place), 64), tok] = attended[b * 64:(b + 1) * 64]
        right_s[tok, pl.ds(col, 128)] = dot_tn(ds.reshape(2 * part, part), k2).astype(BF16)
        right_s[tok, pl.ds(width + col, 128)] = dot_nn(
            jnp.concatenate([ds[0], ds[1]], axis=1), split(q)
        ).astype(BF16)
        right_s[tok, pl.ds(2 * width + col, 128)] = dot_nn(
            jnp.concatenate([low[0], low[1]], axis=1), split(da)
        ).astype(BF16)
        return carry

    lax.fori_loop(0, clips * halves * (width // 128), attend_step, 0, unroll=4)

    copies = [
        pltpu.make_async_copy(left_s, left_hbm, sems.at[0]),
        pltpu.make_async_copy(right_s, right_hbm, sems.at[1]),
    ]
    for copy in copies:
        copy.start()
    half = width // 2
    for k in range(4):
        rhs = right_s[:, chunk((place[0] + k) % 4)]
        g = dot_nn(left_s[0, half:, :], rhs)
        send_s[:, k] = g.reshape(8, 64, CHUNK).astype(BF16)
        copies.append(pltpu.make_async_copy(send_s.at[:, k], send_hbm.at[:, k], sems.at[2 + k]))
        copies[-1].start()
        g = dot_nn(left_s[0, :half, :], rhs)
        keep_s[:, k] = g.reshape(8, 64, CHUNK)
        copies.append(pltpu.make_async_copy(keep_s.at[:, k], keep_hbm.at[:, k], sems.at[6 + k]))
        copies[-1].start()
    for copy in copies:
        copy.wait()


def run_main(place, tokens, gain, bias, wqkv, wout):
    frames, clips, positions, width = tokens.shape
    rows = clips // 2 * frames * positions
    vm = pl.BlockSpec(memory_space=pltpu.VMEM)
    hbm = pl.BlockSpec(memory_space=pl.ANY)
    piece = (8, 4, 64, CHUNK)
    return pl.pallas_call(
        main_kernel,
        out_shape=(
            jax.ShapeDtypeStruct(piece, BF16),
            jax.ShapeDtypeStruct(piece, F32),
            jax.ShapeDtypeStruct((2, width, rows), BF16),
            jax.ShapeDtypeStruct((rows, 4 * width), BF16),
        ),
        in_specs=[pl.BlockSpec(memory_space=pltpu.SMEM)] + [vm] * 5,
        out_specs=(hbm,) * 4,
        scratch_shapes=[
            pltpu.VMEM((2, width, rows), BF16),
            pltpu.VMEM((rows, 4 * width), BF16),
            pltpu.VMEM((rows, width), BF16),
            pltpu.VMEM((rows, 3 * width), BF16),
            pltpu.VMEM((rows, width), BF16),
            pltpu.VMEM(piece, BF16),
            pltpu.VMEM(piece, F32),
            pltpu.SemaphoreType.DMA((10,)),
        ],
        compiler_params=pltpu.CompilerParams(vmem_limit_bytes=36 * MIB),
        cost_estimate=pl.CostEstimate(flops=12 * 1024**3, bytes_accessed=20 * MIB, transcendentals=MIB),
        name="sublayer",
    )(place, tokens, gain, bias, wqkv, wout)


def grads_kernel(place_ref, left_ref, right_ref, send_ref, keep_ref):
    half = left_ref.shape[1] // 2
    rhs = right_ref[...]
    send_ref[0] = dot_nn(left_ref[0, half:, :], rhs).reshape(8, 64, CHUNK).astype(BF16)
    keep_ref[0] = dot_nn(left_ref[0, :half, :], rhs).reshape(8, 64, CHUNK)


def run_grads(place, left, right):
    _, width, rows = left.shape
    piece = (4, 8, 64, CHUNK)
    out = pl.BlockSpec((1, 8, 64, CHUNK), lambda k, place: (k, 0, 0, 0))
    return pl.pallas_call(
        grads_kernel,
        grid_spec=pltpu.PrefetchScalarGridSpec(
            num_scalar_prefetch=1,
            grid=(4,),
            in_specs=[
                pl.BlockSpec((1, width, rows), lambda k, place: ((place[0] + k) % 4 // 2, 0, 0)),
                pl.BlockSpec((rows, CHUNK), lambda k, place: (0, 4 + (place[0] + k) % 4)),
            ],
            out_specs=(out, out),
        ),
        out_shape=(
            jax.ShapeDtypeStruct(piece, BF16),
            jax.ShapeDtypeStruct(piece, F32),
        ),
        compiler_params=pltpu.CompilerParams(vmem_limit_bytes=24 * MIB),
        cost_estimate=pl.CostEstimate(flops=2 * 1024**3, bytes_accessed=12 * MIB, transcendentals=0),
        name="weight_grads",
    )(place, left, right)


def back_kernel(tokens_ref, gain_ref, dpk_ref, wqkv_ref, gv_ref, dn_s):
    frames, clips, positions, width = tokens_ref.shape
    clips = clips // 2
    halves = positions // 8
    part = frames * 8
    gain = gain_ref[...]
    for n in range(width // CHUNK):
        cols = slice(n * CHUNK, (n + 1) * CHUNK)
        dn_s[:, cols] = dot_nt(dpk_ref[...], wqkv_ref[cols, :])

    def back_step(i, carry):
        dgain, dbias = carry
        c = i // (frames // 2)
        q = i % (frames // 2)
        x = tokens_ref[pl.ds(2 * q, 2), c].astype(F32).reshape(2, halves, 8, width)
        g = tokens_ref[pl.ds(2 * q, 2), clips + c].astype(F32).reshape(2, halves, 8, width)
        outs = []
        for hf in range(halves):
            at = pl.multiple_of((c * halves + hf) * part + q * 16, 16)
            dn = dn_s[pl.ds(at, 16), :]
            wh, inv = whiten(x[:, hf].reshape(16, width))
            dw = dn * wh
            dgain = dgain + dw[:8] + dw[8:]
            dbias = dbias + dn[:8] + dn[8:]
            scaled = dn * gain
            m1 = jnp.mean(scaled, axis=-1, keepdims=True)
            m2 = jnp.mean(scaled * wh, axis=-1, keepdims=True)
            grad = g[:, hf].reshape(16, width) + inv * (scaled - m1 - wh * m2)
            outs.append(grad.reshape(2, 8, width))
        cols = pl.ds(pl.multiple_of(c * width, width), width)
        gv_ref[pl.ds(2 * q, 2), :, cols] = jnp.concatenate(outs, axis=1).astype(BF16)
        return dgain, dbias

    zeros = jnp.zeros((8, width), F32)
    dgain, dbias = lax.fori_loop(0, clips * frames // 2, back_step, (zeros, zeros))
    dgain = jnp.sum(dgain, axis=0, keepdims=True)
    dbias = jnp.sum(dbias, axis=0, keepdims=True)
    lane = lax.broadcasted_iota(jnp.int32, (1, 128), 1)
    row = lax.broadcasted_iota(jnp.int32, (16, 128), 0)
    for f in range(frames):
        at = f // 2 * 128
        a = dgain[:, at:at + 128]
        b = dbias[:, at:at + 128]
        if f % 2 == 0:
            b = jnp.concatenate([b[:, 64:], b[:, :64]], axis=1)
        else:
            a = jnp.concatenate([a[:, 64:], a[:, :64]], axis=1)
        both = jnp.where(lane < 64, a, b)
        hi = both.astype(BF16).astype(F32)
        mid = (both - hi).astype(BF16).astype(F32)
        low = both - hi - mid
        terms = jnp.where(row == 0, hi, jnp.where(row == 1, mid, jnp.where(row == 2, low, 0.0)))
        gv_ref[f, :, clips * width:] = terms.astype(BF16)


def run_back(tokens, gain, right, wqkv):
    frames, clips, positions, width = tokens.shape
    clips = clips // 2
    rows = clips * frames * positions
    whole = lambda *shape: pl.BlockSpec(shape, lambda i: (0,) * len(shape))
    message = (frames, positions, clips * width + 128)
    return pl.pallas_call(
        back_kernel,
        grid=(1,),
        out_shape=jax.ShapeDtypeStruct(message, BF16),
        in_specs=[
            whole(*tokens.shape),
            whole(1, width),
            whole(rows, 3 * width),
            whole(width, 3 * width),
        ],
        out_specs=whole(*message),
        scratch_shapes=[pltpu.VMEM((rows, width), F32)],
        compiler_params=pltpu.CompilerParams(vmem_limit_bytes=40 * MIB),
        cost_estimate=pl.CostEstimate(flops=4 * 1024**3, bytes_accessed=12 * MIB, transcendentals=0),
        name="video_grads",
    )(tokens, gain, right, wqkv)


def place_kernel(scale, place_ref, d0, d1, d2, d3, qkv_ref, out_ref):
    for j, d in enumerate((d0, d1, d2, d3)):
        block = (place_ref[0] - j) % 4
        qkv_ref[:, chunk(block)] = d[:64, :] * scale

        @pl.when(block < 2)
        def _():
            qkv_ref[:, chunk(4 + block)] = d[64:, :] * scale

        @pl.when(block >= 2)
        def _():
            out_ref[:, chunk(block - 2)] = d[64:, :] * scale


def run_place(place, scale, pieces):
    vm = pl.BlockSpec(memory_space=pltpu.VMEM)
    return pl.pallas_call(
        functools.partial(place_kernel, scale),
        out_shape=(
            jax.ShapeDtypeStruct((64, 6 * CHUNK), F32),
            jax.ShapeDtypeStruct((64, 2 * CHUNK), F32),
        ),
        in_specs=[pl.BlockSpec(memory_space=pltpu.SMEM)] + [vm] * 4,
        out_specs=(vm,) * 2,
        name="place_grads",
    )(place, *pieces)


def frame_pairs(move):
    pairs = []
    for i in range(16):
        y, z, core = move(i // 4, i // 2 % 2, i % 2)
        pairs.append((i, y % 4 * 4 + z % 2 * 2 + core % 2))
    return pairs


def dp_pairs(move):
    pairs = []
    for i in range(16):
        x, h = move(i // 4, i % 4)
        pairs.append((i, x % 4 * 4 + h % 4))
    return pairs


def go_core(a):
    return lax.ppermute(a, "frame", frame_pairs(lambda y, z, c: (y, z, c + 1)))


def trade_yz(a):
    groups = [[2 * i + core for i in range(8)] for core in range(2)]
    return lax.all_to_all(a, "frame", 0, 0, tiled=True, axis_index_groups=groups)


def go_x(a, k):
    return lax.ppermute(a, "dp", dp_pairs(lambda x, h: (x + k, h)))


def go_h(a, k):
    return lax.ppermute(a, "dp", dp_pairs(lambda x, h: (x, h + k)))


def combine(own, got):
    for part in got:
        own = own + part.astype(F32)
    return own


def exchange(pieces, go):
    return [go(pieces[k], k) for k in range(1, 4)]


def pick(array, index):
    return lax.dynamic_index_in_dim(array, index, 0, keepdims=False)


def reduce_yz(own, got, yz):
    mine = (jnp.arange(8) == yz).reshape((8,) + (1,) * own.ndim)
    return jnp.sum(jnp.where(mine, own[None], got.astype(F32)), axis=0)


def local(video, cotangent, norm_gain, norm_bias, qkv_weight, out_weight):
    clips, frames_here, positions, width = video.shape
    grad_scale = 1.0 / math.sqrt(clips * positions * 256)
    frame = lax.axis_index("frame")
    dp = lax.axis_index("dp")
    yz, core = frame // 2, frame % 2
    place = jnp.stack([dp // 4, core]).astype(jnp.int32)
    gain = norm_gain.reshape(1, width)
    bias = norm_bias.reshape(1, width)
    tokens = jnp.concatenate([video, cotangent], axis=0).reshape(2 * clips, 16, positions // 16, width)
    tokens = lax.all_to_all(tokens.transpose(1, 0, 2, 3), "frame", 0, 0, tiled=True)

    send_a, keep_a, left, right = run_main(place, tokens, gain, bias, qkv_weight, out_weight)
    send_b, keep_b = run_grads(place, left, right)
    got_a, send_b = lax.optimization_barrier((go_core(send_a), send_b))
    got_b = go_core(send_b)
    own_a = pick(keep_a, yz) + pick(got_a, yz).astype(F32)
    terms_a = (keep_a + got_a.astype(F32)).astype(BF16)
    terms_b = [keep_b[0] + got_b[0].astype(F32)]
    terms_b += [(keep_b[k] + got_b[k].astype(F32)).astype(BF16) for k in range(1, 4)]
    got_a = trade_yz(terms_a)
    got_b = exchange(terms_b, go_x)
    back = run_back(tokens, gain, right, qkv_weight)
    back, got_a, got_b = lax.optimization_barrier((back, got_a, got_b))
    a = reduce_yz(own_a, got_a, yz)
    b = combine(terms_b[0], got_b)
    got_a = exchange([a[0]] + [a[k].astype(BF16) for k in range(1, 4)], go_x)
    got_b = trade_yz(b.astype(BF16))

    back, got_a, got_b = lax.optimization_barrier((back, got_a, got_b))
    back = lax.all_to_all(back, "frame", 0, 0, tiled=True)

    a = combine(a[0], got_a)
    b = reduce_yz(pick(b, yz), got_b, yz)
    own = jnp.concatenate([a, b], axis=0)
    own = combine(own, exchange([own.astype(BF16)] * 4, go_h))
    pieces = [own] + exchange([own] * 4, go_x)
    parts = [back[:, :, c * width : (c + 1) * width].reshape(positions, width) for c in range(clips)]
    grad_video = jnp.stack(parts).reshape(video.shape)
    pieces, grad_video = lax.optimization_barrier((pieces, grad_video))
    grad_qkv, grad_out = run_place(place, grad_scale, pieces)

    small = jnp.sum(back[:, :3, clips * width :].astype(F32), axis=(0, 1)).reshape(1, 1, 128)
    small = lax.all_to_all(jnp.broadcast_to(small, (16, 1, 128)), "dp", 0, 0, tiled=True)
    small = jnp.sum(small, axis=(0, 1)) * grad_scale
    return grad_video, grad_qkv, grad_out, small[:64], small[64:]


def solution(mesh):
    in_specs = (P("dp", "frame", None, None), P("dp", "frame", None, None), P(), P(), P(), P())
    out_specs = (
        P("dp", "frame", None, None),
        P("frame", None),
        P("frame", None),
        P("frame"),
        P("frame"),
    )
    return jax.shard_map(local, mesh=mesh, in_specs=in_specs, out_specs=out_specs, check_vma=False)
```

```python
import functools
import math

import jax
import jax.numpy as jnp
from jax import lax
from jax.experimental import pallas as pl
from jax.experimental.pallas import tpu as pltpu
from jax.sharding import PartitionSpec as P

F32 = jnp.float32
BF16 = jnp.bfloat16
MIB = 1024 * 1024
CHUNK = 512


def dot_nn(a, b):
    return lax.dot_general(a, b, (((1,), (0,)), ((), ())), preferred_element_type=F32)


def dot_nt(a, b):
    return lax.dot_general(a, b, (((1,), (1,)), ((), ())), preferred_element_type=F32)


def dot_tn(a, b):
    return lax.dot_general(a, b, (((0,), (0,)), ((), ())), preferred_element_type=F32)


def chunk(n):
    return pl.ds(pl.multiple_of(n * CHUNK, CHUNK), CHUNK)


def block_row(block, place):
    return pl.multiple_of(((block % 2 - place[1]) % 2 * 8 + block // 2) * 64, 64)


def read_place(place_ref):
    return tuple(place_ref[i] for i in range(2))


def whiten(xh):
    centred = xh - jnp.mean(xh, axis=-1, keepdims=True)
    inv = lax.rsqrt(jnp.mean(centred * centred, axis=-1, keepdims=True) + 1e-05)
    return centred * inv, inv


def main_kernel(
    place_ref, tokens_ref, gain_ref, bias_ref, wqkv_ref, wout_ref,
    back_ref, left_hbm, right_hbm,
    left_s, right_s, normed_s, packed_s, datt_s, wh_s, inv_s, dn_s, sems,
):
    place = read_place(place_ref)
    frames, clips, positions, width = tokens_ref.shape
    clips = clips // 2
    halves = positions // 8
    part = frames * 8
    gain = gain_ref[...]
    bias = bias_ref[...]

    def norm_step(i, carry):
        c = i // (frames // 2)
        q = i % (frames // 2)
        x = tokens_ref[pl.ds(2 * q, 2), c].astype(F32).reshape(2, halves, 8, width)
        g = tokens_ref[pl.ds(2 * q, 2), clips + c].astype(F32).reshape(2, halves, 8, width)
        for hf in range(halves):
            at = pl.multiple_of((c * halves + hf) * part + q * 16, 16)
            wh, inv = whiten(x[:, hf].reshape(16, width))
            wh_s[pl.ds(at, 16), :] = wh
            inv_s[pl.ds(at, 16), :] = jnp.broadcast_to(inv, (16, 128))
            normed_s[pl.ds(at, 16), :] = (wh * gain + bias).astype(BF16)
            right_s[pl.ds(at, 16), pl.ds(3 * width, width)] = g[:, hf].reshape(16, width).astype(BF16)
        return carry

    lax.fori_loop(0, clips * frames // 2, norm_step, 0)

    def qkv_step(n, carry):
        packed_s[:, chunk(n)] = dot_nn(normed_s[...], wqkv_ref[:, chunk(n)]).astype(BF16)
        return carry

    lax.fori_loop(0, 3 * width // CHUNK, qkv_step, 0, unroll=2)

    for n in range(width // CHUNK):
        cols = slice(n * CHUNK, (n + 1) * CHUNK)
        datt_s[:, cols] = dot_nt(right_s[:, 3 * width:], wout_ref[cols, :]).astype(BF16)
        turned = normed_s[:, cols].T
        for b in range(CHUNK // 64):
            at = block_row(n * (CHUNK // 64) + b, place)
            left_s[0, pl.ds(at, 64), :] = turned[b * 64:(b + 1) * 64]

    lane = lax.broadcasted_iota(jnp.int32, (part, 128), 1)
    first = lane < 64
    same = lax.broadcasted_iota(jnp.int32, (1, 8, part), 1) == (
        lax.broadcasted_iota(jnp.int32, (1, 8, part), 2) % 8
    )
    zero = jnp.zeros((part, 128), BF16)

    def split(a):
        return jnp.concatenate([jnp.where(first, a, zero), jnp.where(first, zero, a)], axis=0)

    def attend_step(i, carry):
        t = i // (width // 128)
        hp = i % (width // 128)
        tok = pl.ds(pl.multiple_of(t * part, part), part)
        col = pl.multiple_of(hp * 128, 128)
        q = packed_s[tok, pl.ds(col, 128)]
        k = packed_s[tok, pl.ds(width + col, 128)]
        v = packed_s[tok, pl.ds(2 * width + col, 128)]
        da = datt_s[tok, pl.ds(col, 128)]
        k2 = split(k)
        v2 = split(v)
        scores = (dot_nt(k2, q) * 0.125).reshape(2, frames, 8, part)
        e = jnp.exp(scores - jnp.max(scores, axis=1, keepdims=True))
        probs = e * (1.0 / jnp.sum(e, axis=1, keepdims=True))
        probs = jnp.where(same[None], probs, 0.0)
        low = probs.astype(BF16).reshape(2, part, part)
        dp = dot_nt(v2, da).reshape(2, frames, 8, part)
        inner = jnp.sum(dp * probs, axis=1, keepdims=True)
        ds = (probs * (dp - inner) * 0.125).astype(BF16).reshape(2, part, part)
        attended = dot_tn(v2, low.reshape(2 * part, part)).astype(BF16)
        for b in range(2):
            left_s[1, pl.ds(block_row(hp * 2 + b, place), 64), tok] = attended[b * 64:(b + 1) * 64]
        right_s[tok, pl.ds(col, 128)] = dot_tn(ds.reshape(2 * part, part), k2).astype(BF16)
        right_s[tok, pl.ds(width + col, 128)] = dot_nn(
            jnp.concatenate([ds[0], ds[1]], axis=1), split(q)
        ).astype(BF16)
        right_s[tok, pl.ds(2 * width + col, 128)] = dot_nn(
            jnp.concatenate([low[0], low[1]], axis=1), split(da)
        ).astype(BF16)
        return carry

    lax.fori_loop(0, clips * halves * (width // 128), attend_step, 0, unroll=4)

    copies = [
        pltpu.make_async_copy(left_s, left_hbm, sems.at[0]),
        pltpu.make_async_copy(right_s, right_hbm, sems.at[1]),
    ]
    for copy in copies:
        copy.start()

    for n in range(width // CHUNK):
        cols = slice(n * CHUNK, (n + 1) * CHUNK)
        dn_s[:, cols] = dot_nt(right_s[:, :3 * width], wqkv_ref[cols, :])

    def back_step(i, carry):
        dgain, dbias = carry
        c = i // (frames // 2)
        q = i % (frames // 2)
        outs = []
        for hf in range(halves):
            at = pl.multiple_of((c * halves + hf) * part + q * 16, 16)
            dn = dn_s[pl.ds(at, 16), :]
            wh = wh_s[pl.ds(at, 16), :]
            inv = inv_s[pl.ds(at, 16), :][:, :1]
            dw = dn * wh
            dgain = dgain + dw[:8] + dw[8:]
            dbias = dbias + dn[:8] + dn[8:]
            scaled = dn * gain
            m1 = jnp.mean(scaled, axis=-1, keepdims=True)
            m2 = jnp.mean(scaled * wh, axis=-1, keepdims=True)
            g = right_s[pl.ds(at, 16), pl.ds(3 * width, width)].astype(F32)
            outs.append((g + inv * (scaled - m1 - wh * m2)).reshape(2, 8, width))
        grads = jnp.concatenate(outs, axis=1).astype(BF16)
        at = pl.ds(pl.multiple_of(c * positions, positions), positions)
        for f in range(2):
            back_ref[(f - place[1]) % 2, q, at, :width] = grads[f]
        return dgain, dbias

    zeros = jnp.zeros((8, width), F32)
    dgain, dbias = lax.fori_loop(0, clips * frames // 2, back_step, (zeros, zeros))
    dgain = jnp.sum(dgain, axis=0, keepdims=True)
    dbias = jnp.sum(dbias, axis=0, keepdims=True)
    lane = lax.broadcasted_iota(jnp.int32, (1, 128), 1)
    row = lax.broadcasted_iota(jnp.int32, (16, 128), 0)
    back_ref[:, :, 16:, width:] = jnp.zeros((2, 8, clips * positions - 16, 128), BF16)
    for f in range(frames):
        at = f // 2 * 128
        a = dgain[:, at:at + 128]
        b = dbias[:, at:at + 128]
        if f % 2 == 0:
            b = jnp.concatenate([b[:, 64:], b[:, :64]], axis=1)
        else:
            a = jnp.concatenate([a[:, 64:], a[:, :64]], axis=1)
        both = jnp.where(lane < 64, a, b)
        hi = both.astype(BF16).astype(F32)
        mid = (both - hi).astype(BF16).astype(F32)
        low = both - hi - mid
        terms = jnp.where(row == 0, hi, jnp.where(row == 1, mid, jnp.where(row == 2, low, 0.0)))
        back_ref[(f % 2 - place[1]) % 2, f // 2, :16, width:] = terms.astype(BF16)
    for copy in copies:
        copy.wait()


def run_main(place, tokens, gain, bias, wqkv, wout):
    frames, clips, positions, width = tokens.shape
    clips = clips // 2
    rows = clips * frames * positions
    vm = pl.BlockSpec(memory_space=pltpu.VMEM)
    hbm = pl.BlockSpec(memory_space=pl.ANY)
    return pl.pallas_call(
        main_kernel,
        out_shape=(
            jax.ShapeDtypeStruct((2, frames // 2, clips * positions, width + 128), BF16),
            jax.ShapeDtypeStruct((2, width, rows), BF16),
            jax.ShapeDtypeStruct((rows, 4 * width), BF16),
        ),
        in_specs=[pl.BlockSpec(memory_space=pltpu.SMEM)] + [vm] * 5,
        out_specs=(vm, hbm, hbm),
        scratch_shapes=[
            pltpu.VMEM((2, width, rows), BF16),
            pltpu.VMEM((rows, 4 * width), BF16),
            pltpu.VMEM((rows, width), BF16),
            pltpu.VMEM((rows, 3 * width), BF16),
            pltpu.VMEM((rows, width), BF16),
            pltpu.VMEM((rows, width), F32),
            pltpu.VMEM((rows, 128), F32),
            pltpu.VMEM((rows, width), F32),
            pltpu.SemaphoreType.DMA((2,)),
        ],
        compiler_params=pltpu.CompilerParams(vmem_limit_bytes=36 * MIB),
        cost_estimate=pl.CostEstimate(flops=12 * 1024**3, bytes_accessed=20 * MIB, transcendentals=MIB),
        name="sublayer",
    )(place, tokens, gain, bias, wqkv, wout)


def rows_of(left_ref, sibling):
    half = left_ref.shape[1] // 2
    return left_ref[0, half:, :] if sibling else left_ref[0, :half, :]


def send_b_kernel(place_ref, left_ref, right_ref, send_ref):
    send_ref[0] = dot_nn(rows_of(left_ref, True), right_ref[...]).reshape(send_ref.shape[1:]).astype(BF16)


def own_b_kernel(place_ref, left_ref, right_ref, got_ref, own_ref, *term_refs):
    k = pl.program_id(0)
    g = dot_nn(rows_of(left_ref, False), right_ref[...]).reshape(own_ref.shape) + got_ref[0].astype(F32)

    @pl.when(k == 0)
    def _():
        own_ref[...] = g

    for i, term_ref in enumerate(term_refs):
        @pl.when(k == i + 1)
        def _():
            term_ref[...] = g.astype(BF16)


def send_a_kernel(place_ref, left_ref, right_ref, send_ref):
    send_ref[...] = dot_nn(rows_of(left_ref, True), right_ref[...]).reshape(send_ref.shape).astype(BF16)


def own_a_kernel(place_ref, left_ref, right_ref, got_ref, back_ref, theirs_ref, own_ref, message_ref, g_s):
    g = dot_nn(rows_of(left_ref, False), right_ref[...]).reshape(got_ref.shape) + got_ref[...].astype(F32)
    width = got_ref.shape[2]
    message_ref[:, :64, :width] = g.astype(BF16)
    message_ref[:, :64, width:] = jnp.zeros((8, 64, 128), BF16)
    message_ref[:, 64:96, :] = back_ref[0]
    message_ref[:, 96:, :] = theirs_ref[...]
    g_s[...] = g
    own_ref[...] = g_s[place_ref[2]]


def grads_call(kernel, name, grid, in_specs, outs, scratch=()):
    return pl.pallas_call(
        kernel,
        grid_spec=pltpu.PrefetchScalarGridSpec(
            num_scalar_prefetch=1,
            grid=grid,
            in_specs=in_specs,
            out_specs=tuple(spec for spec, _ in outs),
            scratch_shapes=scratch,
        ),
        out_shape=tuple(shape for _, shape in outs),
        compiler_params=pltpu.CompilerParams(vmem_limit_bytes=24 * MIB),
        cost_estimate=pl.CostEstimate(flops=2 * 1024**3, bytes_accessed=8 * MIB, transcendentals=0),
        name=name,
    )


def whole(*shape):
    return pl.BlockSpec(shape, lambda k, place: (0,) * len(shape))


def run_send_b(place, left, right):
    _, width, rows = left.shape
    block = (1, 8, 64, 768)
    ins = [
        whole(1, width, rows),
        pl.BlockSpec((rows, 768), lambda k, place: (0, (place[0] + k) % 4)),
    ]
    out = pl.BlockSpec(block, lambda k, place: (k, 0, 0, 0))
    outs = [(out, jax.ShapeDtypeStruct((4, 8, 64, 768), BF16))]
    return grads_call(send_b_kernel, "send_b", (4,), ins, outs)(place, left, right)[0]


def run_own_b(place, left, right, got):
    _, width, rows = left.shape
    ins = [
        whole(1, width, rows),
        pl.BlockSpec((rows, 768), lambda k, place: (0, (place[0] + k) % 4)),
        pl.BlockSpec((1, 8, 64, 768), lambda k, place: (k, 0, 0, 0)),
    ]
    outs = [(whole(8, 64, 768), jax.ShapeDtypeStruct((8, 64, 768), t)) for t in (F32, BF16, BF16, BF16)]
    return grads_call(own_b_kernel, "own_b", (4,), ins, outs)(place, left, right, got)


def run_send_a(place, left, right):
    _, width, rows = left.shape
    ins = [
        pl.BlockSpec((1, width, rows), lambda k, place: (1, 0, 0)),
        pl.BlockSpec((rows, width), lambda k, place: (0, 3)),
    ]
    outs = [(whole(8, 64, width), jax.ShapeDtypeStruct((8, 64, width), BF16))]
    return grads_call(send_a_kernel, "send_a", (1,), ins, outs)(place, left, right)[0]


def run_own_a(place, left, right, got, back, theirs):
    _, width, rows = left.shape
    ins = [
        pl.BlockSpec((1, width, rows), lambda k, place: (1, 0, 0)),
        pl.BlockSpec((rows, width), lambda k, place: (0, 3)),
        whole(8, 64, width),
        whole(1, 8, 32, width + 128),
        whole(8, 32, width + 128),
    ]
    outs = [
        (whole(64, width), jax.ShapeDtypeStruct((64, width), F32)),
        (whole(8, 128, width + 128), jax.ShapeDtypeStruct((8, 128, width + 128), BF16)),
    ]
    scratch = (pltpu.VMEM((8, 64, width), F32),)
    return grads_call(own_a_kernel, "own_a", (1,), ins, outs, scratch)(place, left, right, got, back, theirs)


def unpack_kernel(place_ref, message_ref, out_ref):
    clips = out_ref.shape[0]
    core = place_ref[1]
    for i in range(8):
        for which in range(2):
            at = pl.multiple_of(i * 32 + (which + core) % 2 * 16, 16)
            for c in range(clips):
                row = 64 + which * 32 + c * 16
                out_ref[c, pl.ds(at, 16), :] = message_ref[i, row:row + 16, :out_ref.shape[2]]


def run_unpack(place, message, clips):
    width = message.shape[2] - 128
    return pl.pallas_call(
        unpack_kernel,
        out_shape=jax.ShapeDtypeStruct((clips, 256, width), BF16),
        in_specs=[pl.BlockSpec(memory_space=pltpu.SMEM), pl.BlockSpec(memory_space=pltpu.VMEM)],
        out_specs=pl.BlockSpec(memory_space=pltpu.VMEM),
        name="unpack",
    )(place, message)


def place_kernel(scale, place_ref, d0, d1, d2, d3, qkv_ref, out_ref):
    for j, d in enumerate((d0, d1, d2, d3)):
        block = (place_ref[0] - j) % 4
        qkv_ref[:, pl.ds(pl.multiple_of(block * 768, 256), 768)] = d[:, :768] * scale
        out_ref[:, pl.ds(pl.multiple_of(block * 256, 256), 256)] = d[:, 768:] * scale


def run_place(place, scale, pieces):
    vm = pl.BlockSpec(memory_space=pltpu.VMEM)
    return pl.pallas_call(
        functools.partial(place_kernel, scale),
        out_shape=(
            jax.ShapeDtypeStruct((64, 6 * CHUNK), F32),
            jax.ShapeDtypeStruct((64, 2 * CHUNK), F32),
        ),
        in_specs=[pl.BlockSpec(memory_space=pltpu.SMEM)] + [vm] * 4,
        out_specs=(vm,) * 2,
        name="place_grads",
    )(place, *pieces)


def frame_pairs(move):
    pairs = []
    for i in range(16):
        y, z, core = move(i // 4, i // 2 % 2, i % 2)
        pairs.append((i, y % 4 * 4 + z % 2 * 2 + core % 2))
    return pairs


def dp_pairs(move):
    pairs = []
    for i in range(16):
        x, h = move(i // 4, i % 4)
        pairs.append((i, x % 4 * 4 + h % 4))
    return pairs


def go_core(a):
    return lax.ppermute(a, "frame", frame_pairs(lambda y, z, c: (y, z, c + 1)))


def trade_yz(a):
    groups = [[2 * i + core for i in range(8)] for core in range(2)]
    return lax.all_to_all(a, "frame", 0, 0, tiled=True, axis_index_groups=groups)


def go_x(a, k):
    return lax.ppermute(a, "dp", dp_pairs(lambda x, h: (x + k, h)))


def go_h(a, k):
    return lax.ppermute(a, "dp", dp_pairs(lambda x, h: (x, h + k)))


def combine(own, got):
    for part in got:
        own = own + part.astype(F32)
    return own


def exchange(pieces, go):
    return [go(pieces[k], k) for k in range(1, 4)]


def pick(array, index):
    return lax.dynamic_index_in_dim(array, index, 0, keepdims=False)


def reduce_yz(own, got, yz):
    mine = (jnp.arange(8) == yz).reshape((8,) + (1,) * own.ndim)
    return jnp.sum(jnp.where(mine, own[None], got.astype(F32)), axis=0)


def local(video, cotangent, norm_gain, norm_bias, qkv_weight, out_weight):
    clips, frames_here, positions, width = video.shape
    grad_scale = 1.0 / math.sqrt(clips * positions * 256)
    frame = lax.axis_index("frame")
    dp = lax.axis_index("dp")
    yz, core = frame // 2, frame % 2
    place = jnp.stack([dp // 4, core, yz]).astype(jnp.int32)
    gain = norm_gain.reshape(1, width)
    bias = norm_bias.reshape(1, width)
    tokens = jnp.concatenate([video, cotangent], axis=0).reshape(2 * clips, 16, positions // 16, width)
    tokens = lax.all_to_all(tokens.transpose(1, 0, 2, 3), "frame", 0, 0, tiled=True)

    back, left, right = run_main(place, tokens, gain, bias, qkv_weight, out_weight)
    theirs = go_core(back[1])

    got_a = go_core(run_send_a(place, left, right))
    send_b = run_send_b(place, left, right)
    got_a, send_b = lax.optimization_barrier((got_a, send_b))
    got_b = go_core(send_b)
    own_a, message = run_own_a(place, left, right, got_a, back, theirs)
    message = trade_yz(message)
    terms_b = run_own_b(place, left, right, got_b)
    got_b = exchange(terms_b, go_x)
    message, got_b = lax.optimization_barrier((message, got_b))

    b = combine(terms_b[0], got_b)
    got_b = trade_yz(b.astype(BF16))
    a = reduce_yz(own_a, message[:, :64, :width], yz).reshape(64, 4, 256)
    terms_a = [lax.dynamic_index_in_dim(a, (dp // 4 + k) % 4, 1, keepdims=False) for k in range(4)]
    got_a = exchange([t.astype(BF16) for t in terms_a], go_x)
    message, got_a, got_b = lax.optimization_barrier((message, got_a, got_b))

    a = combine(terms_a[0], got_a)
    b = reduce_yz(pick(b, yz), got_b, yz)
    own = jnp.concatenate([b, a], axis=1)
    own = combine(own, exchange([own.astype(BF16)] * 4, go_h))
    pieces = [own] + exchange([own] * 4, go_x)

    grad_video = run_unpack(place, message, clips).reshape(video.shape)
    small = jnp.sum(message[:, 64:, width:].astype(F32), axis=(0, 1)).reshape(1, 1, 128)
    small = lax.all_to_all(jnp.broadcast_to(small, (16, 1, 128)), "dp", 0, 0, tiled=True)
    small = jnp.sum(small, axis=(0, 1)) * grad_scale
    pieces, grad_video = lax.optimization_barrier((pieces, grad_video))
    grad_qkv, grad_out = run_place(place, grad_scale, pieces)
    return grad_video, grad_qkv, grad_out, small[:64], small[64:]


def solution(mesh):
    in_specs = (P("dp", "frame", None, None), P("dp", "frame", None, None), P(), P(), P(), P())
    out_specs = (
        P("dp", "frame", None, None),
        P("frame", None),
        P("frame", None),
        P("frame"),
        P("frame"),
    )
    return jax.shard_map(local, mesh=mesh, in_specs=in_specs, out_specs=out_specs, check_vma=False)
```

```python
import functools
import math

import jax
import jax.numpy as jnp
from jax import lax
from jax.experimental import pallas as pl
from jax.experimental.pallas import tpu as pltpu
from jax.sharding import PartitionSpec as P

F32 = jnp.float32
BF16 = jnp.bfloat16
MIB = 1024 * 1024
CHUNK = 512


def dot_nn(a, b):
    return lax.dot_general(a, b, (((1,), (0,)), ((), ())), preferred_element_type=F32)


def dot_nt(a, b):
    return lax.dot_general(a, b, (((1,), (1,)), ((), ())), preferred_element_type=F32)


def dot_tn(a, b):
    return lax.dot_general(a, b, (((0,), (0,)), ((), ())), preferred_element_type=F32)


def chunk(n):
    return pl.ds(pl.multiple_of(n * CHUNK, CHUNK), CHUNK)


def block_row(block, place):
    return pl.multiple_of(((block % 2 - place[1]) % 2 * 8 + block // 2) * 64, 64)


def read_place(place_ref):
    return tuple(place_ref[i] for i in range(2))


def whiten(xh):
    centred = xh - jnp.mean(xh, axis=-1, keepdims=True)
    inv = lax.rsqrt(jnp.mean(centred * centred, axis=-1, keepdims=True) + 1e-05)
    return centred * inv, inv


def main_kernel(
    place_ref, tokens_hbm, gain_ref, bias_ref, wqkv_hbm, wout_hbm,
    left_hbm, right_hbm, send_a_hbm, send_b_hbm,
    tokens_s, wqkv_s, wout_s, left_s, right_s, normed_s, packed_s, datt_s, send_a_s, send_b_s,
    token_sems, weight_sems, out_sems,
):
    place = read_place(place_ref)
    frames, clips, positions, width = tokens_s.shape
    clips = clips // 2
    halves = positions // 8
    part = frames * 8
    gain = gain_ref[...]
    bias = bias_ref[...]

    def load_tokens(q):
        pair = pl.ds(2 * q, 2)
        return pltpu.make_async_copy(tokens_hbm.at[pair], tokens_s.at[pair], token_sems.at[q])

    def load_wqkv(n):
        return pltpu.make_async_copy(wqkv_hbm.at[:, chunk(n)], wqkv_s.at[:, chunk(n)], weight_sems.at[n])

    blocks = 3 * width // CHUNK
    load_wout = pltpu.make_async_copy(wout_hbm, wout_s, weight_sems.at[blocks])
    for q in range(frames // 2):
        load_tokens(q).start()
    for n in range(blocks):
        load_wqkv(n).start()
    load_wout.start()

    def norm_step(q, carry):
        load_tokens(q).wait()
        for c in range(clips):
            x = tokens_s[pl.ds(2 * q, 2), c].astype(F32).reshape(2, halves, 8, width)
            g = tokens_s[pl.ds(2 * q, 2), clips + c].astype(F32).reshape(2, halves, 8, width)
            for hf in range(halves):
                at = pl.multiple_of((c * halves + hf) * part + q * 16, 16)
                wh, _ = whiten(x[:, hf].reshape(16, width))
                normed_s[pl.ds(at, 16), :] = (wh * gain + bias).astype(BF16)
                right_s[pl.ds(at, 16), pl.ds(3 * width, width)] = g[:, hf].reshape(16, width).astype(BF16)
        return carry

    lax.fori_loop(0, frames // 2, norm_step, 0)

    def qkv_step(n, carry):
        for i in range(2):
            load_wqkv(2 * n + i).wait()
        for i in range(2):
            cols = chunk(2 * n + i)
            packed_s[:, cols] = dot_nn(normed_s[...], wqkv_s[:, cols]).astype(BF16)
        return carry

    lax.fori_loop(0, blocks // 2, qkv_step, 0)
    load_wout.wait()

    for n in range(width // CHUNK):
        cols = slice(n * CHUNK, (n + 1) * CHUNK)
        datt_s[:, cols] = dot_nt(right_s[:, 3 * width:], wout_s[cols, :]).astype(BF16)
        turned = normed_s[:, cols].T
        for b in range(CHUNK // 64):
            at = block_row(n * (CHUNK // 64) + b, place)
            left_s[0, pl.ds(at, 64), :] = turned[b * 64:(b + 1) * 64]

    lane = lax.broadcasted_iota(jnp.int32, (part, 128), 1)
    first = lane < 64
    same = lax.broadcasted_iota(jnp.int32, (1, 8, part), 1) == (
        lax.broadcasted_iota(jnp.int32, (1, 8, part), 2) % 8
    )
    zero = jnp.zeros((part, 128), BF16)

    def split(a):
        return jnp.concatenate([jnp.where(first, a, zero), jnp.where(first, zero, a)], axis=0)

    def attend_step(i, carry):
        t = i // (width // 128)
        hp = i % (width // 128)
        tok = pl.ds(pl.multiple_of(t * part, part), part)
        col = pl.multiple_of(hp * 128, 128)
        q = packed_s[tok, pl.ds(col, 128)]
        k = packed_s[tok, pl.ds(width + col, 128)]
        v = packed_s[tok, pl.ds(2 * width + col, 128)]
        da = datt_s[tok, pl.ds(col, 128)]
        k2 = split(k)
        v2 = split(v)
        scores = (dot_nt(k2, q) * 0.125).reshape(2, frames, 8, part)
        e = jnp.exp(scores - jnp.max(scores, axis=1, keepdims=True))
        probs = e * (1.0 / jnp.sum(e, axis=1, keepdims=True))
        probs = jnp.where(same[None], probs, 0.0)
        low = probs.astype(BF16).reshape(2, part, part)
        dp = dot_nt(v2, da).reshape(2, frames, 8, part)
        inner = jnp.sum(dp * probs, axis=1, keepdims=True)
        ds = (probs * (dp - inner) * 0.125).astype(BF16).reshape(2, part, part)
        attended = dot_tn(v2, low.reshape(2 * part, part)).astype(BF16)
        for b in range(2):
            left_s[1, pl.ds(block_row(hp * 2 + b, place), 64), tok] = attended[b * 64:(b + 1) * 64]
        right_s[tok, pl.ds(col, 128)] = dot_tn(ds.reshape(2 * part, part), k2).astype(BF16)
        right_s[tok, pl.ds(width + col, 128)] = dot_nn(
            jnp.concatenate([ds[0], ds[1]], axis=1), split(q)
        ).astype(BF16)
        right_s[tok, pl.ds(2 * width + col, 128)] = dot_nn(
            jnp.concatenate([low[0], low[1]], axis=1), split(da)
        ).astype(BF16)
        return carry

    lax.fori_loop(0, clips * halves * (width // 128), attend_step, 0, unroll=4)

    copies = [
        pltpu.make_async_copy(left_s, left_hbm, out_sems.at[0]),
        pltpu.make_async_copy(right_s, right_hbm, out_sems.at[1]),
    ]
    g = dot_nn(left_s[1, width // 2:, :], right_s[:, 3 * width:])
    send_a_s[...] = g.reshape(send_a_s.shape).astype(BF16)
    copies.append(pltpu.make_async_copy(send_a_s, send_a_hbm, out_sems.at[2]))
    copies[-1].start()
    for k in range(4):
        cols = pl.ds(pl.multiple_of((place[0] + k) % 4 * 768, 256), 768)
        g = dot_nn(left_s[0, width // 2:, :], right_s[:, cols])
        send_b_s[k] = g.reshape(send_b_s.shape[1:]).astype(BF16)
        copies.append(pltpu.make_async_copy(send_b_s.at[k], send_b_hbm.at[k], out_sems.at[3 + k]))
        copies[-1].start()
    for copy in copies[:2]:
        copy.start()
    for copy in copies:
        copy.wait()


def run_main(place, tokens, gain, bias, wqkv, wout):
    frames, clips, positions, width = tokens.shape
    rows = clips // 2 * frames * positions
    vm = pl.BlockSpec(memory_space=pltpu.VMEM)
    hbm = pl.BlockSpec(memory_space=pl.ANY)
    outs = [(2, width, rows), (rows, 4 * width), (8, 64, width), (4, 8, 64, 768)]
    return pl.pallas_call(
        main_kernel,
        out_shape=tuple(jax.ShapeDtypeStruct(shape, BF16) for shape in outs),
        in_specs=[pl.BlockSpec(memory_space=pltpu.SMEM), hbm, vm, vm, hbm, hbm],
        out_specs=(hbm,) * 4,
        scratch_shapes=[
            pltpu.VMEM(tokens.shape, BF16),
            pltpu.VMEM(wqkv.shape, BF16),
            pltpu.VMEM(wout.shape, BF16),
            pltpu.VMEM(outs[0], BF16),
            pltpu.VMEM(outs[1], BF16),
            pltpu.VMEM((rows, width), BF16),
            pltpu.VMEM((rows, 3 * width), BF16),
            pltpu.VMEM((rows, width), BF16),
            pltpu.VMEM(outs[2], BF16),
            pltpu.VMEM(outs[3], BF16),
            pltpu.SemaphoreType.DMA((frames // 2,)),
            pltpu.SemaphoreType.DMA((3 * width // CHUNK + 1,)),
            pltpu.SemaphoreType.DMA((7,)),
        ],
        compiler_params=pltpu.CompilerParams(vmem_limit_bytes=63 * MIB),
        cost_estimate=pl.CostEstimate(flops=12 * 1024**3, bytes_accessed=20 * MIB, transcendentals=MIB),
        name="sublayer",
    )(place, tokens, gain, bias, wqkv, wout)


def back_kernel(
    place_ref, tokens_hbm, gain_ref, right_hbm, wqkv_hbm, back_ref,
    tokens_s, right_s, wqkv_s, dn_s, sems,
):
    core = place_ref[1]
    frames, clips, positions, width = tokens_s.shape
    clips = clips // 2
    halves = positions // 8
    part = frames * 8
    gain = gain_ref[...]
    load_right = pltpu.make_async_copy(right_hbm.at[:, pl.ds(0, 3 * width)], right_s, sems.at[0])
    load_right.start()
    loads = []
    for n in range(width // CHUNK):
        rows = pl.ds(n * CHUNK, CHUNK)
        loads.append(pltpu.make_async_copy(wqkv_hbm.at[rows], wqkv_s.at[rows], sems.at[1 + n]))
        loads[-1].start()
    load_tokens = pltpu.make_async_copy(tokens_hbm, tokens_s, sems.at[1 + len(loads)])
    load_tokens.start()
    load_right.wait()
    for n, load in enumerate(loads):
        cols = slice(n * CHUNK, (n + 1) * CHUNK)
        load.wait()
        dn_s[:, cols] = dot_nt(right_s[...], wqkv_s[cols, :])
    load_tokens.wait()

    def back_step(i, carry):
        dgain, dbias = carry
        c = i // (frames // 2)
        q = i % (frames // 2)
        x = tokens_s[pl.ds(2 * q, 2), c].astype(F32).reshape(2, halves, 8, width)
        g = tokens_s[pl.ds(2 * q, 2), clips + c].astype(F32).reshape(2, halves, 8, width)
        outs = []
        for hf in range(halves):
            at = pl.multiple_of((c * halves + hf) * part + q * 16, 16)
            dn = dn_s[pl.ds(at, 16), :]
            wh, inv = whiten(x[:, hf].reshape(16, width))
            dw = dn * wh
            dgain = dgain + dw[:8] + dw[8:]
            dbias = dbias + dn[:8] + dn[8:]
            scaled = dn * gain
            m1 = jnp.mean(scaled, axis=-1, keepdims=True)
            m2 = jnp.mean(scaled * wh, axis=-1, keepdims=True)
            grad = g[:, hf].reshape(16, width) + inv * (scaled - m1 - wh * m2)
            outs.append(grad.reshape(2, 8, width))
        grads = jnp.concatenate(outs, axis=1).astype(BF16)
        at = pl.ds(pl.multiple_of(c * positions, positions), positions)
        for f in range(2):
            back_ref[(f - core) % 2, q, at, :width] = grads[f]
        return dgain, dbias

    zeros = jnp.zeros((8, width), F32)
    dgain, dbias = lax.fori_loop(0, clips * frames // 2, back_step, (zeros, zeros))
    dgain = jnp.sum(dgain, axis=0, keepdims=True)
    dbias = jnp.sum(dbias, axis=0, keepdims=True)
    lane = lax.broadcasted_iota(jnp.int32, (1, 128), 1)
    row = lax.broadcasted_iota(jnp.int32, (16, 128), 0)
    back_ref[:, :, 16:, width:] = jnp.zeros((2, 8, clips * positions - 16, 128), BF16)
    for f in range(frames):
        at = f // 2 * 128
        a = dgain[:, at:at + 128]
        b = dbias[:, at:at + 128]
        if f % 2 == 0:
            b = jnp.concatenate([b[:, 64:], b[:, :64]], axis=1)
        else:
            a = jnp.concatenate([a[:, 64:], a[:, :64]], axis=1)
        both = jnp.where(lane < 64, a, b)
        hi = both.astype(BF16).astype(F32)
        mid = (both - hi).astype(BF16).astype(F32)
        low = both - hi - mid
        terms = jnp.where(row == 0, hi, jnp.where(row == 1, mid, jnp.where(row == 2, low, 0.0)))
        back_ref[(f % 2 - core) % 2, f // 2, :16, width:] = terms.astype(BF16)


def run_back(place, tokens, gain, right, wqkv):
    frames, clips, positions, width = tokens.shape
    clips = clips // 2
    rows = clips * frames * positions
    vm = pl.BlockSpec(memory_space=pltpu.VMEM)
    hbm = pl.BlockSpec(memory_space=pl.ANY)
    return pl.pallas_call(
        back_kernel,
        out_shape=jax.ShapeDtypeStruct((2, frames // 2, clips * positions, width + 128), BF16),
        in_specs=[pl.BlockSpec(memory_space=pltpu.SMEM), hbm, vm, hbm, hbm],
        out_specs=vm,
        scratch_shapes=[
            pltpu.VMEM(tokens.shape, BF16),
            pltpu.VMEM((rows, 3 * width), BF16),
            pltpu.VMEM(wqkv.shape, BF16),
            pltpu.VMEM((rows, width), F32),
            pltpu.SemaphoreType.DMA((4,)),
        ],
        compiler_params=pltpu.CompilerParams(vmem_limit_bytes=63 * MIB),
        cost_estimate=pl.CostEstimate(flops=4 * 1024**3, bytes_accessed=12 * MIB, transcendentals=0),
        name="video_grads",
    )(place, tokens, gain, right, wqkv)


def rows_of(left_ref, sibling):
    half = left_ref.shape[1] // 2
    return left_ref[0, half:, :] if sibling else left_ref[0, :half, :]


def own_b_kernel(place_ref, left_ref, right_ref, got_ref, own_hbm, t1, t2, t3, own_s, terms_s, sems):
    k = pl.program_id(0)
    g = dot_nn(rows_of(left_ref, False), right_ref[...]).reshape(own_s.shape) + got_ref[0].astype(F32)
    copies = [pltpu.make_async_copy(own_s, own_hbm, sems.at[0])]
    for i, term in enumerate((t1, t2, t3)):
        copies.append(pltpu.make_async_copy(terms_s.at[i], term, sems.at[i + 1]))

    @pl.when(k == 0)
    def _():
        own_s[...] = g
        copies[0].start()

    for i in range(1, 4):
        @pl.when(k == i)
        def _():
            terms_s[i - 1] = g.astype(BF16)
            copies[i].start()

    @pl.when(k == 3)
    def _():
        for copy in copies:
            copy.wait()


def own_a_kernel(place_ref, left_ref, right_ref, got_ref, back_ref, theirs_ref, own_ref, message_ref, g_s):
    g = dot_nn(rows_of(left_ref, False), right_ref[...]).reshape(got_ref.shape) + got_ref[...].astype(F32)
    width = got_ref.shape[2]
    message_ref[:, :64, :width] = g.astype(BF16)
    message_ref[:, :64, width:] = jnp.zeros((8, 64, 128), BF16)
    message_ref[:, 64:96, :] = back_ref[0]
    message_ref[:, 96:, :] = theirs_ref[...]
    g_s[...] = g
    own_ref[...] = g_s[place_ref[2]]


def grads_call(kernel, name, grid, in_specs, outs, scratch=()):
    return pl.pallas_call(
        kernel,
        grid_spec=pltpu.PrefetchScalarGridSpec(
            num_scalar_prefetch=1,
            grid=grid,
            in_specs=in_specs,
            out_specs=tuple(spec for spec, _ in outs),
            scratch_shapes=scratch,
        ),
        out_shape=tuple(shape for _, shape in outs),
        compiler_params=pltpu.CompilerParams(vmem_limit_bytes=63 * MIB),
        cost_estimate=pl.CostEstimate(flops=2 * 1024**3, bytes_accessed=8 * MIB, transcendentals=0),
        name=name,
    )


def whole(*shape):
    return pl.BlockSpec(shape, lambda k, place: (0,) * len(shape))


def run_own_b(place, left, right, got):
    _, width, rows = left.shape
    ins = [
        whole(1, width, rows),
        pl.BlockSpec((rows, 768), lambda k, place: (0, (place[0] + k) % 4)),
        pl.BlockSpec((1, 8, 64, 768), lambda k, place: (k, 0, 0, 0)),
    ]
    hbm = pl.BlockSpec(memory_space=pl.ANY)
    outs = [(hbm, jax.ShapeDtypeStruct((8, 64, 768), t)) for t in (F32, BF16, BF16, BF16)]
    scratch = (
        pltpu.VMEM((8, 64, 768), F32),
        pltpu.VMEM((3, 8, 64, 768), BF16),
        pltpu.SemaphoreType.DMA((4,)),
    )
    return grads_call(own_b_kernel, "own_b", (4,), ins, outs, scratch)(place, left, right, got)


def run_own_a(place, left, right, got, back, theirs):
    _, width, rows = left.shape
    ins = [
        pl.BlockSpec((1, width, rows), lambda k, place: (1, 0, 0)),
        pl.BlockSpec((rows, width), lambda k, place: (0, 3)),
        whole(8, 64, width),
        whole(1, 8, 32, width + 128),
        whole(8, 32, width + 128),
    ]
    outs = [
        (whole(64, width), jax.ShapeDtypeStruct((64, width), F32)),
        (whole(8, 128, width + 128), jax.ShapeDtypeStruct((8, 128, width + 128), BF16)),
    ]
    scratch = (pltpu.VMEM((8, 64, width), F32),)
    return grads_call(own_a_kernel, "own_a", (1,), ins, outs, scratch)(place, left, right, got, back, theirs)


def unpack_kernel(place_ref, message_ref, out_ref):
    clips = out_ref.shape[0]
    core = place_ref[1]
    for i in range(8):
        for which in range(2):
            at = pl.multiple_of(i * 32 + (which + core) % 2 * 16, 16)
            for c in range(clips):
                row = 64 + which * 32 + c * 16
                out_ref[c, pl.ds(at, 16), :] = message_ref[i, row:row + 16, :out_ref.shape[2]]


def run_unpack(place, message, clips):
    width = message.shape[2] - 128
    return pl.pallas_call(
        unpack_kernel,
        out_shape=jax.ShapeDtypeStruct((clips, 256, width), BF16),
        in_specs=[pl.BlockSpec(memory_space=pltpu.SMEM), pl.BlockSpec(memory_space=pltpu.VMEM)],
        out_specs=pl.BlockSpec(memory_space=pltpu.VMEM),
        name="unpack",
    )(place, message)


def place_kernel(scale, place_ref, d0, d1, d2, d3, qkv_ref, out_ref, gain_ref, bias_ref):
    small = jnp.zeros((8, 128), F32)
    for j, d in enumerate((d0, d1, d2, d3)):
        block = (place_ref[0] - j) % 4
        qkv_ref[:, pl.ds(pl.multiple_of(block * 768, 256), 768)] = d[:, :768] * scale
        out_ref[:, pl.ds(pl.multiple_of(block * 256, 256), 256)] = d[:, 768:1024] * scale
        small = small + d[:8, 1024:]
    small = jnp.sum(small, axis=0, keepdims=True) * scale
    gain_ref[...] = small[:, :64]
    bias_ref[...] = small[:, 64:]


def run_place(place, scale, pieces):
    vm = pl.BlockSpec(memory_space=pltpu.VMEM)
    return pl.pallas_call(
        functools.partial(place_kernel, scale),
        out_shape=(
            jax.ShapeDtypeStruct((64, 3072), F32),
            jax.ShapeDtypeStruct((64, 1024), F32),
            jax.ShapeDtypeStruct((1, 64), F32),
            jax.ShapeDtypeStruct((1, 64), F32),
        ),
        in_specs=[pl.BlockSpec(memory_space=pltpu.SMEM)] + [vm] * 4,
        out_specs=(vm,) * 4,
        name="place_grads",
    )(place, *pieces)


def frame_pairs(move):
    pairs = []
    for i in range(16):
        y, z, core = move(i // 4, i // 2 % 2, i % 2)
        pairs.append((i, y % 4 * 4 + z % 2 * 2 + core % 2))
    return pairs


def dp_pairs(move):
    pairs = []
    for i in range(16):
        x, h = move(i // 4, i % 4)
        pairs.append((i, x % 4 * 4 + h % 4))
    return pairs


def go_core(a):
    return lax.ppermute(a, "frame", frame_pairs(lambda y, z, c: (y, z, c + 1)))


def trade_yz(a):
    groups = [[2 * i + core for i in range(8)] for core in range(2)]
    return lax.all_to_all(a, "frame", 0, 0, tiled=True, axis_index_groups=groups)


def go_x(a, k):
    return lax.ppermute(a, "dp", dp_pairs(lambda x, h: (x + k, h)))


def go_h(a, k):
    return lax.ppermute(a, "dp", dp_pairs(lambda x, h: (x, h + k)))


def combine(own, got):
    for part in got:
        own = own + part.astype(F32)
    return own


def exchange(pieces, go):
    return [go(pieces[k], k) for k in range(1, 4)]


def pick(array, index):
    return lax.dynamic_index_in_dim(array, index, 0, keepdims=False)


def reduce_yz(own, got, yz):
    mine = (jnp.arange(8) == yz).reshape((8,) + (1,) * own.ndim)
    return jnp.sum(jnp.where(mine, own[None], got.astype(F32)), axis=0)


def three_terms(value):
    hi = lax.reduce_precision(value, 8, 7)
    mid = lax.reduce_precision(value - hi, 8, 7)
    return jnp.pad(jnp.concatenate([hi, mid, value - hi - mid], axis=0), ((0, 61), (0, 0)))


def local(video, cotangent, norm_gain, norm_bias, qkv_weight, out_weight):
    clips, frames_here, positions, width = video.shape
    grad_scale = 1.0 / math.sqrt(clips * positions * 256)
    frame = lax.axis_index("frame")
    dp = lax.axis_index("dp")
    yz, core = frame // 2, frame % 2
    place = jnp.stack([dp // 4, core, yz]).astype(jnp.int32)
    gain = norm_gain.reshape(1, width)
    bias = norm_bias.reshape(1, width)
    tokens = jnp.concatenate([video, cotangent], axis=0).reshape(2 * clips, 16, positions // 16, width)
    tokens = lax.all_to_all(tokens.transpose(1, 0, 2, 3), "frame", 0, 0, tiled=True)

    left, right, send_a, send_b = run_main(place, tokens, gain, bias, qkv_weight, out_weight)

    got_b = go_core(send_b)
    got_a = go_core(send_a)
    back = run_back(place, tokens, gain, right, qkv_weight)
    back, got_b = lax.optimization_barrier((back, got_b))
    terms_b = run_own_b(place, left, right, got_b)
    theirs = go_core(back[1])
    terms_b, got_a = lax.optimization_barrier((terms_b, got_a))
    own_a, message = run_own_a(place, left, right, got_a, back, theirs)
    message = trade_yz(message)
    got_b = exchange(terms_b, go_x)
    message, got_b = lax.optimization_barrier((message, got_b))

    b = combine(terms_b[0], got_b)
    got_b = trade_yz(b.astype(BF16))
    a = reduce_yz(own_a, message[:, :64, :width], yz).reshape(64, 4, 256)
    terms_a = [lax.dynamic_index_in_dim(a, (dp // 4 + k) % 4, 1, keepdims=False) for k in range(4)]
    got_a = exchange([t.astype(BF16) for t in terms_a], go_x)
    message, got_a, got_b = lax.optimization_barrier((message, got_a, got_b))

    a = combine(terms_a[0], got_a)
    b = reduce_yz(pick(b, yz), got_b, yz)
    small = jnp.sum(message[:, 64:, width:].astype(F32), axis=(0, 1)).reshape(1, 128)
    own = jnp.concatenate([b, a, three_terms(small)], axis=1)
    own = combine(own, exchange([own.astype(BF16)] * 4, go_h))
    pieces = [own] + exchange([own] * 4, go_x)

    grad_video = run_unpack(place, message, clips).reshape(video.shape)
    pieces, grad_video = lax.optimization_barrier((pieces, grad_video))
    grad_qkv, grad_out, total_gain, total_bias = run_place(place, grad_scale, pieces)
    return grad_video, grad_qkv, grad_out, total_gain.reshape(64), total_bias.reshape(64)


def solution(mesh):
    in_specs = (P("dp", "frame", None, None), P("dp", "frame", None, None), P(), P(), P(), P())
    out_specs = (
        P("dp", "frame", None, None),
        P("frame", None),
        P("frame", None),
        P("frame"),
        P("frame"),
    )
    return jax.shard_map(local, mesh=mesh, in_specs=in_specs, out_specs=out_specs, check_vma=False)
```

```python
import functools
import math

import jax
import jax.numpy as jnp
from jax import lax
from jax.experimental import pallas as pl
from jax.experimental.pallas import tpu as pltpu
from jax.sharding import PartitionSpec as P

F32 = jnp.float32
BF16 = jnp.bfloat16
MIB = 1024 * 1024
CHUNK = 512


def dot_nn(a, b):
    return lax.dot_general(a, b, (((1,), (0,)), ((), ())), preferred_element_type=F32)


def dot_nt(a, b):
    return lax.dot_general(a, b, (((1,), (1,)), ((), ())), preferred_element_type=F32)


def dot_tn(a, b):
    return lax.dot_general(a, b, (((0,), (0,)), ((), ())), preferred_element_type=F32)


def chunk(n):
    return pl.ds(pl.multiple_of(n * CHUNK, CHUNK), CHUNK)


def block_row(block, place):
    return pl.multiple_of(((block % 2 - place[1]) % 2 * 8 + block // 2) * 64, 64)


def read_place(place_ref):
    return tuple(place_ref[i] for i in range(2))


def whiten(xh):
    centred = xh - jnp.mean(xh, axis=-1, keepdims=True)
    inv = lax.rsqrt(jnp.mean(centred * centred, axis=-1, keepdims=True) + 1e-05)
    return centred * inv, inv


def main_kernel(
    place_ref, tokens_hbm, gain_ref, bias_ref, wqkv_hbm, wout_hbm,
    back_ref, send_a_hbm, send_b_hbm, keep_a_hbm, keep_b_hbm,
    tokens_s, wqkv_s, wout_s, left_s, right_s, normed_s, packed_s, datt_s, wh_s, inv_s, dn_s,
    send_a_s, send_b_s, keep_a_s, keep_b_s,
    token_sems, weight_sems, out_sems,
):
    place = read_place(place_ref)
    frames, clips, positions, width = tokens_s.shape
    clips = clips // 2
    halves = positions // 8
    part = frames * 8
    gain = gain_ref[...]
    bias = bias_ref[...]

    def load_tokens(q):
        pair = pl.ds(2 * q, 2)
        return pltpu.make_async_copy(tokens_hbm.at[pair], tokens_s.at[pair], token_sems.at[q])

    def load_wqkv(n):
        return pltpu.make_async_copy(wqkv_hbm.at[:, chunk(n)], wqkv_s.at[:, chunk(n)], weight_sems.at[n])

    blocks = 3 * width // CHUNK
    load_wout = pltpu.make_async_copy(wout_hbm, wout_s, weight_sems.at[blocks])
    for q in range(frames // 2):
        load_tokens(q).start()
    for n in range(blocks):
        load_wqkv(n).start()
    load_wout.start()

    def norm_step(q, carry):
        load_tokens(q).wait()
        for c in range(clips):
            x = tokens_s[pl.ds(2 * q, 2), c].astype(F32).reshape(2, halves, 8, width)
            g = tokens_s[pl.ds(2 * q, 2), clips + c].astype(F32).reshape(2, halves, 8, width)
            for hf in range(halves):
                at = pl.multiple_of((c * halves + hf) * part + q * 16, 16)
                wh, inv = whiten(x[:, hf].reshape(16, width))
                wh_s[pl.ds(at, 16), :] = wh
                inv_s[pl.ds(at, 16), :] = jnp.broadcast_to(inv, (16, 128))
                normed_s[pl.ds(at, 16), :] = (wh * gain + bias).astype(BF16)
                right_s[pl.ds(at, 16), pl.ds(3 * width, width)] = g[:, hf].reshape(16, width).astype(BF16)
        return carry

    lax.fori_loop(0, frames // 2, norm_step, 0)

    def qkv_step(n, carry):
        for i in range(2):
            load_wqkv(2 * n + i).wait()
        for i in range(2):
            cols = chunk(2 * n + i)
            packed_s[:, cols] = dot_nn(normed_s[...], wqkv_s[:, cols]).astype(BF16)
        return carry

    lax.fori_loop(0, blocks // 2, qkv_step, 0)
    load_wout.wait()

    for n in range(width // CHUNK):
        cols = slice(n * CHUNK, (n + 1) * CHUNK)
        datt_s[:, cols] = dot_nt(right_s[:, 3 * width:], wout_s[cols, :]).astype(BF16)
        turned = normed_s[:, cols].T
        for b in range(CHUNK // 64):
            at = block_row(n * (CHUNK // 64) + b, place)
            left_s[0, pl.ds(at, 64), :] = turned[b * 64:(b + 1) * 64]

    lane = lax.broadcasted_iota(jnp.int32, (part, 128), 1)
    first = lane < 64
    same = lax.broadcasted_iota(jnp.int32, (1, 8, part), 1) == (
        lax.broadcasted_iota(jnp.int32, (1, 8, part), 2) % 8
    )
    zero = jnp.zeros((part, 128), BF16)

    def split(a):
        return jnp.concatenate([jnp.where(first, a, zero), jnp.where(first, zero, a)], axis=0)

    def attend_step(i, carry):
        t = i // (width // 128)
        hp = i % (width // 128)
        tok = pl.ds(pl.multiple_of(t * part, part), part)
        col = pl.multiple_of(hp * 128, 128)
        q = packed_s[tok, pl.ds(col, 128)]
        k = packed_s[tok, pl.ds(width + col, 128)]
        v = packed_s[tok, pl.ds(2 * width + col, 128)]
        da = datt_s[tok, pl.ds(col, 128)]
        k2 = split(k)
        v2 = split(v)
        scores = (dot_nt(k2, q) * 0.125).reshape(2, frames, 8, part)
        e = jnp.exp(scores - jnp.max(scores, axis=1, keepdims=True))
        probs = e * (1.0 / jnp.sum(e, axis=1, keepdims=True))
        probs = jnp.where(same[None], probs, 0.0)
        low = probs.astype(BF16).reshape(2, part, part)
        dp = dot_nt(v2, da).reshape(2, frames, 8, part)
        inner = jnp.sum(dp * probs, axis=1, keepdims=True)
        ds = (probs * (dp - inner) * 0.125).astype(BF16).reshape(2, part, part)
        attended = dot_tn(v2, low.reshape(2 * part, part)).astype(BF16)
        for b in range(2):
            left_s[1, pl.ds(block_row(hp * 2 + b, place), 64), tok] = attended[b * 64:(b + 1) * 64]
        right_s[tok, pl.ds(col, 128)] = dot_tn(ds.reshape(2 * part, part), k2).astype(BF16)
        right_s[tok, pl.ds(width + col, 128)] = dot_nn(
            jnp.concatenate([ds[0], ds[1]], axis=1), split(q)
        ).astype(BF16)
        right_s[tok, pl.ds(2 * width + col, 128)] = dot_nn(
            jnp.concatenate([low[0], low[1]], axis=1), split(da)
        ).astype(BF16)
        return carry

    lax.fori_loop(0, clips * halves * (width // 128), attend_step, 0, unroll=4)

    half = width // 2
    copies = []

    def write(src, dst):
        copies.append(pltpu.make_async_copy(src, dst, out_sems.at[len(copies)]))
        copies[-1].start()

    for k in range(4):
        block = (place[0] + k) % 4
        lanes = slice(k * 384, k * 384 + 128)
        rhs = right_s[:, pl.ds(pl.multiple_of(2560 + block * 128, 128), 128)]
        send_a_s[:, :, lanes] = dot_nn(left_s[0, half:, :], rhs).reshape(8, 64, 128).astype(BF16)
        keep_a_s[:, :, lanes] = dot_nn(left_s[0, :half, :], rhs).reshape(8, 64, 128)
        lanes = slice(k * 384 + 128, k * 384 + 384)
        rhs = right_s[:, pl.ds(pl.multiple_of(3072 + block * 256, 256), 256)]
        send_a_s[:, :, lanes] = dot_nn(left_s[1, half:, :], rhs).reshape(8, 64, 256).astype(BF16)
        keep_a_s[:, :, lanes] = dot_nn(left_s[1, :half, :], rhs).reshape(8, 64, 256)
    write(send_a_s, send_a_hbm)
    for k in range(4):
        block = (place[0] + k) % 4
        rhs = right_s[:, pl.ds(pl.multiple_of(block * 640, 128), 640)]
        send_b_s[k] = dot_nn(left_s[0, half:, :], rhs).reshape(8, 64, 640).astype(BF16)
        write(send_b_s.at[k], send_b_hbm.at[k])
        keep_b_s[k] = dot_nn(left_s[0, :half, :], rhs).reshape(8, 64, 640)
        write(keep_b_s.at[k], keep_b_hbm.at[k])
    write(keep_a_s, keep_a_hbm)

    for n in range(width // CHUNK):
        cols = slice(n * CHUNK, (n + 1) * CHUNK)
        dn_s[:, cols] = dot_nt(right_s[:, :3 * width], wqkv_s[cols, :])

    def back_step(i, carry):
        dgain, dbias = carry
        c = i // (frames // 2)
        q = i % (frames // 2)
        outs = []
        for hf in range(halves):
            at = pl.multiple_of((c * halves + hf) * part + q * 16, 16)
            dn = dn_s[pl.ds(at, 16), :]
            wh = wh_s[pl.ds(at, 16), :]
            inv = inv_s[pl.ds(at, 16), :][:, :1]
            dw = dn * wh
            dgain = dgain + dw[:8] + dw[8:]
            dbias = dbias + dn[:8] + dn[8:]
            scaled = dn * gain
            m1 = jnp.mean(scaled, axis=-1, keepdims=True)
            m2 = jnp.mean(scaled * wh, axis=-1, keepdims=True)
            g = right_s[pl.ds(at, 16), pl.ds(3 * width, width)].astype(F32)
            outs.append((g + inv * (scaled - m1 - wh * m2)).reshape(2, 8, width))
        grads = jnp.concatenate(outs, axis=1).astype(BF16)
        at = pl.ds(pl.multiple_of(c * positions, positions), positions)
        for f in range(2):
            back_ref[(f - place[1]) % 2, q, at, :width] = grads[f]
        return dgain, dbias

    zeros = jnp.zeros((8, width), F32)
    dgain, dbias = lax.fori_loop(0, clips * frames // 2, back_step, (zeros, zeros))
    dgain = jnp.sum(dgain, axis=0, keepdims=True)
    dbias = jnp.sum(dbias, axis=0, keepdims=True)
    lane = lax.broadcasted_iota(jnp.int32, (1, 128), 1)
    row = lax.broadcasted_iota(jnp.int32, (16, 128), 0)
    back_ref[:, :, 16:, width:] = jnp.zeros((2, 8, clips * positions - 16, 128), BF16)
    for f in range(frames):
        at = f // 2 * 128
        a = dgain[:, at:at + 128]
        b = dbias[:, at:at + 128]
        if f % 2 == 0:
            b = jnp.concatenate([b[:, 64:], b[:, :64]], axis=1)
        else:
            a = jnp.concatenate([a[:, 64:], a[:, :64]], axis=1)
        both = jnp.where(lane < 64, a, b)
        hi = both.astype(BF16).astype(F32)
        mid = (both - hi).astype(BF16).astype(F32)
        low = both - hi - mid
        terms = jnp.where(row == 0, hi, jnp.where(row == 1, mid, jnp.where(row == 2, low, 0.0)))
        back_ref[(f % 2 - place[1]) % 2, f // 2, :16, width:] = terms.astype(BF16)
    for copy in copies:
        copy.wait()


def run_main(place, tokens, gain, bias, wqkv, wout):
    frames, clips, positions, width = tokens.shape
    clips = clips // 2
    rows = clips * frames * positions
    vm = pl.BlockSpec(memory_space=pltpu.VMEM)
    hbm = pl.BlockSpec(memory_space=pl.ANY)
    a, b = (8, 64, 1536), (4, 8, 64, 640)
    return pl.pallas_call(
        main_kernel,
        out_shape=(
            jax.ShapeDtypeStruct((2, frames // 2, clips * positions, width + 128), BF16),
            jax.ShapeDtypeStruct(a, BF16),
            jax.ShapeDtypeStruct(b, BF16),
            jax.ShapeDtypeStruct(a, F32),
            jax.ShapeDtypeStruct(b, F32),
        ),
        in_specs=[pl.BlockSpec(memory_space=pltpu.SMEM), hbm, vm, vm, hbm, hbm],
        out_specs=(vm, hbm, hbm, hbm, hbm),
        scratch_shapes=[
            pltpu.VMEM(tokens.shape, BF16),
            pltpu.VMEM(wqkv.shape, BF16),
            pltpu.VMEM(wout.shape, BF16),
            pltpu.VMEM((2, width, rows), BF16),
            pltpu.VMEM((rows, 4 * width), BF16),
            pltpu.VMEM((rows, width), BF16),
            pltpu.VMEM((rows, 3 * width), BF16),
            pltpu.VMEM((rows, width), BF16),
            pltpu.VMEM((rows, width), F32),
            pltpu.VMEM((rows, 128), F32),
            pltpu.VMEM((rows, width), F32),
            pltpu.VMEM(a, BF16),
            pltpu.VMEM(b, BF16),
            pltpu.VMEM(a, F32),
            pltpu.VMEM(b, F32),
            pltpu.SemaphoreType.DMA((frames // 2,)),
            pltpu.SemaphoreType.DMA((3 * width // CHUNK + 1,)),
            pltpu.SemaphoreType.DMA((10,)),
        ],
        compiler_params=pltpu.CompilerParams(vmem_limit_bytes=63 * MIB),
        cost_estimate=pl.CostEstimate(flops=12 * 1024**3, bytes_accessed=20 * MIB, transcendentals=MIB),
        name="sublayer",
    )(place, tokens, gain, bias, wqkv, wout)


def message_kernel(place_ref, keep_ref, got_ref, back_ref, theirs_ref, own_ref, message_ref):
    g = keep_ref[0] + got_ref[0].astype(F32)
    message_ref[0, :, :1536] = g.astype(BF16)
    message_ref[0, :32, 1536:] = back_ref[0, 0]
    message_ref[0, 32:, 1536:] = theirs_ref[0]

    @pl.when(pl.program_id(0) == place_ref[2])
    def _():
        own_ref[...] = g


def run_message(place, keep, got, back, theirs):
    lanes = back.shape[3]
    rows = pl.BlockSpec((1, 64, 1536), lambda k, place: (k, 0, 0))
    return pl.pallas_call(
        message_kernel,
        grid_spec=pltpu.PrefetchScalarGridSpec(
            num_scalar_prefetch=1,
            grid=(8,),
            in_specs=[
                rows,
                rows,
                pl.BlockSpec((1, 1, 32, lanes), lambda k, place: (0, k, 0, 0)),
                pl.BlockSpec((1, 32, lanes), lambda k, place: (k, 0, 0)),
            ],
            out_specs=(
                pl.BlockSpec((64, 1536), lambda k, place: (0, 0)),
                pl.BlockSpec((1, 64, 1536 + lanes), lambda k, place: (k, 0, 0)),
            ),
        ),
        out_shape=(
            jax.ShapeDtypeStruct((64, 1536), F32),
            jax.ShapeDtypeStruct((8, 64, 1536 + lanes), BF16),
        ),
        compiler_params=pltpu.CompilerParams(vmem_limit_bytes=63 * MIB),
        cost_estimate=pl.CostEstimate(flops=MIB, bytes_accessed=9 * MIB, transcendentals=0),
        name="message",
    )(place, keep, got, back, theirs)


def unpack_kernel(place_ref, message_ref, out_ref):
    clips, _, width = out_ref.shape
    for which in range(2):
        at = pl.multiple_of((which + place_ref[1]) % 2 * 16, 16)
        for c in range(clips):
            row = which * 32 + c * 16
            out_ref[c, pl.ds(at, 16), :] = message_ref[0, row:row + 16, 1536:1536 + width]


def run_unpack(place, message, clips, width):
    return pl.pallas_call(
        unpack_kernel,
        grid_spec=pltpu.PrefetchScalarGridSpec(
            num_scalar_prefetch=1,
            grid=(8,),
            in_specs=[pl.BlockSpec((1,) + message.shape[1:], lambda k, place: (k, 0, 0))],
            out_specs=pl.BlockSpec((clips, 32, width), lambda k, place: (0, k, 0)),
        ),
        out_shape=jax.ShapeDtypeStruct((clips, 256, width), BF16),
        compiler_params=pltpu.CompilerParams(vmem_limit_bytes=63 * MIB),
        name="unpack",
    )(place, message)


def place_kernel(scale, place_ref, d0, d1, d2, d3, qkv_ref, out_ref, gain_ref, bias_ref):
    small = jnp.zeros((8, 128), F32)
    for j, d in enumerate((d0, d1, d2, d3)):
        block = (place_ref[0] - j) % 4
        qkv_ref[:, pl.ds(pl.multiple_of(block * 640, 128), 640)] = d[:, :640] * scale
        qkv_ref[:, pl.ds(pl.multiple_of(2560 + block * 128, 128), 128)] = d[:, 640:768] * scale
        out_ref[:, pl.ds(pl.multiple_of(block * 256, 256), 256)] = d[:, 768:1024] * scale
        small = small + d[:8, 1024:]
    small = jnp.sum(small, axis=0, keepdims=True) * scale
    gain_ref[...] = small[:, :64]
    bias_ref[...] = small[:, 64:]


def run_place(place, scale, pieces):
    vm = pl.BlockSpec(memory_space=pltpu.VMEM)
    return pl.pallas_call(
        functools.partial(place_kernel, scale),
        out_shape=(
            jax.ShapeDtypeStruct((64, 3072), F32),
            jax.ShapeDtypeStruct((64, 1024), F32),
            jax.ShapeDtypeStruct((1, 64), F32),
            jax.ShapeDtypeStruct((1, 64), F32),
        ),
        in_specs=[pl.BlockSpec(memory_space=pltpu.SMEM)] + [vm] * 4,
        out_specs=(vm,) * 4,
        name="place_grads",
    )(place, *pieces)


def frame_pairs(move):
    pairs = []
    for i in range(16):
        y, z, core = move(i // 4, i // 2 % 2, i % 2)
        pairs.append((i, y % 4 * 4 + z % 2 * 2 + core % 2))
    return pairs


def dp_pairs(move):
    pairs = []
    for i in range(16):
        x, h = move(i // 4, i % 4)
        pairs.append((i, x % 4 * 4 + h % 4))
    return pairs


def go_core(a):
    return lax.ppermute(a, "frame", frame_pairs(lambda y, z, c: (y, z, c + 1)))


def trade_yz(a):
    groups = [[2 * i + core for i in range(8)] for core in range(2)]
    return lax.all_to_all(a, "frame", 0, 0, tiled=True, axis_index_groups=groups)


def go_x(a, k):
    return lax.ppermute(a, "dp", dp_pairs(lambda x, h: (x + k, h)))


def go_h(a, k):
    return lax.ppermute(a, "dp", dp_pairs(lambda x, h: (x, h + k)))


def combine(own, got):
    for part in got:
        own = own + part.astype(F32)
    return own


def exchange(pieces, go):
    return [go(pieces[k], k) for k in range(1, 4)]


def pick(array, index):
    return lax.dynamic_index_in_dim(array, index, 0, keepdims=False)


def reduce_yz(own, got, yz):
    mine = (jnp.arange(8) == yz).reshape((8,) + (1,) * own.ndim)
    return jnp.sum(jnp.where(mine, own[None], got.astype(F32)), axis=0)


def three_terms(value):
    hi = lax.reduce_precision(value, 8, 7)
    mid = lax.reduce_precision(value - hi, 8, 7)
    return jnp.pad(jnp.concatenate([hi, mid, value - hi - mid], axis=0), ((0, 61), (0, 0)))


def local(video, cotangent, norm_gain, norm_bias, qkv_weight, out_weight):
    clips, frames_here, positions, width = video.shape
    grad_scale = 1.0 / math.sqrt(clips * positions * 256)
    frame = lax.axis_index("frame")
    dp = lax.axis_index("dp")
    yz, core = frame // 2, frame % 2
    place = jnp.stack([dp // 4, core, yz]).astype(jnp.int32)
    gain = norm_gain.reshape(1, width)
    bias = norm_bias.reshape(1, width)
    tokens = jnp.concatenate([video, cotangent], axis=0).reshape(2 * clips, 16, positions // 16, width)
    tokens = lax.all_to_all(tokens.transpose(1, 0, 2, 3), "frame", 0, 0, tiled=True)

    back, send_a, send_b, keep_a, keep_b = run_main(place, tokens, gain, bias, qkv_weight, out_weight)

    got_a = go_core(send_a)
    theirs = go_core(back[1])
    got_b = go_core(send_b)
    own_a, message = run_message(place, keep_a, got_a, back, theirs)
    message = trade_yz(message)
    terms_b = [keep_b[0] + got_b[0].astype(F32)]
    terms_b += [(keep_b[k] + got_b[k].astype(F32)).astype(BF16) for k in range(1, 4)]
    got_b = exchange(terms_b, go_x)
    message, got_b = lax.optimization_barrier((message, got_b))

    b = combine(terms_b[0], got_b)
    got_b = trade_yz(b.astype(BF16))
    a = reduce_yz(own_a, message[:, :, :1536], yz)
    terms_a = [a[:, k * 384 : (k + 1) * 384] for k in range(4)]
    got_a = exchange([t.astype(BF16) for t in terms_a], go_x)
    message, got_a, got_b = lax.optimization_barrier((message, got_a, got_b))

    a = combine(terms_a[0], got_a)
    b = reduce_yz(pick(b, yz), got_b, yz)
    small = jnp.sum(message[:, :, 1536 + width :].astype(F32), axis=(0, 1)).reshape(1, 128)
    own = jnp.concatenate([b, a, three_terms(small)], axis=1)
    own = combine(own, exchange([own.astype(BF16)] * 4, go_h))
    pieces = [own] + exchange([own] * 4, go_x)

    grad_video = run_unpack(place, message, clips, width).reshape(video.shape)
    pieces, grad_video = lax.optimization_barrier((pieces, grad_video))
    grad_qkv, grad_out, total_gain, total_bias = run_place(place, grad_scale, pieces)
    return grad_video, grad_qkv, grad_out, total_gain.reshape(64), total_bias.reshape(64)


def solution(mesh):
    in_specs = (P("dp", "frame", None, None), P("dp", "frame", None, None), P(), P(), P(), P())
    out_specs = (
        P("dp", "frame", None, None),
        P("frame", None),
        P("frame", None),
        P("frame"),
        P("frame"),
    )
    return jax.shard_map(local, mesh=mesh, in_specs=in_specs, out_specs=out_specs, check_vma=False)
```

```python
import functools
import math

import jax
import jax.numpy as jnp
from jax import lax
from jax.experimental import pallas as pl
from jax.experimental.pallas import tpu as pltpu
from jax.sharding import PartitionSpec as P

F32 = jnp.float32
BF16 = jnp.bfloat16
MIB = 1024 * 1024
CHUNK = 512


def dot_nn(a, b):
    return lax.dot_general(a, b, (((1,), (0,)), ((), ())), preferred_element_type=F32)


def dot_nt(a, b):
    return lax.dot_general(a, b, (((1,), (1,)), ((), ())), preferred_element_type=F32)


def dot_tn(a, b):
    return lax.dot_general(a, b, (((0,), (0,)), ((), ())), preferred_element_type=F32)


def chunk(n):
    return pl.ds(pl.multiple_of(n * CHUNK, CHUNK), CHUNK)


def block_row(block, place):
    return pl.multiple_of(((block % 2 - place[1]) % 2 * 8 + block // 2) * 64, 64)


def read_place(place_ref):
    return tuple(place_ref[i] for i in range(2))


def whiten(xh):
    centred = xh - jnp.mean(xh, axis=-1, keepdims=True)
    inv = lax.rsqrt(jnp.mean(centred * centred, axis=-1, keepdims=True) + 1e-05)
    return centred * inv, inv


def main_kernel(
    place_ref, tokens_hbm, gain_ref, bias_ref, wqkv_hbm, wout_hbm,
    back_hbm, theirs_hbm, send_a_hbm, send_b_hbm, keep_a_hbm, keep_b_hbm,
    tokens_s, wqkv_s, wout_s, left_s, right_s, normed_s, packed_s, datt_s, wh_s, inv_s, dn_s,
    send_a_s, send_b_s, keep_a_s, keep_b_s, back_ref,
    token_sems, weight_sems, out_sems,
):
    place = read_place(place_ref)
    frames, clips, positions, width = tokens_s.shape
    clips = clips // 2
    halves = positions // 8
    part = frames * 8
    gain = gain_ref[...]
    bias = bias_ref[...]

    def load_tokens(q):
        pair = pl.ds(2 * q, 2)
        return pltpu.make_async_copy(tokens_hbm.at[pair], tokens_s.at[pair], token_sems.at[q])

    def load_wqkv(n):
        return pltpu.make_async_copy(wqkv_hbm.at[:, chunk(n)], wqkv_s.at[:, chunk(n)], weight_sems.at[n])

    blocks = 3 * width // CHUNK
    load_wout = pltpu.make_async_copy(wout_hbm, wout_s, weight_sems.at[blocks])
    for q in range(frames // 2):
        load_tokens(q).start()
    for n in range(blocks):
        load_wqkv(n).start()
    load_wout.start()

    def norm_step(q, carry):
        load_tokens(q).wait()
        for c in range(clips):
            x = tokens_s[pl.ds(2 * q, 2), c].astype(F32).reshape(2, halves, 8, width)
            g = tokens_s[pl.ds(2 * q, 2), clips + c].astype(F32).reshape(2, halves, 8, width)
            for hf in range(halves):
                at = pl.multiple_of((c * halves + hf) * part + q * 16, 16)
                wh, inv = whiten(x[:, hf].reshape(16, width))
                wh_s[pl.ds(at, 16), :] = wh
                inv_s[pl.ds(at, 16), :] = jnp.broadcast_to(inv, (16, 128))
                normed_s[pl.ds(at, 16), :] = (wh * gain + bias).astype(BF16)
                right_s[pl.ds(at, 16), pl.ds(3 * width, width)] = g[:, hf].reshape(16, width).astype(BF16)
        return carry

    lax.fori_loop(0, frames // 2, norm_step, 0, unroll=2)

    def qkv_step(n, carry):
        for i in range(2):
            load_wqkv(2 * n + i).wait()
        for i in range(2):
            cols = chunk(2 * n + i)
            packed_s[:, cols] = dot_nn(normed_s[...], wqkv_s[:, cols]).astype(BF16)
        return carry

    lax.fori_loop(0, blocks // 2, qkv_step, 0)
    load_wout.wait()

    for n in range(width // CHUNK):
        cols = slice(n * CHUNK, (n + 1) * CHUNK)
        datt_s[:, cols] = dot_nt(right_s[:, 3 * width:], wout_s[cols, :]).astype(BF16)
        turned = normed_s[:, cols].T
        for b in range(CHUNK // 64):
            at = block_row(n * (CHUNK // 64) + b, place)
            left_s[0, pl.ds(at, 64), :] = turned[b * 64:(b + 1) * 64]

    lane = lax.broadcasted_iota(jnp.int32, (part, 128), 1)
    first = lane < 64
    same = lax.broadcasted_iota(jnp.int32, (1, 8, part), 1) == (
        lax.broadcasted_iota(jnp.int32, (1, 8, part), 2) % 8
    )
    zero = jnp.zeros((part, 128), BF16)
    scale = jnp.asarray(0.125, BF16)

    def split(a):
        return jnp.concatenate([jnp.where(first, a, zero), jnp.where(first, zero, a)], axis=0)

    def attend_step(i, carry):
        t = i // (width // 128)
        hp = i % (width // 128)
        tok = pl.ds(pl.multiple_of(t * part, part), part)
        col = pl.multiple_of(hp * 128, 128)
        q = packed_s[tok, pl.ds(col, 128)]
        k = packed_s[tok, pl.ds(width + col, 128)]
        v = packed_s[tok, pl.ds(2 * width + col, 128)]
        da = datt_s[tok, pl.ds(col, 128)]
        k2 = split(k)
        v2 = split(v)
        scores = dot_nt(k2, q * scale).reshape(2, frames, 8, part)
        e = jnp.exp(scores - jnp.max(scores, axis=1, keepdims=True))
        probs = e * (1.0 / jnp.sum(e, axis=1, keepdims=True))
        probs = jnp.where(same[None], probs, 0.0)
        low = probs.astype(BF16).reshape(2, part, part)
        dp = dot_nt(v2, da * scale).reshape(2, frames, 8, part)
        inner = jnp.sum(dp * probs, axis=1, keepdims=True)
        ds = (probs * (dp - inner)).astype(BF16).reshape(2, part, part)
        attended = dot_tn(v2, low.reshape(2 * part, part)).astype(BF16)
        for b in range(2):
            left_s[1, pl.ds(block_row(hp * 2 + b, place), 64), tok] = attended[b * 64:(b + 1) * 64]
        right_s[tok, pl.ds(col, 128)] = dot_tn(ds.reshape(2 * part, part), k2).astype(BF16)
        right_s[tok, pl.ds(width + col, 128)] = dot_nn(
            jnp.concatenate([ds[0], ds[1]], axis=1), split(q)
        ).astype(BF16)
        right_s[tok, pl.ds(2 * width + col, 128)] = dot_nn(
            jnp.concatenate([low[0], low[1]], axis=1), split(da)
        ).astype(BF16)
        return carry

    lax.fori_loop(0, clips * halves * (width // 128), attend_step, 0, unroll=8)

    half = width // 2
    copies = []

    def write(src, dst):
        copies.append(pltpu.make_async_copy(src, dst, out_sems.at[len(copies)]))
        copies[-1].start()

    for k in range(4):
        block = (place[0] + k) % 4
        lanes = slice(k * 384, k * 384 + 128)
        rhs = right_s[:, pl.ds(pl.multiple_of(2560 + block * 128, 128), 128)]
        send_a_s[:, :, lanes] = dot_nn(left_s[0, half:, :], rhs).reshape(8, 64, 128).astype(BF16)
        keep_a_s[:, :, lanes] = dot_nn(left_s[0, :half, :], rhs).reshape(8, 64, 128)
        lanes = slice(k * 384 + 128, k * 384 + 384)
        rhs = right_s[:, pl.ds(pl.multiple_of(3072 + block * 256, 256), 256)]
        send_a_s[:, :, lanes] = dot_nn(left_s[1, half:, :], rhs).reshape(8, 64, 256).astype(BF16)
        keep_a_s[:, :, lanes] = dot_nn(left_s[1, :half, :], rhs).reshape(8, 64, 256)
    write(send_a_s, send_a_hbm)
    for k in range(4):
        block = (place[0] + k) % 4
        rhs = right_s[:, pl.ds(pl.multiple_of(block * 640, 128), 640)]
        send_b_s[k] = dot_nn(left_s[0, half:, :], rhs).reshape(8, 64, 640).astype(BF16)
        write(send_b_s.at[k], send_b_hbm.at[k])
        keep_b_s[k] = dot_nn(left_s[0, :half, :], rhs).reshape(8, 64, 640)
        write(keep_b_s.at[k], keep_b_hbm.at[k])
    write(keep_a_s, keep_a_hbm)

    for n in range(width // CHUNK):
        cols = slice(n * CHUNK, (n + 1) * CHUNK)
        dn_s[:, cols] = dot_nt(right_s[:, :3 * width], wqkv_s[cols, :])

    def back_step(i, carry):
        dgain, dbias = carry
        c = i // (frames // 2)
        q = i % (frames // 2)
        outs = []
        for hf in range(halves):
            at = pl.multiple_of((c * halves + hf) * part + q * 16, 16)
            dn = dn_s[pl.ds(at, 16), :]
            wh = wh_s[pl.ds(at, 16), :]
            inv = inv_s[pl.ds(at, 16), :][:, :1]
            dw = dn * wh
            dgain = dgain + dw[:8] + dw[8:]
            dbias = dbias + dn[:8] + dn[8:]
            scaled = dn * gain
            m1 = jnp.mean(scaled, axis=-1, keepdims=True)
            m2 = jnp.mean(scaled * wh, axis=-1, keepdims=True)
            g = right_s[pl.ds(at, 16), pl.ds(3 * width, width)].astype(F32)
            outs.append((g + inv * (scaled - m1 - wh * m2)).reshape(2, 8, width))
        grads = jnp.concatenate(outs, axis=1).astype(BF16)
        at = pl.ds(pl.multiple_of(c * positions, positions), positions)
        for f in range(2):
            back_ref[(f - place[1]) % 2, q, at, :width] = grads[f]
        return dgain, dbias

    zeros = jnp.zeros((8, width), F32)
    dgain, dbias = lax.fori_loop(0, clips * frames // 2, back_step, (zeros, zeros), unroll=2)
    dgain = jnp.sum(dgain, axis=0, keepdims=True)
    dbias = jnp.sum(dbias, axis=0, keepdims=True)
    lane = lax.broadcasted_iota(jnp.int32, (1, 128), 1)
    row = lax.broadcasted_iota(jnp.int32, (16, 128), 0)
    back_ref[:, :, 16:, width:] = jnp.zeros((2, 8, clips * positions - 16, 128), BF16)
    for f in range(frames):
        at = f // 2 * 128
        a = dgain[:, at:at + 128]
        b = dbias[:, at:at + 128]
        if f % 2 == 0:
            b = jnp.concatenate([b[:, 64:], b[:, :64]], axis=1)
        else:
            a = jnp.concatenate([a[:, 64:], a[:, :64]], axis=1)
        both = jnp.where(lane < 64, a, b)
        hi = both.astype(BF16).astype(F32)
        mid = (both - hi).astype(BF16).astype(F32)
        low = both - hi - mid
        terms = jnp.where(row == 0, hi, jnp.where(row == 1, mid, jnp.where(row == 2, low, 0.0)))
        back_ref[(f % 2 - place[1]) % 2, f // 2, :16, width:] = terms.astype(BF16)
    write(back_ref.at[1], theirs_hbm)
    write(back_ref.at[0], back_hbm)
    for copy in copies:
        copy.wait()


def run_main(place, tokens, gain, bias, wqkv, wout):
    frames, clips, positions, width = tokens.shape
    clips = clips // 2
    rows = clips * frames * positions
    vm = pl.BlockSpec(memory_space=pltpu.VMEM)
    hbm = pl.BlockSpec(memory_space=pl.ANY)
    a, b = (8, 64, 1536), (4, 8, 64, 640)
    back = (frames // 2, clips * positions, width + 128)
    return pl.pallas_call(
        main_kernel,
        out_shape=(
            jax.ShapeDtypeStruct(back, BF16),
            jax.ShapeDtypeStruct(back, BF16),
            jax.ShapeDtypeStruct(a, BF16),
            jax.ShapeDtypeStruct(b, BF16),
            jax.ShapeDtypeStruct(a, F32),
            jax.ShapeDtypeStruct(b, F32),
        ),
        in_specs=[pl.BlockSpec(memory_space=pltpu.SMEM), hbm, vm, vm, hbm, hbm],
        out_specs=(hbm,) * 6,
        scratch_shapes=[
            pltpu.VMEM(tokens.shape, BF16),
            pltpu.VMEM(wqkv.shape, BF16),
            pltpu.VMEM(wout.shape, BF16),
            pltpu.VMEM((2, width, rows), BF16),
            pltpu.VMEM((rows, 4 * width), BF16),
            pltpu.VMEM((rows, width), BF16),
            pltpu.VMEM((rows, 3 * width), BF16),
            pltpu.VMEM((rows, width), BF16),
            pltpu.VMEM((rows, width), F32),
            pltpu.VMEM((rows, 128), F32),
            pltpu.VMEM((rows, width), F32),
            pltpu.VMEM(a, BF16),
            pltpu.VMEM(b, BF16),
            pltpu.VMEM(a, F32),
            pltpu.VMEM(b, F32),
            pltpu.VMEM((2,) + back, BF16),
            pltpu.SemaphoreType.DMA((frames // 2,)),
            pltpu.SemaphoreType.DMA((3 * width // CHUNK + 1,)),
            pltpu.SemaphoreType.DMA((12,)),
        ],
        compiler_params=pltpu.CompilerParams(vmem_limit_bytes=63 * MIB),
        cost_estimate=pl.CostEstimate(flops=12 * 1024**3, bytes_accessed=20 * MIB, transcendentals=MIB),
        name="sublayer",
    )(place, tokens, gain, bias, wqkv, wout)


def message_kernel(place_ref, keep_ref, got_ref, back_ref, theirs_ref, own_ref, message_ref):
    message_ref[:, :32, 1536:] = back_ref[...]
    message_ref[:, 32:, 1536:] = theirs_ref[...]
    for i in range(4):
        g = keep_ref[i] + got_ref[i].astype(F32)
        message_ref[i, :, :1536] = g.astype(BF16)

        @pl.when(pl.program_id(0) * 4 + i == place_ref[2])
        def _():
            own_ref[...] = g


def step_call(kernel, name, in_blocks, outs):
    def spec(shape):
        if len(shape) == 2:
            return pl.BlockSpec(shape, lambda k, place: (0, 0))
        return pl.BlockSpec((4,) + shape[1:], lambda k, place: (k, 0, 0))

    return pl.pallas_call(
        kernel,
        grid_spec=pltpu.PrefetchScalarGridSpec(
            num_scalar_prefetch=1,
            grid=(2,),
            in_specs=[spec(shape) for shape in in_blocks],
            out_specs=tuple(spec(shape) for shape, _ in outs),
        ),
        out_shape=tuple(jax.ShapeDtypeStruct(shape, dtype) for shape, dtype in outs),
        compiler_params=pltpu.CompilerParams(vmem_limit_bytes=63 * MIB),
        cost_estimate=pl.CostEstimate(flops=MIB, bytes_accessed=9 * MIB, transcendentals=0),
        name=name,
    )


def run_message(place, keep, got, back, theirs):
    ins = [keep.shape, got.shape, back.shape, theirs.shape]
    outs = [((64, 1536), F32), ((8, 64, 1536 + back.shape[2]), BF16)]
    return step_call(message_kernel, "message", ins, outs)(place, keep, got, back, theirs)


def sum_kernel(place_ref, keep_ref, t1, t2, t3, own_ref, total_ref):
    for i in range(4):
        g = keep_ref[i] + t1[i].astype(F32) + t2[i].astype(F32) + t3[i].astype(F32)
        total_ref[i] = g.astype(BF16)

        @pl.when(pl.program_id(0) * 4 + i == place_ref[2])
        def _():
            own_ref[...] = g


def run_sum(place, keep, got):
    ins = [keep.shape] * 4
    outs = [(keep.shape[1:], F32), (keep.shape, BF16)]
    return step_call(sum_kernel, "sum_b", ins, outs)(place, keep, *got)


def unpack_kernel(place_ref, message_ref, out_ref):
    clips, rows, width = out_ref.shape
    for i in range(rows // 32):
        for which in range(2):
            at = pl.multiple_of(i * 32 + (which + place_ref[1]) % 2 * 16, 16)
            for c in range(clips):
                row = which * 32 + c * 16
                out_ref[c, pl.ds(at, 16), :] = message_ref[i, row:row + 16, 1536:1536 + width]


def run_unpack(place, message, clips, width):
    return pl.pallas_call(
        unpack_kernel,
        grid_spec=pltpu.PrefetchScalarGridSpec(
            num_scalar_prefetch=1,
            grid=(2,),
            in_specs=[pl.BlockSpec((4,) + message.shape[1:], lambda k, place: (k, 0, 0))],
            out_specs=pl.BlockSpec((clips, 128, width), lambda k, place: (0, k, 0)),
        ),
        out_shape=jax.ShapeDtypeStruct((clips, 256, width), BF16),
        compiler_params=pltpu.CompilerParams(vmem_limit_bytes=63 * MIB),
        name="unpack",
    )(place, message)


def pack_kernel(video_ref, cot_ref, out_ref):
    clips = video_ref.shape[0]
    for d in range(4):
        rows = slice(d * 16, d * 16 + 16)
        for c in range(clips):
            out_ref[d, c] = video_ref[c, 0, rows]
            out_ref[d, clips + c] = cot_ref[c, 0, rows]


def run_pack(video, cotangent):
    clips, _, positions, width = video.shape
    block = pl.BlockSpec((clips, 1, positions // 4, width), lambda k: (0, 0, k, 0))
    return pl.pallas_call(
        pack_kernel,
        grid=(4,),
        in_specs=[block, block],
        out_specs=pl.BlockSpec((4, 2 * clips, 16, width), lambda k: (k, 0, 0, 0)),
        out_shape=jax.ShapeDtypeStruct((16, 2 * clips, 16, width), BF16),
        compiler_params=pltpu.CompilerParams(vmem_limit_bytes=63 * MIB),
        name="pack",
    )(video, cotangent)


def place_kernel(scale, place_ref, d0, d1, d2, d3, qkv_ref, out_ref, gain_ref, bias_ref):
    small = jnp.zeros((8, 128), F32)
    for j, d in enumerate((d0, d1, d2, d3)):
        block = (place_ref[0] - j) % 4
        qkv_ref[:, pl.ds(pl.multiple_of(block * 640, 128), 640)] = d[:, :640] * scale
        qkv_ref[:, pl.ds(pl.multiple_of(2560 + block * 128, 128), 128)] = d[:, 640:768] * scale
        out_ref[:, pl.ds(pl.multiple_of(block * 256, 256), 256)] = d[:, 768:1024] * scale
        small = small + d[:8, 1024:]
    small = jnp.sum(small, axis=0, keepdims=True) * scale
    gain_ref[...] = small[:, :64]
    bias_ref[...] = small[:, 64:]


def run_place(place, scale, pieces):
    vm = pl.BlockSpec(memory_space=pltpu.VMEM)
    return pl.pallas_call(
        functools.partial(place_kernel, scale),
        out_shape=(
            jax.ShapeDtypeStruct((64, 3072), F32),
            jax.ShapeDtypeStruct((64, 1024), F32),
            jax.ShapeDtypeStruct((1, 64), F32),
            jax.ShapeDtypeStruct((1, 64), F32),
        ),
        in_specs=[pl.BlockSpec(memory_space=pltpu.SMEM)] + [vm] * 4,
        out_specs=(vm,) * 4,
        name="place_grads",
    )(place, *pieces)


def frame_pairs(move):
    pairs = []
    for i in range(16):
        y, z, core = move(i // 4, i // 2 % 2, i % 2)
        pairs.append((i, y % 4 * 4 + z % 2 * 2 + core % 2))
    return pairs


def dp_pairs(move):
    pairs = []
    for i in range(16):
        x, h = move(i // 4, i % 4)
        pairs.append((i, x % 4 * 4 + h % 4))
    return pairs


def go_core(a):
    return lax.ppermute(a, "frame", frame_pairs(lambda y, z, c: (y, z, c + 1)))


def trade_yz(a):
    groups = [[2 * i + core for i in range(8)] for core in range(2)]
    return lax.all_to_all(a, "frame", 0, 0, tiled=True, axis_index_groups=groups)


def go_x(a, k):
    return lax.ppermute(a, "dp", dp_pairs(lambda x, h: (x + k, h)))


def go_h(a, k):
    return lax.ppermute(a, "dp", dp_pairs(lambda x, h: (x, h + k)))


def combine(own, got):
    for part in got:
        own = own + part.astype(F32)
    return own


def exchange(pieces, go):
    return [go(pieces[k], k) for k in range(1, 4)]


def pick(array, index):
    return lax.dynamic_index_in_dim(array, index, 0, keepdims=False)


def reduce_yz(own, got, yz):
    mine = (jnp.arange(8) == yz).reshape((8,) + (1,) * own.ndim)
    return jnp.sum(jnp.where(mine, own[None], got.astype(F32)), axis=0)


def three_terms(value):
    hi = lax.reduce_precision(value, 8, 7)
    mid = lax.reduce_precision(value - hi, 8, 7)
    return jnp.pad(jnp.concatenate([hi, mid, value - hi - mid], axis=0), ((0, 61), (0, 0)))


def local(video, cotangent, norm_gain, norm_bias, qkv_weight, out_weight):
    clips, frames_here, positions, width = video.shape
    grad_scale = 1.0 / math.sqrt(clips * positions * 256)
    frame = lax.axis_index("frame")
    dp = lax.axis_index("dp")
    yz, core = frame // 2, frame % 2
    place = jnp.stack([dp // 4, core, yz]).astype(jnp.int32)
    gain = norm_gain.reshape(1, width)
    bias = norm_bias.reshape(1, width)
    tokens = lax.all_to_all(run_pack(video, cotangent), "frame", 0, 0, tiled=True)
    back, theirs, send_a, send_b, keep_a, keep_b = run_main(
        place, tokens, gain, bias, qkv_weight, out_weight
    )

    got_a = go_core(send_a)
    theirs = go_core(theirs)
    got_b = go_core(send_b)
    got_a, got_b = lax.optimization_barrier((got_a, got_b))
    own_a, message = run_message(place, keep_a, got_a, back, theirs)
    message = trade_yz(message)
    terms_b = [keep_b[0] + got_b[0].astype(F32)]
    terms_b += [(keep_b[k] + got_b[k].astype(F32)).astype(BF16) for k in range(1, 4)]
    got_b = exchange(terms_b, go_x)
    message, got_b = lax.optimization_barrier((message, got_b))

    own_b, total_b = run_sum(place, terms_b[0], got_b)
    got_b = trade_yz(total_b)
    a = reduce_yz(own_a, message[:, :, :1536], yz)
    terms_a = [a[:, k * 384 : (k + 1) * 384] for k in range(4)]
    got_a = exchange([t.astype(BF16) for t in terms_a], go_x)
    message, got_a, got_b = lax.optimization_barrier((message, got_a, got_b))

    a = combine(terms_a[0], got_a)
    b = reduce_yz(own_b, got_b, yz)
    small = jnp.sum(message[:, :, 1536 + width :].astype(F32), axis=(0, 1)).reshape(1, 128)
    own = jnp.concatenate([b, a, three_terms(small)], axis=1)
    own = combine(own, exchange([own.astype(BF16)] * 4, go_h))
    pieces = [own] + exchange([own] * 4, go_x)

    grad_video = run_unpack(place, message, clips, width).reshape(video.shape)
    pieces, grad_video = lax.optimization_barrier((pieces, grad_video))
    grad_qkv, grad_out, total_gain, total_bias = run_place(place, grad_scale, pieces)
    return grad_video, grad_qkv, grad_out, total_gain.reshape(64), total_bias.reshape(64)


def solution(mesh):
    in_specs = (P("dp", "frame", None, None), P("dp", "frame", None, None), P(), P(), P(), P())
    out_specs = (
        P("dp", "frame", None, None),
        P("frame", None),
        P("frame", None),
        P("frame"),
        P("frame"),
    )
    return jax.shard_map(local, mesh=mesh, in_specs=in_specs, out_specs=out_specs, check_vma=False)
```

```python
import functools
import math

import jax
import jax.numpy as jnp
from jax import lax
from jax.experimental import pallas as pl
from jax.experimental.pallas import tpu as pltpu
from jax.sharding import PartitionSpec as P

F32 = jnp.float32
BF16 = jnp.bfloat16
MIB = 1024 * 1024
CHUNK = 512


def dot_nn(a, b):
    return lax.dot_general(a, b, (((1,), (0,)), ((), ())), preferred_element_type=F32)


def dot_nt(a, b):
    return lax.dot_general(a, b, (((1,), (1,)), ((), ())), preferred_element_type=F32)


def dot_tn(a, b):
    return lax.dot_general(a, b, (((0,), (0,)), ((), ())), preferred_element_type=F32)


def chunk(n):
    return pl.ds(pl.multiple_of(n * CHUNK, CHUNK), CHUNK)


def block_row(block, place):
    return pl.multiple_of(((block % 2 - place[1]) % 2 * 8 + block // 2) * 64, 64)


def read_place(place_ref):
    return tuple(place_ref[i] for i in range(2))


def whiten(xh):
    centred = xh - jnp.mean(xh, axis=-1, keepdims=True)
    inv = lax.rsqrt(jnp.mean(centred * centred, axis=-1, keepdims=True) + 1e-05)
    return centred * inv, inv


def main_kernel(
    place_ref, tokens_hbm, gain_ref, bias_ref, wqkv_hbm, wout_hbm,
    back_hbm, theirs_hbm, send_a_hbm, send_b_hbm, keep_a_hbm, keep_b_hbm,
    tokens_s, wqkv_s, wout_s, left_s, right_s, normed_s, packed_s, datt_s, wh_s, inv_s, dn_s,
    send_a_s, send_b_s, keep_a_s, keep_b_s, back_ref,
    token_sems, weight_sems, out_sems,
):
    place = read_place(place_ref)
    frames, clips, positions, width = tokens_s.shape
    clips = clips // 2
    halves = positions // 8
    part = frames * 8
    gain = gain_ref[...]
    bias = bias_ref[...]

    def load_tokens(q):
        pair = pl.ds(2 * q, 2)
        return pltpu.make_async_copy(tokens_hbm.at[pair], tokens_s.at[pair], token_sems.at[q])

    def load_wqkv(n):
        return pltpu.make_async_copy(wqkv_hbm.at[:, chunk(n)], wqkv_s.at[:, chunk(n)], weight_sems.at[n])

    blocks = 3 * width // CHUNK
    load_wout = pltpu.make_async_copy(wout_hbm, wout_s, weight_sems.at[blocks])
    for q in range(frames // 2):
        load_tokens(q).start()
    for n in range(blocks):
        load_wqkv(n).start()
    load_wout.start()

    def norm_step(q, carry):
        load_tokens(q).wait()
        for c in range(clips):
            x = tokens_s[pl.ds(2 * q, 2), c].astype(F32).reshape(2, halves, 8, width)
            g = tokens_s[pl.ds(2 * q, 2), clips + c].astype(F32).reshape(2, halves, 8, width)
            for hf in range(halves):
                at = pl.multiple_of((c * halves + hf) * part + q * 16, 16)
                wh, inv = whiten(x[:, hf].reshape(16, width))
                wh_s[pl.ds(at, 16), :] = wh
                inv_s[pl.ds(at, 16), :] = jnp.broadcast_to(inv, (16, 128))
                normed_s[pl.ds(at, 16), :] = (wh * gain + bias).astype(BF16)
                right_s[pl.ds(at, 16), pl.ds(3 * width, width)] = g[:, hf].reshape(16, width).astype(BF16)
        return carry

    lax.fori_loop(0, frames // 2, norm_step, 0, unroll=2)

    def qkv_step(n, carry):
        for i in range(2):
            load_wqkv(2 * n + i).wait()
        for i in range(2):
            cols = chunk(2 * n + i)
            packed_s[:, cols] = dot_nn(normed_s[...], wqkv_s[:, cols]).astype(BF16)
        return carry

    lax.fori_loop(0, blocks // 2, qkv_step, 0)
    load_wout.wait()

    for n in range(width // CHUNK):
        cols = slice(n * CHUNK, (n + 1) * CHUNK)
        datt_s[:, cols] = dot_nt(right_s[:, 3 * width:], wout_s[cols, :]).astype(BF16)
        turned = normed_s[:, cols].T
        for b in range(CHUNK // 64):
            at = block_row(n * (CHUNK // 64) + b, place)
            left_s[0, pl.ds(at, 64), :] = turned[b * 64:(b + 1) * 64]

    lane = lax.broadcasted_iota(jnp.int32, (part, 128), 1)
    first = lane < 64
    same = lax.broadcasted_iota(jnp.int32, (1, 8, part), 1) == (
        lax.broadcasted_iota(jnp.int32, (1, 8, part), 2) % 8
    )
    zero = jnp.zeros((part, 128), BF16)
    scale = jnp.asarray(0.125, BF16)

    def split(a):
        return jnp.concatenate([jnp.where(first, a, zero), jnp.where(first, zero, a)], axis=0)

    def attend_step(i, carry):
        t = i // (width // 128)
        hp = i % (width // 128)
        tok = pl.ds(pl.multiple_of(t * part, part), part)
        col = pl.multiple_of(hp * 128, 128)
        q = packed_s[tok, pl.ds(col, 128)]
        k = packed_s[tok, pl.ds(width + col, 128)]
        v = packed_s[tok, pl.ds(2 * width + col, 128)]
        da = datt_s[tok, pl.ds(col, 128)]
        k2 = split(k)
        v2 = split(v)
        scores = dot_nt(k2, q * scale).reshape(2, frames, 8, part)
        e = jnp.exp(scores - jnp.max(scores, axis=1, keepdims=True))
        probs = e * (1.0 / jnp.sum(e, axis=1, keepdims=True))
        probs = jnp.where(same[None], probs, 0.0)
        low = probs.astype(BF16).reshape(2, part, part)
        dp = dot_nt(v2, da * scale).reshape(2, frames, 8, part)
        inner = jnp.sum(dp * probs, axis=1, keepdims=True)
        ds = (probs * (dp - inner)).astype(BF16).reshape(2, part, part)
        attended = dot_tn(v2, low.reshape(2 * part, part)).astype(BF16)
        for b in range(2):
            left_s[1, pl.ds(block_row(hp * 2 + b, place), 64), tok] = attended[b * 64:(b + 1) * 64]
        right_s[tok, pl.ds(col, 128)] = dot_tn(ds.reshape(2 * part, part), k2).astype(BF16)
        right_s[tok, pl.ds(width + col, 128)] = dot_nn(
            jnp.concatenate([ds[0], ds[1]], axis=1), split(q)
        ).astype(BF16)
        right_s[tok, pl.ds(2 * width + col, 128)] = dot_nn(
            jnp.concatenate([low[0], low[1]], axis=1), split(da)
        ).astype(BF16)
        return carry

    lax.fori_loop(0, clips * halves * (width // 128), attend_step, 0, unroll=8)

    half = width // 2
    copies = []

    def write(src, dst):
        copies.append(pltpu.make_async_copy(src, dst, out_sems.at[len(copies)]))
        copies[-1].start()

    for k in range(4):
        block = (place[0] + k) % 4
        lanes = slice(k * 384, k * 384 + 128)
        rhs = right_s[:, pl.ds(pl.multiple_of(2560 + block * 128, 128), 128)]
        send_a_s[:, :, lanes] = dot_nn(left_s[0, half:, :], rhs).reshape(8, 64, 128).astype(BF16)
        keep_a_s[:, :, lanes] = dot_nn(left_s[0, :half, :], rhs).reshape(8, 64, 128)
        lanes = slice(k * 384 + 128, k * 384 + 384)
        rhs = right_s[:, pl.ds(pl.multiple_of(3072 + block * 256, 256), 256)]
        send_a_s[:, :, lanes] = dot_nn(left_s[1, half:, :], rhs).reshape(8, 64, 256).astype(BF16)
        keep_a_s[:, :, lanes] = dot_nn(left_s[1, :half, :], rhs).reshape(8, 64, 256)
    write(send_a_s, send_a_hbm)
    for k in range(4):
        block = (place[0] + k) % 4
        rhs = right_s[:, pl.ds(pl.multiple_of(block * 640, 128), 640)]
        send_b_s[k] = dot_nn(left_s[0, half:, :], rhs).reshape(8, 64, 640).astype(BF16)
        write(send_b_s.at[k], send_b_hbm.at[k])
        keep_b_s[k] = dot_nn(left_s[0, :half, :], rhs).reshape(8, 64, 640)
        write(keep_b_s.at[k], keep_b_hbm.at[k])
    write(keep_a_s, keep_a_hbm)

    for n in range(width // CHUNK):
        cols = slice(n * CHUNK, (n + 1) * CHUNK)
        dn_s[:, cols] = dot_nt(right_s[:, :3 * width], wqkv_s[cols, :])

    def back_step(i, carry):
        dgain, dbias = carry
        c = i // (frames // 2)
        q = i % (frames // 2)
        outs = []
        for hf in range(halves):
            at = pl.multiple_of((c * halves + hf) * part + q * 16, 16)
            dn = dn_s[pl.ds(at, 16), :]
            wh = wh_s[pl.ds(at, 16), :]
            inv = inv_s[pl.ds(at, 16), :][:, :1]
            dw = dn * wh
            dgain = dgain + dw[:8] + dw[8:]
            dbias = dbias + dn[:8] + dn[8:]
            scaled = dn * gain
            m1 = jnp.mean(scaled, axis=-1, keepdims=True)
            m2 = jnp.mean(scaled * wh, axis=-1, keepdims=True)
            g = right_s[pl.ds(at, 16), pl.ds(3 * width, width)].astype(F32)
            outs.append((g + inv * (scaled - m1 - wh * m2)).reshape(2, 8, width))
        grads = jnp.concatenate(outs, axis=1).astype(BF16)
        at = pl.ds(pl.multiple_of(c * positions, positions), positions)
        for f in range(2):
            back_ref[(f - place[1]) % 2, q, at, :width] = grads[f]
        return dgain, dbias

    zeros = jnp.zeros((8, width), F32)
    dgain, dbias = lax.fori_loop(0, clips * frames // 2, back_step, (zeros, zeros), unroll=2)
    dgain = jnp.sum(dgain, axis=0, keepdims=True)
    dbias = jnp.sum(dbias, axis=0, keepdims=True)
    lane = lax.broadcasted_iota(jnp.int32, (1, 128), 1)
    row = lax.broadcasted_iota(jnp.int32, (16, 128), 0)
    back_ref[:, :, 16:, width:] = jnp.zeros((2, 8, clips * positions - 16, 128), BF16)
    for f in range(frames):
        at = f // 2 * 128
        a = dgain[:, at:at + 128]
        b = dbias[:, at:at + 128]
        if f % 2 == 0:
            b = jnp.concatenate([b[:, 64:], b[:, :64]], axis=1)
        else:
            a = jnp.concatenate([a[:, 64:], a[:, :64]], axis=1)
        both = jnp.where(lane < 64, a, b)
        hi = both.astype(BF16).astype(F32)
        mid = (both - hi).astype(BF16).astype(F32)
        low = both - hi - mid
        terms = jnp.where(row == 0, hi, jnp.where(row == 1, mid, jnp.where(row == 2, low, 0.0)))
        back_ref[(f % 2 - place[1]) % 2, f // 2, :16, width:] = terms.astype(BF16)
    write(back_ref.at[1], theirs_hbm)
    write(back_ref.at[0], back_hbm)
    for copy in copies:
        copy.wait()


def run_main(place, tokens, gain, bias, wqkv, wout):
    frames, clips, positions, width = tokens.shape
    clips = clips // 2
    rows = clips * frames * positions
    vm = pl.BlockSpec(memory_space=pltpu.VMEM)
    hbm = pl.BlockSpec(memory_space=pl.ANY)
    a, b = (8, 64, 1536), (4, 8, 64, 640)
    back = (frames // 2, clips * positions, width + 128)
    return pl.pallas_call(
        main_kernel,
        out_shape=(
            jax.ShapeDtypeStruct(back, BF16),
            jax.ShapeDtypeStruct(back, BF16),
            jax.ShapeDtypeStruct(a, BF16),
            jax.ShapeDtypeStruct(b, BF16),
            jax.ShapeDtypeStruct(a, F32),
            jax.ShapeDtypeStruct(b, F32),
        ),
        in_specs=[pl.BlockSpec(memory_space=pltpu.SMEM), hbm, vm, vm, hbm, hbm],
        out_specs=(hbm,) * 6,
        scratch_shapes=[
            pltpu.VMEM(tokens.shape, BF16),
            pltpu.VMEM(wqkv.shape, BF16),
            pltpu.VMEM(wout.shape, BF16),
            pltpu.VMEM((2, width, rows), BF16),
            pltpu.VMEM((rows, 4 * width), BF16),
            pltpu.VMEM((rows, width), BF16),
            pltpu.VMEM((rows, 3 * width), BF16),
            pltpu.VMEM((rows, width), BF16),
            pltpu.VMEM((rows, width), F32),
            pltpu.VMEM((rows, 128), F32),
            pltpu.VMEM((rows, width), F32),
            pltpu.VMEM(a, BF16),
            pltpu.VMEM(b, BF16),
            pltpu.VMEM(a, F32),
            pltpu.VMEM(b, F32),
            pltpu.VMEM((2,) + back, BF16),
            pltpu.SemaphoreType.DMA((frames // 2,)),
            pltpu.SemaphoreType.DMA((3 * width // CHUNK + 1,)),
            pltpu.SemaphoreType.DMA((12,)),
        ],
        compiler_params=pltpu.CompilerParams(vmem_limit_bytes=63 * MIB),
        cost_estimate=pl.CostEstimate(flops=12 * 1024**3, bytes_accessed=20 * MIB, transcendentals=MIB),
        name="sublayer",
    )(place, tokens, gain, bias, wqkv, wout)


def message_kernel(place_ref, keep_ref, got_ref, back_ref, theirs_ref, own_ref, message_ref):
    message_ref[:, :32, 1536:] = back_ref[...]
    message_ref[:, 32:, 1536:] = theirs_ref[...]
    for i in range(4):
        g = keep_ref[i] + got_ref[i].astype(F32)
        message_ref[i, :, :1536] = g.astype(BF16)

        @pl.when(pl.program_id(0) * 4 + i == place_ref[2])
        def _():
            own_ref[...] = g


def step_call(kernel, name, in_blocks, outs):
    def spec(shape):
        if len(shape) == 2:
            return pl.BlockSpec(shape, lambda k, place: (0, 0))
        return pl.BlockSpec((4,) + shape[1:], lambda k, place: (k, 0, 0))

    return pl.pallas_call(
        kernel,
        grid_spec=pltpu.PrefetchScalarGridSpec(
            num_scalar_prefetch=1,
            grid=(2,),
            in_specs=[spec(shape) for shape in in_blocks],
            out_specs=tuple(spec(shape) for shape, _ in outs),
        ),
        out_shape=tuple(jax.ShapeDtypeStruct(shape, dtype) for shape, dtype in outs),
        compiler_params=pltpu.CompilerParams(vmem_limit_bytes=63 * MIB),
        cost_estimate=pl.CostEstimate(flops=MIB, bytes_accessed=9 * MIB, transcendentals=0),
        name=name,
    )


def run_message(place, keep, got, back, theirs):
    ins = [keep.shape, got.shape, back.shape, theirs.shape]
    outs = [((64, 1536), F32), ((8, 64, 1536 + back.shape[2]), BF16)]
    return step_call(message_kernel, "message", ins, outs)(place, keep, got, back, theirs)


def sum_kernel(place_ref, keep_ref, t1, t2, t3, own_ref, total_ref):
    for i in range(4):
        g = keep_ref[i] + t1[i].astype(F32) + t2[i].astype(F32) + t3[i].astype(F32)
        total_ref[i] = g.astype(BF16)

        @pl.when(pl.program_id(0) * 4 + i == place_ref[2])
        def _():
            own_ref[...] = g


def run_sum(place, keep, got):
    ins = [keep.shape] * 4
    outs = [(keep.shape[1:], F32), (keep.shape, BF16)]
    return step_call(sum_kernel, "sum_b", ins, outs)(place, keep, *got)


def unpack_kernel(place_ref, message_ref, out_ref):
    clips, rows, width = out_ref.shape
    for i in range(rows // 32):
        for which in range(2):
            at = pl.multiple_of(i * 32 + (which + place_ref[1]) % 2 * 16, 16)
            for c in range(clips):
                row = which * 32 + c * 16
                out_ref[c, pl.ds(at, 16), :] = message_ref[i, row:row + 16, 1536:1536 + width]


def run_unpack(place, message, clips, width):
    return pl.pallas_call(
        unpack_kernel,
        grid_spec=pltpu.PrefetchScalarGridSpec(
            num_scalar_prefetch=1,
            grid=(2,),
            in_specs=[pl.BlockSpec((4,) + message.shape[1:], lambda k, place: (k, 0, 0))],
            out_specs=pl.BlockSpec((clips, 128, width), lambda k, place: (0, k, 0)),
        ),
        out_shape=jax.ShapeDtypeStruct((clips, 256, width), BF16),
        compiler_params=pltpu.CompilerParams(vmem_limit_bytes=63 * MIB),
        name="unpack",
    )(place, message)


def pack_kernel(video_ref, cot_ref, out_ref, sems):
    clips = video_ref.shape[0]
    copies = []
    for c in range(clips):
        copies.append(pltpu.make_async_copy(video_ref.at[c], out_ref.at[:, c], sems.at[2 * c]))
        copies.append(pltpu.make_async_copy(cot_ref.at[c], out_ref.at[:, clips + c], sems.at[2 * c + 1]))
    for copy in copies:
        copy.start()
    for copy in copies:
        copy.wait()


def run_pack(video, cotangent):
    clips, _, positions, width = video.shape
    shape = (clips, 16, positions // 16, width)
    hbm = pl.BlockSpec(memory_space=pl.ANY)
    return pl.pallas_call(
        pack_kernel,
        in_specs=[hbm, hbm],
        out_specs=hbm,
        out_shape=jax.ShapeDtypeStruct((16, 2 * clips, positions // 16, width), BF16),
        scratch_shapes=[pltpu.SemaphoreType.DMA((2 * clips,))],
        compiler_params=pltpu.CompilerParams(vmem_limit_bytes=63 * MIB),
        name="pack",
    )(video.reshape(shape), cotangent.reshape(shape))


def terms_kernel(keep_ref, got_ref, own_ref, *term_refs):
    own_ref[...] = keep_ref[0] + got_ref[0].astype(F32)
    for i, term_ref in enumerate(term_refs):
        term_ref[...] = (keep_ref[i + 1] + got_ref[i + 1].astype(F32)).astype(BF16)


def run_terms(keep, got):
    shape = keep.shape[1:]
    ins = pl.BlockSpec((4, 2) + shape[1:], lambda k: (0, k, 0, 0))
    out = pl.BlockSpec((2,) + shape[1:], lambda k: (k, 0, 0))
    return pl.pallas_call(
        terms_kernel,
        grid=(4,),
        in_specs=[ins, ins],
        out_specs=(out,) * 4,
        out_shape=tuple(jax.ShapeDtypeStruct(shape, dtype) for dtype in (F32, BF16, BF16, BF16)),
        compiler_params=pltpu.CompilerParams(vmem_limit_bytes=63 * MIB),
        cost_estimate=pl.CostEstimate(flops=MIB, bytes_accessed=11 * MIB, transcendentals=0),
        name="terms_b",
    )(keep, got)


def place_kernel(scale, place_ref, d0, d1, d2, d3, qkv_ref, out_ref, gain_ref, bias_ref):
    small = jnp.zeros((8, 128), F32)
    for j, d in enumerate((d0, d1, d2, d3)):
        block = (place_ref[0] - j) % 4
        qkv_ref[:, pl.ds(pl.multiple_of(block * 640, 128), 640)] = d[:, :640] * scale
        qkv_ref[:, pl.ds(pl.multiple_of(2560 + block * 128, 128), 128)] = d[:, 640:768] * scale
        out_ref[:, pl.ds(pl.multiple_of(block * 256, 256), 256)] = d[:, 768:1024] * scale
        small = small + d[:8, 1024:]
    small = jnp.sum(small, axis=0, keepdims=True) * scale
    gain_ref[...] = small[:, :64]
    bias_ref[...] = small[:, 64:]


def run_place(place, scale, pieces):
    vm = pl.BlockSpec(memory_space=pltpu.VMEM)
    return pl.pallas_call(
        functools.partial(place_kernel, scale),
        out_shape=(
            jax.ShapeDtypeStruct((64, 3072), F32),
            jax.ShapeDtypeStruct((64, 1024), F32),
            jax.ShapeDtypeStruct((1, 64), F32),
            jax.ShapeDtypeStruct((1, 64), F32),
        ),
        in_specs=[pl.BlockSpec(memory_space=pltpu.SMEM)] + [vm] * 4,
        out_specs=(vm,) * 4,
        name="place_grads",
    )(place, *pieces)


def frame_pairs(move):
    pairs = []
    for i in range(16):
        y, z, core = move(i // 4, i // 2 % 2, i % 2)
        pairs.append((i, y % 4 * 4 + z % 2 * 2 + core % 2))
    return pairs


def dp_pairs(move):
    pairs = []
    for i in range(16):
        x, h = move(i // 4, i % 4)
        pairs.append((i, x % 4 * 4 + h % 4))
    return pairs


def go_core(a):
    return lax.ppermute(a, "frame", frame_pairs(lambda y, z, c: (y, z, c + 1)))


def trade_yz(a):
    groups = [[2 * i + core for i in range(8)] for core in range(2)]
    return lax.all_to_all(a, "frame", 0, 0, tiled=True, axis_index_groups=groups)


def go_x(a, k):
    return lax.ppermute(a, "dp", dp_pairs(lambda x, h: (x + k, h)))


def go_h(a, k):
    return lax.ppermute(a, "dp", dp_pairs(lambda x, h: (x, h + k)))


def combine(own, got):
    for part in got:
        own = own + part.astype(F32)
    return own


def exchange(pieces, go):
    return [go(pieces[k], k) for k in range(1, 4)]


def pick(array, index):
    return lax.dynamic_index_in_dim(array, index, 0, keepdims=False)


def reduce_yz(own, got, yz):
    mine = (jnp.arange(8) == yz).reshape((8,) + (1,) * own.ndim)
    return jnp.sum(jnp.where(mine, own[None], got.astype(F32)), axis=0)


def three_terms(value):
    hi = lax.reduce_precision(value, 8, 7)
    mid = lax.reduce_precision(value - hi, 8, 7)
    return jnp.pad(jnp.concatenate([hi, mid, value - hi - mid], axis=0), ((0, 61), (0, 0)))


def local(video, cotangent, norm_gain, norm_bias, qkv_weight, out_weight):
    clips, frames_here, positions, width = video.shape
    grad_scale = 1.0 / math.sqrt(clips * positions * 256)
    frame = lax.axis_index("frame")
    dp = lax.axis_index("dp")
    yz, core = frame // 2, frame % 2
    place = jnp.stack([dp // 4, core, yz]).astype(jnp.int32)
    gain = norm_gain.reshape(1, width)
    bias = norm_bias.reshape(1, width)
    tokens = lax.all_to_all(run_pack(video, cotangent), "frame", 0, 0, tiled=True)
    back, theirs, send_a, send_b, keep_a, keep_b = run_main(
        place, tokens, gain, bias, qkv_weight, out_weight
    )

    got_a = go_core(send_a)
    got_a, theirs, send_b = lax.optimization_barrier((got_a, go_core(theirs), send_b))
    got_b = go_core(send_b)
    own_a, message = run_message(place, keep_a, got_a, back, theirs)
    terms_b = run_terms(keep_b, got_b)
    message, terms_b = lax.optimization_barrier((message, terms_b))
    message = trade_yz(message)
    got_b = exchange(terms_b, go_x)
    message, got_b = lax.optimization_barrier((message, got_b))

    own_b, total_b = run_sum(place, terms_b[0], got_b)
    got_b = trade_yz(total_b)
    a = reduce_yz(own_a, message[:, :, :1536], yz)
    terms_a = [a[:, k * 384 : (k + 1) * 384] for k in range(4)]
    got_a = exchange([t.astype(BF16) for t in terms_a], go_x)
    message, got_a, got_b = lax.optimization_barrier((message, got_a, got_b))

    a = combine(terms_a[0], got_a)
    b = reduce_yz(own_b, got_b, yz)
    small = jnp.sum(message[:, :, 1536 + width :].astype(F32), axis=(0, 1)).reshape(1, 128)
    own = jnp.concatenate([b, a, three_terms(small)], axis=1)
    own = combine(own, exchange([own.astype(BF16)] * 4, go_h))
    pieces = [own] + exchange([own] * 4, go_x)

    grad_video = run_unpack(place, message, clips, width).reshape(video.shape)
    pieces, grad_video = lax.optimization_barrier((pieces, grad_video))
    grad_qkv, grad_out, total_gain, total_bias = run_place(place, grad_scale, pieces)
    return grad_video, grad_qkv, grad_out, total_gain.reshape(64), total_bias.reshape(64)


def solution(mesh):
    in_specs = (P("dp", "frame", None, None), P("dp", "frame", None, None), P(), P(), P(), P())
    out_specs = (
        P("dp", "frame", None, None),
        P("frame", None),
        P("frame", None),
        P("frame"),
        P("frame"),
    )
    return jax.shard_map(local, mesh=mesh, in_specs=in_specs, out_specs=out_specs, check_vma=False)
```

```python
import functools
import math

import jax
import jax.numpy as jnp
from jax import lax
from jax.experimental import pallas as pl
from jax.experimental.pallas import tpu as pltpu
from jax.sharding import PartitionSpec as P

F32 = jnp.float32
BF16 = jnp.bfloat16
MIB = 1024 * 1024
CHUNK = 512


def dot_nn(a, b):
    return lax.dot_general(a, b, (((1,), (0,)), ((), ())), preferred_element_type=F32)


def dot_nt(a, b):
    return lax.dot_general(a, b, (((1,), (1,)), ((), ())), preferred_element_type=F32)


def dot_tn(a, b):
    return lax.dot_general(a, b, (((0,), (0,)), ((), ())), preferred_element_type=F32)


def chunk(n):
    return pl.ds(pl.multiple_of(n * CHUNK, CHUNK), CHUNK)


def block_row(block, place):
    return pl.multiple_of(((block % 2 - place[1]) % 2 * 8 + block // 2) * 64, 64)


def read_place(place_ref):
    return tuple(place_ref[i] for i in range(2))


def whiten(xh):
    centred = xh - jnp.mean(xh, axis=-1, keepdims=True)
    inv = lax.rsqrt(jnp.mean(centred * centred, axis=-1, keepdims=True) + 1e-05)
    return centred * inv, inv


def main_kernel(
    place_ref, tokens_hbm, gain_ref, bias_ref, wqkv_hbm, wout_hbm,
    back_hbm, theirs_hbm, send_a_hbm, send_b_hbm, keep_a_hbm, keep_b_hbm,
    tokens_s, wqkv_s, wout_s, left_s, right_s, normed_s, packed_s, datt_s, wh_s, inv_s, dn_s,
    send_a_s, send_b_s, keep_a_s, keep_b_s, back_ref,
    token_sems, weight_sems, out_sems,
):
    place = read_place(place_ref)
    frames, clips, positions, width = tokens_s.shape
    clips = clips // 2
    halves = positions // 8
    part = frames * 8
    gain = gain_ref[...]
    bias = bias_ref[...]

    def load_tokens(q):
        pair = pl.ds(2 * q, 2)
        return pltpu.make_async_copy(tokens_hbm.at[pair], tokens_s.at[pair], token_sems.at[q])

    def load_wqkv(n):
        return pltpu.make_async_copy(wqkv_hbm.at[:, chunk(n)], wqkv_s.at[:, chunk(n)], weight_sems.at[n])

    blocks = 3 * width // CHUNK
    load_wout = pltpu.make_async_copy(wout_hbm, wout_s, weight_sems.at[blocks])
    for q in range(frames // 2):
        load_tokens(q).start()
    for n in range(blocks):
        load_wqkv(n).start()
    load_wout.start()

    def norm_step(q, carry):
        load_tokens(q).wait()
        for c in range(clips):
            x = tokens_s[pl.ds(2 * q, 2), c].astype(F32).reshape(2, halves, 8, width)
            g = tokens_s[pl.ds(2 * q, 2), clips + c].astype(F32).reshape(2, halves, 8, width)
            for hf in range(halves):
                at = pl.multiple_of((c * halves + hf) * part + q * 16, 16)
                wh, inv = whiten(x[:, hf].reshape(16, width))
                wh_s[pl.ds(at, 16), :] = wh
                inv_s[pl.ds(at, 16), :] = jnp.broadcast_to(inv, (16, 128))
                normed_s[pl.ds(at, 16), :] = (wh * gain + bias).astype(BF16)
                right_s[pl.ds(at, 16), pl.ds(3 * width, width)] = g[:, hf].reshape(16, width).astype(BF16)
        return carry

    lax.fori_loop(0, frames // 2, norm_step, 0, unroll=2)

    def qkv_step(n, carry):
        for i in range(2):
            load_wqkv(2 * n + i).wait()
        for i in range(2):
            cols = chunk(2 * n + i)
            packed_s[:, cols] = dot_nn(normed_s[...], wqkv_s[:, cols]).astype(BF16)
        return carry

    lax.fori_loop(0, blocks // 2, qkv_step, 0)
    load_wout.wait()

    for n in range(width // CHUNK):
        cols = slice(n * CHUNK, (n + 1) * CHUNK)
        datt_s[:, cols] = dot_nt(right_s[:, 3 * width:], wout_s[cols, :]).astype(BF16)
        turned = normed_s[:, cols].T
        for b in range(CHUNK // 64):
            at = block_row(n * (CHUNK // 64) + b, place)
            left_s[0, pl.ds(at, 64), :] = turned[b * 64:(b + 1) * 64]

    lane = lax.broadcasted_iota(jnp.int32, (part, 128), 1)
    first = lane < 64
    same = lax.broadcasted_iota(jnp.int32, (1, 8, part), 1) == (
        lax.broadcasted_iota(jnp.int32, (1, 8, part), 2) % 8
    )
    zero = jnp.zeros((part, 128), BF16)
    scale = jnp.asarray(0.125, BF16)

    def split(a):
        return jnp.concatenate([jnp.where(first, a, zero), jnp.where(first, zero, a)], axis=0)

    def attend_step(i, carry):
        t = i // (width // 128)
        hp = i % (width // 128)
        tok = pl.ds(pl.multiple_of(t * part, part), part)
        col = pl.multiple_of(hp * 128, 128)
        q = packed_s[tok, pl.ds(col, 128)]
        k = packed_s[tok, pl.ds(width + col, 128)]
        v = packed_s[tok, pl.ds(2 * width + col, 128)]
        da = datt_s[tok, pl.ds(col, 128)]
        k2 = split(k)
        v2 = split(v)
        scores = dot_nt(k2, q * scale).reshape(2, frames, 8, part)
        e = jnp.exp(scores - jnp.max(scores, axis=1, keepdims=True))
        probs = e * (1.0 / jnp.sum(e, axis=1, keepdims=True))
        probs = jnp.where(same[None], probs, 0.0)
        low = probs.astype(BF16).reshape(2, part, part)
        dp = dot_nt(v2, da * scale).reshape(2, frames, 8, part)
        inner = jnp.sum(dp * probs, axis=1, keepdims=True)
        ds = (probs * (dp - inner)).astype(BF16).reshape(2, part, part)
        attended = dot_tn(v2, low.reshape(2 * part, part)).astype(BF16)
        for b in range(2):
            left_s[1, pl.ds(block_row(hp * 2 + b, place), 64), tok] = attended[b * 64:(b + 1) * 64]
        right_s[tok, pl.ds(col, 128)] = dot_tn(ds.reshape(2 * part, part), k2).astype(BF16)
        right_s[tok, pl.ds(width + col, 128)] = dot_nn(
            jnp.concatenate([ds[0], ds[1]], axis=1), split(q)
        ).astype(BF16)
        right_s[tok, pl.ds(2 * width + col, 128)] = dot_nn(
            jnp.concatenate([low[0], low[1]], axis=1), split(da)
        ).astype(BF16)
        return carry

    lax.fori_loop(0, clips * halves * (width // 128), attend_step, 0, unroll=8)

    half = width // 2
    copies = []

    def write(src, dst):
        copies.append(pltpu.make_async_copy(src, dst, out_sems.at[len(copies)]))
        copies[-1].start()

    for k in range(4):
        block = (place[0] + k) % 4
        lanes = slice(k * 384, k * 384 + 128)
        rhs = right_s[:, pl.ds(pl.multiple_of(2560 + block * 128, 128), 128)]
        send_a_s[:, :, lanes] = dot_nn(left_s[0, half:, :], rhs).reshape(8, 64, 128).astype(BF16)
        keep_a_s[:, :, lanes] = dot_nn(left_s[0, :half, :], rhs).reshape(8, 64, 128)
        lanes = slice(k * 384 + 128, k * 384 + 384)
        rhs = right_s[:, pl.ds(pl.multiple_of(3072 + block * 256, 256), 256)]
        send_a_s[:, :, lanes] = dot_nn(left_s[1, half:, :], rhs).reshape(8, 64, 256).astype(BF16)
        keep_a_s[:, :, lanes] = dot_nn(left_s[1, :half, :], rhs).reshape(8, 64, 256)
    write(send_a_s, send_a_hbm)
    for k in range(4):
        block = (place[0] + k) % 4
        rhs = right_s[:, pl.ds(pl.multiple_of(block * 640, 128), 640)]
        send_b_s[k] = dot_nn(left_s[0, half:, :], rhs).reshape(8, 64, 640).astype(BF16)
        write(send_b_s.at[k], send_b_hbm.at[k])
        keep_b_s[k] = dot_nn(left_s[0, :half, :], rhs).reshape(8, 64, 640)
        write(keep_b_s.at[k], keep_b_hbm.at[k])
    write(keep_a_s, keep_a_hbm)

    for n in range(width // CHUNK):
        cols = slice(n * CHUNK, (n + 1) * CHUNK)
        dn_s[:, cols] = dot_nt(right_s[:, :3 * width], wqkv_s[cols, :])

    def back_step(i, carry):
        dgain, dbias = carry
        c = i // (frames // 2)
        q = i % (frames // 2)
        outs = []
        for hf in range(halves):
            at = pl.multiple_of((c * halves + hf) * part + q * 16, 16)
            dn = dn_s[pl.ds(at, 16), :]
            wh = wh_s[pl.ds(at, 16), :]
            inv = inv_s[pl.ds(at, 16), :][:, :1]
            dw = dn * wh
            dgain = dgain + dw[:8] + dw[8:]
            dbias = dbias + dn[:8] + dn[8:]
            scaled = dn * gain
            m1 = jnp.mean(scaled, axis=-1, keepdims=True)
            m2 = jnp.mean(scaled * wh, axis=-1, keepdims=True)
            g = right_s[pl.ds(at, 16), pl.ds(3 * width, width)].astype(F32)
            outs.append((g + inv * (scaled - m1 - wh * m2)).reshape(2, 8, width))
        grads = jnp.concatenate(outs, axis=1).astype(BF16)
        at = pl.ds(pl.multiple_of(c * positions, positions), positions)
        for f in range(2):
            back_ref[(f - place[1]) % 2, q, at, :width] = grads[f]
        return dgain, dbias

    zeros = jnp.zeros((8, width), F32)
    dgain, dbias = lax.fori_loop(0, clips * frames // 2, back_step, (zeros, zeros), unroll=2)
    dgain = jnp.sum(dgain, axis=0, keepdims=True)
    dbias = jnp.sum(dbias, axis=0, keepdims=True)
    lane = lax.broadcasted_iota(jnp.int32, (1, 128), 1)
    row = lax.broadcasted_iota(jnp.int32, (16, 128), 0)
    back_ref[:, :, 16:, width:] = jnp.zeros((2, 8, clips * positions - 16, 128), BF16)
    for f in range(frames):
        at = f // 2 * 128
        a = dgain[:, at:at + 128]
        b = dbias[:, at:at + 128]
        if f % 2 == 0:
            b = jnp.concatenate([b[:, 64:], b[:, :64]], axis=1)
        else:
            a = jnp.concatenate([a[:, 64:], a[:, :64]], axis=1)
        both = jnp.where(lane < 64, a, b)
        hi = both.astype(BF16).astype(F32)
        mid = (both - hi).astype(BF16).astype(F32)
        low = both - hi - mid
        terms = jnp.where(row == 0, hi, jnp.where(row == 1, mid, jnp.where(row == 2, low, 0.0)))
        back_ref[(f % 2 - place[1]) % 2, f // 2, :16, width:] = terms.astype(BF16)
    write(back_ref.at[1], theirs_hbm)
    write(back_ref.at[0], back_hbm)
    for copy in copies:
        copy.wait()


def run_main(place, tokens, gain, bias, wqkv, wout):
    frames, clips, positions, width = tokens.shape
    clips = clips // 2
    rows = clips * frames * positions
    vm = pl.BlockSpec(memory_space=pltpu.VMEM)
    hbm = pl.BlockSpec(memory_space=pl.ANY)
    a, b = (8, 64, 1536), (4, 8, 64, 640)
    back = (frames // 2, clips * positions, width + 128)
    return pl.pallas_call(
        main_kernel,
        out_shape=(
            jax.ShapeDtypeStruct(back, BF16),
            jax.ShapeDtypeStruct(back, BF16),
            jax.ShapeDtypeStruct(a, BF16),
            jax.ShapeDtypeStruct(b, BF16),
            jax.ShapeDtypeStruct(a, F32),
            jax.ShapeDtypeStruct(b, F32),
        ),
        in_specs=[pl.BlockSpec(memory_space=pltpu.SMEM), hbm, vm, vm, hbm, hbm],
        out_specs=(hbm,) * 6,
        scratch_shapes=[
            pltpu.VMEM(tokens.shape, BF16),
            pltpu.VMEM(wqkv.shape, BF16),
            pltpu.VMEM(wout.shape, BF16),
            pltpu.VMEM((2, width, rows), BF16),
            pltpu.VMEM((rows, 4 * width), BF16),
            pltpu.VMEM((rows, width), BF16),
            pltpu.VMEM((rows, 3 * width), BF16),
            pltpu.VMEM((rows, width), BF16),
            pltpu.VMEM((rows, width), F32),
            pltpu.VMEM((rows, 128), F32),
            pltpu.VMEM((rows, width), F32),
            pltpu.VMEM(a, BF16),
            pltpu.VMEM(b, BF16),
            pltpu.VMEM(a, F32),
            pltpu.VMEM(b, F32),
            pltpu.VMEM((2,) + back, BF16),
            pltpu.SemaphoreType.DMA((frames // 2,)),
            pltpu.SemaphoreType.DMA((3 * width // CHUNK + 1,)),
            pltpu.SemaphoreType.DMA((12,)),
        ],
        compiler_params=pltpu.CompilerParams(vmem_limit_bytes=63 * MIB),
        cost_estimate=pl.CostEstimate(flops=12 * 1024**3, bytes_accessed=20 * MIB, transcendentals=MIB),
        name="sublayer",
    )(place, tokens, gain, bias, wqkv, wout)


def message_kernel(place_ref, keep_ref, got_ref, back_ref, theirs_ref, own_ref, message_ref):
    message_ref[:, :32, 1536:] = back_ref[...]
    message_ref[:, 32:, 1536:] = theirs_ref[...]
    for i in range(4):
        g = keep_ref[i] + got_ref[i].astype(F32)
        message_ref[i, :, :1536] = g.astype(BF16)

        @pl.when(pl.program_id(0) * 4 + i == place_ref[2])
        def _():
            own_ref[...] = g


def step_call(kernel, name, in_blocks, outs):
    def spec(shape):
        if len(shape) == 2:
            return pl.BlockSpec(shape, lambda k, place: (0, 0))
        return pl.BlockSpec((4,) + shape[1:], lambda k, place: (k, 0, 0))

    return pl.pallas_call(
        kernel,
        grid_spec=pltpu.PrefetchScalarGridSpec(
            num_scalar_prefetch=1,
            grid=(2,),
            in_specs=[spec(shape) for shape in in_blocks],
            out_specs=tuple(spec(shape) for shape, _ in outs),
        ),
        out_shape=tuple(jax.ShapeDtypeStruct(shape, dtype) for shape, dtype in outs),
        compiler_params=pltpu.CompilerParams(vmem_limit_bytes=63 * MIB),
        cost_estimate=pl.CostEstimate(flops=MIB, bytes_accessed=9 * MIB, transcendentals=0),
        name=name,
    )


def run_message(place, keep, got, back, theirs):
    ins = [keep.shape, got.shape, back.shape, theirs.shape]
    outs = [((64, 1536), F32), ((8, 64, 1536 + back.shape[2]), BF16)]
    return step_call(message_kernel, "message", ins, outs)(place, keep, got, back, theirs)


def sum_kernel(place_ref, keep_ref, t1, t2, t3, own_ref, total_ref):
    for i in range(4):
        g = keep_ref[i] + t1[i].astype(F32) + t2[i].astype(F32) + t3[i].astype(F32)
        total_ref[i] = g.astype(BF16)

        @pl.when(pl.program_id(0) * 4 + i == place_ref[2])
        def _():
            own_ref[...] = g


def run_sum(place, keep, got):
    ins = [keep.shape] * 4
    outs = [(keep.shape[1:], F32), (keep.shape, BF16)]
    return step_call(sum_kernel, "sum_b", ins, outs)(place, keep, *got)


def unpack_kernel(place_ref, message_ref, out_ref):
    clips, rows, width = out_ref.shape
    for i in range(rows // 32):
        for which in range(2):
            at = pl.multiple_of(i * 32 + (which + place_ref[1]) % 2 * 16, 16)
            for c in range(clips):
                row = which * 32 + c * 16
                out_ref[c, pl.ds(at, 16), :] = message_ref[i, row:row + 16, 1536:1536 + width]


def run_unpack(place, message, clips, width):
    return pl.pallas_call(
        unpack_kernel,
        grid_spec=pltpu.PrefetchScalarGridSpec(
            num_scalar_prefetch=1,
            grid=(2,),
            in_specs=[pl.BlockSpec((4,) + message.shape[1:], lambda k, place: (k, 0, 0))],
            out_specs=pl.BlockSpec((clips, 128, width), lambda k, place: (0, k, 0)),
        ),
        out_shape=jax.ShapeDtypeStruct((clips, 256, width), BF16),
        compiler_params=pltpu.CompilerParams(vmem_limit_bytes=63 * MIB),
        name="unpack",
    )(place, message)


def pack_kernel(video_ref, cot_ref, out_ref, packed_s, sems):
    clips = video_ref.shape[0]
    loads = []
    for c in range(clips):
        loads.append(pltpu.make_async_copy(video_ref.at[c], packed_s.at[:, c], sems.at[2 * c]))
        loads.append(pltpu.make_async_copy(cot_ref.at[c], packed_s.at[:, clips + c], sems.at[2 * c + 1]))
    for load in loads:
        load.start()
    for load in loads:
        load.wait()
    store = pltpu.make_async_copy(packed_s, out_ref, sems.at[2 * clips])
    store.start()
    store.wait()


def run_pack(video, cotangent):
    clips, _, positions, width = video.shape
    shape = (clips, 16, positions // 16, width)
    packed = (16, 2 * clips, positions // 16, width)
    hbm = pl.BlockSpec(memory_space=pl.ANY)
    return pl.pallas_call(
        pack_kernel,
        in_specs=[hbm, hbm],
        out_specs=hbm,
        out_shape=jax.ShapeDtypeStruct(packed, BF16),
        scratch_shapes=[pltpu.VMEM(packed, BF16), pltpu.SemaphoreType.DMA((2 * clips + 1,))],
        compiler_params=pltpu.CompilerParams(vmem_limit_bytes=63 * MIB),
        name="pack",
    )(video.reshape(shape), cotangent.reshape(shape))


def terms_kernel(keep_ref, got_ref, own_ref, *term_refs):
    own_ref[...] = keep_ref[0] + got_ref[0].astype(F32)
    for i, term_ref in enumerate(term_refs):
        term_ref[...] = (keep_ref[i + 1] + got_ref[i + 1].astype(F32)).astype(BF16)


def run_terms(keep, got):
    shape = keep.shape[1:]
    ins = pl.BlockSpec((4, 4) + shape[1:], lambda k: (0, k, 0, 0))
    out = pl.BlockSpec((4,) + shape[1:], lambda k: (k, 0, 0))
    return pl.pallas_call(
        terms_kernel,
        grid=(2,),
        in_specs=[ins, ins],
        out_specs=(out,) * 4,
        out_shape=tuple(jax.ShapeDtypeStruct(shape, dtype) for dtype in (F32, BF16, BF16, BF16)),
        compiler_params=pltpu.CompilerParams(vmem_limit_bytes=63 * MIB),
        cost_estimate=pl.CostEstimate(flops=MIB, bytes_accessed=11 * MIB, transcendentals=0),
        name="terms_b",
    )(keep, got)


def place_kernel(scale, place_ref, d0, d1, d2, d3, qkv_ref, out_ref, gain_ref, bias_ref):
    small = jnp.zeros((8, 128), F32)
    for j, d in enumerate((d0, d1, d2, d3)):
        block = (place_ref[0] - j) % 4
        qkv_ref[:, pl.ds(pl.multiple_of(block * 640, 128), 640)] = d[:, :640] * scale
        qkv_ref[:, pl.ds(pl.multiple_of(2560 + block * 128, 128), 128)] = d[:, 640:768] * scale
        out_ref[:, pl.ds(pl.multiple_of(block * 256, 256), 256)] = d[:, 768:1024] * scale
        small = small + d[:8, 1024:]
    small = jnp.sum(small, axis=0, keepdims=True) * scale
    gain_ref[...] = small[:, :64]
    bias_ref[...] = small[:, 64:]


def run_place(place, scale, pieces):
    vm = pl.BlockSpec(memory_space=pltpu.VMEM)
    return pl.pallas_call(
        functools.partial(place_kernel, scale),
        out_shape=(
            jax.ShapeDtypeStruct((64, 3072), F32),
            jax.ShapeDtypeStruct((64, 1024), F32),
            jax.ShapeDtypeStruct((1, 64), F32),
            jax.ShapeDtypeStruct((1, 64), F32),
        ),
        in_specs=[pl.BlockSpec(memory_space=pltpu.SMEM)] + [vm] * 4,
        out_specs=(vm,) * 4,
        name="place_grads",
    )(place, *pieces)


def frame_pairs(move):
    pairs = []
    for i in range(16):
        y, z, core = move(i // 4, i // 2 % 2, i % 2)
        pairs.append((i, y % 4 * 4 + z % 2 * 2 + core % 2))
    return pairs


def dp_pairs(move):
    pairs = []
    for i in range(16):
        x, h = move(i // 4, i % 4)
        pairs.append((i, x % 4 * 4 + h % 4))
    return pairs


def go_core(a):
    return lax.ppermute(a, "frame", frame_pairs(lambda y, z, c: (y, z, c + 1)))


def trade_yz(a):
    groups = [[2 * i + core for i in range(8)] for core in range(2)]
    return lax.all_to_all(a, "frame", 0, 0, tiled=True, axis_index_groups=groups)


def go_x(a, k):
    return lax.ppermute(a, "dp", dp_pairs(lambda x, h: (x + k, h)))


def go_h(a, k):
    return lax.ppermute(a, "dp", dp_pairs(lambda x, h: (x, h + k)))


def combine(own, got):
    for part in got:
        own = own + part.astype(F32)
    return own


def exchange(pieces, go):
    return [go(pieces[k], k) for k in range(1, 4)]


def pick(array, index):
    return lax.dynamic_index_in_dim(array, index, 0, keepdims=False)


def reduce_yz(own, got, yz):
    mine = (jnp.arange(8) == yz).reshape((8,) + (1,) * own.ndim)
    return jnp.sum(jnp.where(mine, own[None], got.astype(F32)), axis=0)


def three_terms(value):
    hi = lax.reduce_precision(value, 8, 7)
    mid = lax.reduce_precision(value - hi, 8, 7)
    return jnp.pad(jnp.concatenate([hi, mid, value - hi - mid], axis=0), ((0, 61), (0, 0)))


def local(video, cotangent, norm_gain, norm_bias, qkv_weight, out_weight):
    clips, frames_here, positions, width = video.shape
    grad_scale = 1.0 / math.sqrt(clips * positions * 256)
    frame = lax.axis_index("frame")
    dp = lax.axis_index("dp")
    yz, core = frame // 2, frame % 2
    place = jnp.stack([dp // 4, core, yz]).astype(jnp.int32)
    gain = norm_gain.reshape(1, width)
    bias = norm_bias.reshape(1, width)
    tokens = lax.all_to_all(run_pack(video, cotangent), "frame", 0, 0, tiled=True)
    back, theirs, send_a, send_b, keep_a, keep_b = run_main(
        place, tokens, gain, bias, qkv_weight, out_weight
    )

    got_a = go_core(send_a)
    got_a, theirs, send_b = lax.optimization_barrier((got_a, go_core(theirs), send_b))
    got_b = go_core(send_b)
    own_a, message = run_message(place, keep_a, got_a, back, theirs)
    terms_b = run_terms(keep_b, got_b)
    message, terms_b = lax.optimization_barrier((message, terms_b))
    message = trade_yz(message)
    got_b = exchange(terms_b, go_x)
    message, got_b = lax.optimization_barrier((message, got_b))

    own_b, total_b = run_sum(place, terms_b[0], got_b)
    got_b = trade_yz(total_b)
    a = reduce_yz(own_a, message[:, :, :1536], yz)
    terms_a = [a[:, k * 384 : (k + 1) * 384] for k in range(4)]
    got_a = exchange([t.astype(BF16) for t in terms_a], go_x)
    message, got_a, got_b = lax.optimization_barrier((message, got_a, got_b))

    a = combine(terms_a[0], got_a)
    b = reduce_yz(own_b, got_b, yz)
    small = jnp.sum(message[:, :, 1536 + width :].astype(F32), axis=(0, 1)).reshape(1, 128)
    own = jnp.concatenate([b, a, three_terms(small)], axis=1)
    own = combine(own, exchange([own.astype(BF16)] * 4, go_h))
    pieces = [own] + exchange([own] * 4, go_x)

    grad_video = run_unpack(place, message, clips, width).reshape(video.shape)
    pieces, grad_video = lax.optimization_barrier((pieces, grad_video))
    grad_qkv, grad_out, total_gain, total_bias = run_place(place, grad_scale, pieces)
    return grad_video, grad_qkv, grad_out, total_gain.reshape(64), total_bias.reshape(64)


def solution(mesh):
    in_specs = (P("dp", "frame", None, None), P("dp", "frame", None, None), P(), P(), P(), P())
    out_specs = (
        P("dp", "frame", None, None),
        P("frame", None),
        P("frame", None),
        P("frame"),
        P("frame"),
    )
    return jax.shard_map(local, mesh=mesh, in_specs=in_specs, out_specs=out_specs, check_vma=False)
```

```python
import functools
import math

import jax
import jax.numpy as jnp
from jax import lax
from jax.experimental import pallas as pl
from jax.experimental.pallas import tpu as pltpu
from jax.sharding import PartitionSpec as P

F32 = jnp.float32
BF16 = jnp.bfloat16
MIB = 1024 * 1024
CHUNK = 512


def dot_nn(a, b):
    return lax.dot_general(a, b, (((1,), (0,)), ((), ())), preferred_element_type=F32)


def dot_nt(a, b):
    return lax.dot_general(a, b, (((1,), (1,)), ((), ())), preferred_element_type=F32)


def dot_tn(a, b):
    return lax.dot_general(a, b, (((0,), (0,)), ((), ())), preferred_element_type=F32)


def chunk(n):
    return pl.ds(pl.multiple_of(n * CHUNK, CHUNK), CHUNK)


def block_row(block, place):
    return pl.multiple_of(((block % 2 - place[1]) % 2 * 8 + block // 2) * 64, 64)


def read_place(place_ref):
    return tuple(place_ref[i] for i in range(2))


def whiten(xh):
    centred = xh - jnp.mean(xh, axis=-1, keepdims=True)
    inv = lax.rsqrt(jnp.mean(centred * centred, axis=-1, keepdims=True) + 1e-05)
    return centred * inv, inv


def main_kernel(
    place_ref, tokens_hbm, gain_ref, bias_ref, wqkv_hbm, wout_hbm,
    back_hbm, theirs_hbm, send_a_hbm, send_b_hbm, keep_a_hbm, keep_b_hbm,
    tokens_s, wqkv_s, wout_s, left_s, right_s, normed_s, packed_s, datt_s, wh_s, inv_s, dn_s,
    send_a_s, send_b_s, keep_a_s, keep_b_s, back_ref,
    token_sems, weight_sems, out_sems,
):
    place = read_place(place_ref)
    frames, clips, positions, width = tokens_s.shape
    clips = clips // 2
    halves = positions // 8
    part = frames * 8
    gain = gain_ref[...]
    bias = bias_ref[...]

    def load_tokens(q):
        pair = pl.ds(2 * q, 2)
        return pltpu.make_async_copy(tokens_hbm.at[pair], tokens_s.at[pair], token_sems.at[q])

    def load_wqkv(n):
        return pltpu.make_async_copy(wqkv_hbm.at[:, chunk(n)], wqkv_s.at[:, chunk(n)], weight_sems.at[n])

    blocks = 3 * width // CHUNK
    load_wout = pltpu.make_async_copy(wout_hbm, wout_s, weight_sems.at[blocks])
    for q in range(frames // 2):
        load_tokens(q).start()
    for n in range(blocks):
        load_wqkv(n).start()
    load_wout.start()

    def norm_step(q, carry):
        load_tokens(q).wait()
        for c in range(clips):
            x = tokens_s[pl.ds(2 * q, 2), c].astype(F32).reshape(2, halves, 8, width)
            g = tokens_s[pl.ds(2 * q, 2), clips + c].astype(F32).reshape(2, halves, 8, width)
            for hf in range(halves):
                at = pl.multiple_of((c * halves + hf) * part + q * 16, 16)
                wh, inv = whiten(x[:, hf].reshape(16, width))
                wh_s[pl.ds(at, 16), :] = wh
                inv_s[pl.ds(at, 16), :] = jnp.broadcast_to(inv, (16, 128))
                normed_s[pl.ds(at, 16), :] = (wh * gain + bias).astype(BF16)
                right_s[pl.ds(at, 16), pl.ds(3 * width, width)] = g[:, hf].reshape(16, width).astype(BF16)
        return carry

    lax.fori_loop(0, frames // 2, norm_step, 0, unroll=2)

    def qkv_step(n, carry):
        for i in range(2):
            load_wqkv(2 * n + i).wait()
        for i in range(2):
            cols = chunk(2 * n + i)
            packed_s[:, cols] = dot_nn(normed_s[...], wqkv_s[:, cols]).astype(BF16)
        return carry

    lax.fori_loop(0, blocks // 2, qkv_step, 0)
    load_wout.wait()

    for n in range(width // CHUNK):
        cols = slice(n * CHUNK, (n + 1) * CHUNK)
        datt_s[:, cols] = dot_nt(right_s[:, 3 * width:], wout_s[cols, :]).astype(BF16)
        turned = normed_s[:, cols].T
        for b in range(CHUNK // 64):
            at = block_row(n * (CHUNK // 64) + b, place)
            left_s[0, pl.ds(at, 64), :] = turned[b * 64:(b + 1) * 64]

    lane = lax.broadcasted_iota(jnp.int32, (part, 128), 1)
    first = lane < 64
    same = lax.broadcasted_iota(jnp.int32, (1, 8, part), 1) == (
        lax.broadcasted_iota(jnp.int32, (1, 8, part), 2) % 8
    )
    zero = jnp.zeros((part, 128), BF16)
    scale = jnp.asarray(0.125, BF16)

    def split(a):
        return jnp.concatenate([jnp.where(first, a, zero), jnp.where(first, zero, a)], axis=0)

    def attend_step(i, carry):
        t = i // (width // 128)
        hp = i % (width // 128)
        tok = pl.ds(pl.multiple_of(t * part, part), part)
        col = pl.multiple_of(hp * 128, 128)
        q = packed_s[tok, pl.ds(col, 128)]
        k = packed_s[tok, pl.ds(width + col, 128)]
        v = packed_s[tok, pl.ds(2 * width + col, 128)]
        da = datt_s[tok, pl.ds(col, 128)]
        k2 = split(k)
        v2 = split(v)
        scores = dot_nt(k2, q * scale).reshape(2, frames, 8, part)
        e = jnp.exp(scores - jnp.max(scores, axis=1, keepdims=True))
        probs = e * (1.0 / jnp.sum(e, axis=1, keepdims=True))
        probs = jnp.where(same[None], probs, 0.0)
        low = probs.astype(BF16).reshape(2, part, part)
        dp = dot_nt(v2, da * scale).reshape(2, frames, 8, part)
        inner = jnp.sum(dp * probs, axis=1, keepdims=True)
        ds = (probs * (dp - inner)).astype(BF16).reshape(2, part, part)
        attended = dot_tn(v2, low.reshape(2 * part, part)).astype(BF16)
        for b in range(2):
            left_s[1, pl.ds(block_row(hp * 2 + b, place), 64), tok] = attended[b * 64:(b + 1) * 64]
        right_s[tok, pl.ds(col, 128)] = dot_tn(ds.reshape(2 * part, part), k2).astype(BF16)
        right_s[tok, pl.ds(width + col, 128)] = dot_nn(
            jnp.concatenate([ds[0], ds[1]], axis=1), split(q)
        ).astype(BF16)
        right_s[tok, pl.ds(2 * width + col, 128)] = dot_nn(
            jnp.concatenate([low[0], low[1]], axis=1), split(da)
        ).astype(BF16)
        return carry

    lax.fori_loop(0, clips * halves * (width // 128), attend_step, 0, unroll=8)

    half = width // 2
    copies = []

    def write(src, dst):
        copies.append(pltpu.make_async_copy(src, dst, out_sems.at[len(copies)]))
        copies[-1].start()

    for k in range(4):
        block = (place[0] + k) % 4
        lanes = slice(k * 384, k * 384 + 128)
        rhs = right_s[:, pl.ds(pl.multiple_of(2560 + block * 128, 128), 128)]
        send_a_s[:, :, lanes] = dot_nn(left_s[0, half:, :], rhs).reshape(8, 64, 128).astype(BF16)
        keep_a_s[:, :, lanes] = dot_nn(left_s[0, :half, :], rhs).reshape(8, 64, 128)
        lanes = slice(k * 384 + 128, k * 384 + 384)
        rhs = right_s[:, pl.ds(pl.multiple_of(3072 + block * 256, 256), 256)]
        send_a_s[:, :, lanes] = dot_nn(left_s[1, half:, :], rhs).reshape(8, 64, 256).astype(BF16)
        keep_a_s[:, :, lanes] = dot_nn(left_s[1, :half, :], rhs).reshape(8, 64, 256)
    write(send_a_s, send_a_hbm)
    for k in range(4):
        block = (place[0] + k) % 4
        rhs = right_s[:, pl.ds(pl.multiple_of(block * 640, 128), 640)]
        send_b_s[k] = dot_nn(left_s[0, half:, :], rhs).reshape(8, 64, 640).astype(BF16)
        write(send_b_s.at[k], send_b_hbm.at[k])
        keep_b_s[k] = dot_nn(left_s[0, :half, :], rhs).reshape(8, 64, 640)
        write(keep_b_s.at[k], keep_b_hbm.at[k])
    write(keep_a_s, keep_a_hbm)

    for n in range(width // CHUNK):
        cols = slice(n * CHUNK, (n + 1) * CHUNK)
        dn_s[:, cols] = dot_nt(right_s[:, :3 * width], wqkv_s[cols, :])

    def back_step(i, carry):
        dgain, dbias = carry
        c = i // (frames // 2)
        q = i % (frames // 2)
        outs = []
        for hf in range(halves):
            at = pl.multiple_of((c * halves + hf) * part + q * 16, 16)
            dn = dn_s[pl.ds(at, 16), :]
            wh = wh_s[pl.ds(at, 16), :]
            inv = inv_s[pl.ds(at, 16), :][:, :1]
            dw = dn * wh
            dgain = dgain + dw[:8] + dw[8:]
            dbias = dbias + dn[:8] + dn[8:]
            scaled = dn * gain
            m1 = jnp.mean(scaled, axis=-1, keepdims=True)
            m2 = jnp.mean(scaled * wh, axis=-1, keepdims=True)
            g = right_s[pl.ds(at, 16), pl.ds(3 * width, width)].astype(F32)
            outs.append((g + inv * (scaled - m1 - wh * m2)).reshape(2, 8, width))
        grads = jnp.concatenate(outs, axis=1).astype(BF16)
        at = pl.ds(pl.multiple_of(c * positions, positions), positions)
        for f in range(2):
            back_ref[(f - place[1]) % 2, q, at, :width] = grads[f]
        return dgain, dbias

    zeros = jnp.zeros((8, width), F32)
    dgain, dbias = lax.fori_loop(0, clips * frames // 2, back_step, (zeros, zeros), unroll=2)
    dgain = jnp.sum(dgain, axis=0, keepdims=True)
    dbias = jnp.sum(dbias, axis=0, keepdims=True)
    lane = lax.broadcasted_iota(jnp.int32, (1, 128), 1)
    row = lax.broadcasted_iota(jnp.int32, (16, 128), 0)
    back_ref[:, :, 16:, width:] = jnp.zeros((2, 8, clips * positions - 16, 128), BF16)
    for f in range(frames):
        at = f // 2 * 128
        a = dgain[:, at:at + 128]
        b = dbias[:, at:at + 128]
        if f % 2 == 0:
            b = jnp.concatenate([b[:, 64:], b[:, :64]], axis=1)
        else:
            a = jnp.concatenate([a[:, 64:], a[:, :64]], axis=1)
        both = jnp.where(lane < 64, a, b)
        hi = both.astype(BF16).astype(F32)
        mid = (both - hi).astype(BF16).astype(F32)
        low = both - hi - mid
        terms = jnp.where(row == 0, hi, jnp.where(row == 1, mid, jnp.where(row == 2, low, 0.0)))
        back_ref[(f % 2 - place[1]) % 2, f // 2, :16, width:] = terms.astype(BF16)
    write(back_ref.at[1], theirs_hbm)
    write(back_ref.at[0], back_hbm)
    for copy in copies:
        copy.wait()


def run_main(place, tokens, gain, bias, wqkv, wout):
    frames, clips, positions, width = tokens.shape
    clips = clips // 2
    rows = clips * frames * positions
    vm = pl.BlockSpec(memory_space=pltpu.VMEM)
    hbm = pl.BlockSpec(memory_space=pl.ANY)
    a, b = (8, 64, 1536), (4, 8, 64, 640)
    back = (frames // 2, clips * positions, width + 128)
    return pl.pallas_call(
        main_kernel,
        out_shape=(
            jax.ShapeDtypeStruct(back, BF16),
            jax.ShapeDtypeStruct(back, BF16),
            jax.ShapeDtypeStruct(a, BF16),
            jax.ShapeDtypeStruct(b, BF16),
            jax.ShapeDtypeStruct(a, F32),
            jax.ShapeDtypeStruct(b, F32),
        ),
        in_specs=[pl.BlockSpec(memory_space=pltpu.SMEM), hbm, vm, vm, hbm, hbm],
        out_specs=(hbm,) * 6,
        scratch_shapes=[
            pltpu.VMEM(tokens.shape, BF16),
            pltpu.VMEM(wqkv.shape, BF16),
            pltpu.VMEM(wout.shape, BF16),
            pltpu.VMEM((2, width, rows), BF16),
            pltpu.VMEM((rows, 4 * width), BF16),
            pltpu.VMEM((rows, width), BF16),
            pltpu.VMEM((rows, 3 * width), BF16),
            pltpu.VMEM((rows, width), BF16),
            pltpu.VMEM((rows, width), F32),
            pltpu.VMEM((rows, 128), F32),
            pltpu.VMEM((rows, width), F32),
            pltpu.VMEM(a, BF16),
            pltpu.VMEM(b, BF16),
            pltpu.VMEM(a, F32),
            pltpu.VMEM(b, F32),
            pltpu.VMEM((2,) + back, BF16),
            pltpu.SemaphoreType.DMA((frames // 2,)),
            pltpu.SemaphoreType.DMA((3 * width // CHUNK + 1,)),
            pltpu.SemaphoreType.DMA((12,)),
        ],
        compiler_params=pltpu.CompilerParams(vmem_limit_bytes=63 * MIB),
        cost_estimate=pl.CostEstimate(flops=12 * 1024**3, bytes_accessed=20 * MIB, transcendentals=MIB),
        name="sublayer",
    )(place, tokens, gain, bias, wqkv, wout)


def message_kernel(place_ref, keep_ref, got_ref, back_ref, theirs_ref, own_ref, message_ref):
    message_ref[:, :32, 1536:] = back_ref[...]
    message_ref[:, 32:, 1536:] = theirs_ref[...]
    for i in range(4):
        g = keep_ref[i] + got_ref[i].astype(F32)
        message_ref[i, :, :1536] = g.astype(BF16)

        @pl.when(pl.program_id(0) * 4 + i == place_ref[2])
        def _():
            own_ref[...] = g


def step_call(kernel, name, in_blocks, outs):
    def spec(shape):
        if len(shape) == 2:
            return pl.BlockSpec(shape, lambda k, place: (0, 0))
        return pl.BlockSpec((4,) + shape[1:], lambda k, place: (k, 0, 0))

    return pl.pallas_call(
        kernel,
        grid_spec=pltpu.PrefetchScalarGridSpec(
            num_scalar_prefetch=1,
            grid=(2,),
            in_specs=[spec(shape) for shape in in_blocks],
            out_specs=tuple(spec(shape) for shape, _ in outs),
        ),
        out_shape=tuple(jax.ShapeDtypeStruct(shape, dtype) for shape, dtype in outs),
        compiler_params=pltpu.CompilerParams(vmem_limit_bytes=63 * MIB),
        cost_estimate=pl.CostEstimate(flops=MIB, bytes_accessed=9 * MIB, transcendentals=0),
        name=name,
    )


def run_message(place, keep, got, back, theirs):
    ins = [keep.shape, got.shape, back.shape, theirs.shape]
    outs = [((64, 1536), F32), ((8, 64, 1536 + back.shape[2]), BF16)]
    return step_call(message_kernel, "message", ins, outs)(place, keep, got, back, theirs)


def sum_kernel(place_ref, keep_ref, t1, t2, t3, own_ref, total_ref):
    for i in range(4):
        g = keep_ref[i] + t1[i].astype(F32) + t2[i].astype(F32) + t3[i].astype(F32)
        total_ref[i] = g.astype(BF16)

        @pl.when(pl.program_id(0) * 4 + i == place_ref[2])
        def _():
            own_ref[...] = g


def run_sum(place, keep, got):
    ins = [keep.shape] * 4
    outs = [(keep.shape[1:], F32), (keep.shape, BF16)]
    return step_call(sum_kernel, "sum_b", ins, outs)(place, keep, *got)


def unpack_kernel(place_ref, message_ref, out_ref):
    clips, rows, width = out_ref.shape
    for i in range(rows // 32):
        for which in range(2):
            at = pl.multiple_of(i * 32 + (which + place_ref[1]) % 2 * 16, 16)
            for c in range(clips):
                row = which * 32 + c * 16
                out_ref[c, pl.ds(at, 16), :] = message_ref[i, row:row + 16, 1536:1536 + width]


def run_unpack(place, message, clips, width):
    return pl.pallas_call(
        unpack_kernel,
        grid_spec=pltpu.PrefetchScalarGridSpec(
            num_scalar_prefetch=1,
            grid=(2,),
            in_specs=[pl.BlockSpec((4,) + message.shape[1:], lambda k, place: (k, 0, 0))],
            out_specs=pl.BlockSpec((clips, 128, width), lambda k, place: (0, k, 0)),
        ),
        out_shape=jax.ShapeDtypeStruct((clips, 256, width), BF16),
        compiler_params=pltpu.CompilerParams(vmem_limit_bytes=63 * MIB),
        name="unpack",
    )(place, message)


def pack_kernel(video_ref, cot_ref, out_ref, packed_s, sems):
    clips = video_ref.shape[0]
    loads = []
    for c in range(clips):
        loads.append(pltpu.make_async_copy(video_ref.at[c], packed_s.at[:, c], sems.at[2 * c]))
        loads.append(pltpu.make_async_copy(cot_ref.at[c], packed_s.at[:, clips + c], sems.at[2 * c + 1]))
    for load in loads:
        load.start()
    for load in loads:
        load.wait()
    store = pltpu.make_async_copy(packed_s, out_ref, sems.at[2 * clips])
    store.start()
    store.wait()


def run_pack(video, cotangent):
    clips, _, positions, width = video.shape
    shape = (clips, 16, positions // 16, width)
    packed = (16, 2 * clips, positions // 16, width)
    hbm = pl.BlockSpec(memory_space=pl.ANY)
    return pl.pallas_call(
        pack_kernel,
        in_specs=[hbm, hbm],
        out_specs=hbm,
        out_shape=jax.ShapeDtypeStruct(packed, BF16),
        scratch_shapes=[pltpu.VMEM(packed, BF16), pltpu.SemaphoreType.DMA((2 * clips + 1,))],
        compiler_params=pltpu.CompilerParams(vmem_limit_bytes=63 * MIB),
        name="pack",
    )(video.reshape(shape), cotangent.reshape(shape))


def terms_kernel(keep_ref, got_ref, own_ref, *term_refs):
    own_ref[...] = keep_ref[0] + got_ref[0].astype(F32)
    for i, term_ref in enumerate(term_refs):
        term_ref[...] = (keep_ref[i + 1] + got_ref[i + 1].astype(F32)).astype(BF16)


def run_terms(keep, got):
    shape = keep.shape[1:]
    ins = pl.BlockSpec((4, 4) + shape[1:], lambda k: (0, k, 0, 0))
    out = pl.BlockSpec((4,) + shape[1:], lambda k: (k, 0, 0))
    return pl.pallas_call(
        terms_kernel,
        grid=(2,),
        in_specs=[ins, ins],
        out_specs=(out,) * 4,
        out_shape=tuple(jax.ShapeDtypeStruct(shape, dtype) for dtype in (F32, BF16, BF16, BF16)),
        compiler_params=pltpu.CompilerParams(vmem_limit_bytes=63 * MIB),
        cost_estimate=pl.CostEstimate(flops=MIB, bytes_accessed=11 * MIB, transcendentals=0),
        name="terms_b",
    )(keep, got)


def place_kernel(scale, place_ref, d0, d1, d2, d3, qkv_ref, out_ref, gain_ref, bias_ref):
    small = jnp.zeros((8, 128), F32)
    for j, d in enumerate((d0, d1, d2, d3)):
        block = (place_ref[0] - j) % 4
        qkv_ref[:, pl.ds(pl.multiple_of(block * 640, 128), 640)] = d[:, :640] * scale
        qkv_ref[:, pl.ds(pl.multiple_of(2560 + block * 128, 128), 128)] = d[:, 640:768] * scale
        out_ref[:, pl.ds(pl.multiple_of(block * 256, 256), 256)] = d[:, 768:1024] * scale
        small = small + d[:8, 1024:]
    small = jnp.sum(small, axis=0, keepdims=True) * scale
    gain_ref[...] = small[:, :64]
    bias_ref[...] = small[:, 64:]


def run_place(place, scale, pieces):
    vm = pl.BlockSpec(memory_space=pltpu.VMEM)
    return pl.pallas_call(
        functools.partial(place_kernel, scale),
        out_shape=(
            jax.ShapeDtypeStruct((64, 3072), F32),
            jax.ShapeDtypeStruct((64, 1024), F32),
            jax.ShapeDtypeStruct((1, 64), F32),
            jax.ShapeDtypeStruct((1, 64), F32),
        ),
        in_specs=[pl.BlockSpec(memory_space=pltpu.SMEM)] + [vm] * 4,
        out_specs=(vm,) * 4,
        name="place_grads",
    )(place, *pieces)


def frame_pairs(move):
    pairs = []
    for i in range(16):
        y, z, core = move(i // 4, i // 2 % 2, i % 2)
        pairs.append((i, y % 4 * 4 + z % 2 * 2 + core % 2))
    return pairs


def dp_pairs(move):
    pairs = []
    for i in range(16):
        x, h = move(i // 4, i % 4)
        pairs.append((i, x % 4 * 4 + h % 4))
    return pairs


def go_core(a):
    return lax.ppermute(a, "frame", frame_pairs(lambda y, z, c: (y, z, c + 1)))


def trade_yz(a):
    groups = [[2 * i + core for i in range(8)] for core in range(2)]
    return lax.all_to_all(a, "frame", 0, 0, tiled=True, axis_index_groups=groups)


def go_x(a, k):
    return lax.ppermute(a, "dp", dp_pairs(lambda x, h: (x + k, h)))


def go_h(a, k):
    return lax.ppermute(a, "dp", dp_pairs(lambda x, h: (x, h + k)))


def combine(own, got):
    for part in got:
        own = own + part.astype(F32)
    return own


def exchange(pieces, go):
    return [go(pieces[k], k) for k in range(1, 4)]


def pick(array, index):
    return lax.dynamic_index_in_dim(array, index, 0, keepdims=False)


def reduce_yz(own, got, yz):
    mine = (jnp.arange(8) == yz).reshape((8,) + (1,) * own.ndim)
    return jnp.sum(jnp.where(mine, own[None], got.astype(F32)), axis=0)


def three_terms(value):
    hi = lax.reduce_precision(value, 8, 7)
    mid = lax.reduce_precision(value - hi, 8, 7)
    return jnp.pad(jnp.concatenate([hi, mid, value - hi - mid], axis=0), ((0, 61), (0, 0)))


def local(video, cotangent, norm_gain, norm_bias, qkv_weight, out_weight):
    clips, frames_here, positions, width = video.shape
    grad_scale = 1.0 / math.sqrt(clips * positions * 256)
    frame = lax.axis_index("frame")
    dp = lax.axis_index("dp")
    yz, core = frame // 2, frame % 2
    place = jnp.stack([dp // 4, core, yz]).astype(jnp.int32)
    gain = norm_gain.reshape(1, width)
    bias = norm_bias.reshape(1, width)
    tokens = lax.all_to_all(run_pack(video, cotangent), "frame", 0, 0, tiled=True)
    back, theirs, send_a, send_b, keep_a, keep_b = run_main(
        place, tokens, gain, bias, qkv_weight, out_weight
    )

    got_a = go_core(send_a)
    got_a, theirs, send_b = lax.optimization_barrier((got_a, go_core(theirs), send_b))
    got_b = go_core(send_b)
    own_a, message = run_message(place, keep_a, got_a, back, theirs)
    terms_b = run_terms(keep_b, got_b)
    message, terms_b = lax.optimization_barrier((message, terms_b))
    message = trade_yz(message)
    got_b = exchange(terms_b, go_x)
    message, got_b = lax.optimization_barrier((message, got_b))

    own_b, total_b = run_sum(place, terms_b[0], got_b)
    got_b = trade_yz(total_b)
    a = reduce_yz(own_a, message[:, :, :1536], yz)
    terms_a = [a[:, k * 384 : (k + 1) * 384] for k in range(4)]
    got_a = exchange([t.astype(BF16) for t in terms_a], go_x)
    small = jnp.sum(message[:, :, 1536 + width :].astype(F32), axis=(0, 1)).reshape(1, 128)
    terms = three_terms(small)
    message, terms, got_a, got_b = lax.optimization_barrier((message, terms, got_a, got_b))

    a = combine(terms_a[0], got_a)
    b = reduce_yz(own_b, got_b, yz)
    own = jnp.concatenate([b, a, terms], axis=1)
    own = combine(own, exchange([own.astype(BF16)] * 4, go_h))
    pieces = [own] + exchange([own] * 4, go_x)

    grad_video = run_unpack(place, message, clips, width).reshape(video.shape)
    pieces, grad_video = lax.optimization_barrier((pieces, grad_video))
    grad_qkv, grad_out, total_gain, total_bias = run_place(place, grad_scale, pieces)
    return grad_video, grad_qkv, grad_out, total_gain.reshape(64), total_bias.reshape(64)


def solution(mesh):
    in_specs = (P("dp", "frame", None, None), P("dp", "frame", None, None), P(), P(), P(), P())
    out_specs = (
        P("dp", "frame", None, None),
        P("frame", None),
        P("frame", None),
        P("frame"),
        P("frame"),
    )
    return jax.shard_map(local, mesh=mesh, in_specs=in_specs, out_specs=out_specs, check_vma=False)
```

```python
import functools
import math

import jax
import jax.numpy as jnp
from jax import lax
from jax.experimental import pallas as pl
from jax.experimental.pallas import tpu as pltpu
from jax.sharding import PartitionSpec as P

F32 = jnp.float32
BF16 = jnp.bfloat16
MIB = 1024 * 1024
CHUNK = 512


def dot_nn(a, b):
    return lax.dot_general(a, b, (((1,), (0,)), ((), ())), preferred_element_type=F32)


def dot_nt(a, b):
    return lax.dot_general(a, b, (((1,), (1,)), ((), ())), preferred_element_type=F32)


def dot_tn(a, b):
    return lax.dot_general(a, b, (((0,), (0,)), ((), ())), preferred_element_type=F32)


def chunk(n):
    return pl.ds(pl.multiple_of(n * CHUNK, CHUNK), CHUNK)


def block_row(block, place):
    return pl.multiple_of(((block % 2 - place[1]) % 2 * 8 + block // 2) * 64, 64)


def read_place(place_ref):
    return tuple(place_ref[i] for i in range(2))


def whiten(xh):
    centred = xh - jnp.mean(xh, axis=-1, keepdims=True)
    inv = lax.rsqrt(jnp.mean(centred * centred, axis=-1, keepdims=True) + 1e-05)
    return centred * inv, inv


def main_kernel(
    place_ref, tokens_hbm, gain_ref, bias_ref, wqkv_hbm, wout_hbm,
    back_hbm, theirs_hbm, send_a_hbm, send_b_hbm, keep_a_hbm, keep_b_hbm,
    tokens_s, wqkv_s, wout_s, left_s, right_s, normed_s, packed_s, datt_s, wh_s, inv_s, dn_s,
    send_a_s, send_b_s, keep_a_s, keep_b_s, back_ref,
    token_sems, weight_sems, out_sems,
):
    place = read_place(place_ref)
    frames, clips, positions, width = tokens_s.shape
    clips = clips // 2
    halves = positions // 8
    part = frames * 8
    gain = gain_ref[...]
    bias = bias_ref[...]

    def load_tokens(q):
        pair = pl.ds(2 * q, 2)
        return pltpu.make_async_copy(tokens_hbm.at[pair], tokens_s.at[pair], token_sems.at[q])

    def load_wqkv(n):
        return pltpu.make_async_copy(wqkv_hbm.at[:, chunk(n)], wqkv_s.at[:, chunk(n)], weight_sems.at[n])

    blocks = 3 * width // CHUNK
    load_wout = pltpu.make_async_copy(wout_hbm, wout_s, weight_sems.at[blocks])
    for q in range(frames // 2):
        load_tokens(q).start()
    for n in range(blocks):
        load_wqkv(n).start()
    load_wout.start()

    def norm_step(q, carry):
        load_tokens(q).wait()
        for c in range(clips):
            x = tokens_s[pl.ds(2 * q, 2), c].astype(F32).reshape(2, halves, 8, width)
            g = tokens_s[pl.ds(2 * q, 2), clips + c].astype(F32).reshape(2, halves, 8, width)
            for hf in range(halves):
                at = pl.multiple_of((c * halves + hf) * part + q * 16, 16)
                wh, inv = whiten(x[:, hf].reshape(16, width))
                wh_s[pl.ds(at, 16), :] = wh
                inv_s[pl.ds(at, 16), :] = jnp.broadcast_to(inv, (16, 128))
                normed_s[pl.ds(at, 16), :] = (wh * gain + bias).astype(BF16)
                right_s[pl.ds(at, 16), pl.ds(3 * width, width)] = g[:, hf].reshape(16, width).astype(BF16)
        return carry

    lax.fori_loop(0, frames // 2, norm_step, 0, unroll=2)

    def qkv_step(n, carry):
        for i in range(2):
            load_wqkv(2 * n + i).wait()
        for i in range(2):
            cols = chunk(2 * n + i)
            packed_s[:, cols] = dot_nn(normed_s[...], wqkv_s[:, cols]).astype(BF16)
        return carry

    lax.fori_loop(0, blocks // 2, qkv_step, 0)
    load_wout.wait()

    for n in range(width // CHUNK):
        cols = slice(n * CHUNK, (n + 1) * CHUNK)
        datt_s[:, cols] = dot_nt(right_s[:, 3 * width:], wout_s[cols, :]).astype(BF16)
        turned = normed_s[:, cols].T
        for b in range(CHUNK // 64):
            at = block_row(n * (CHUNK // 64) + b, place)
            left_s[0, pl.ds(at, 64), :] = turned[b * 64:(b + 1) * 64]

    lane = lax.broadcasted_iota(jnp.int32, (part, 128), 1)
    first = lane < 64
    same = lax.broadcasted_iota(jnp.int32, (1, 8, part), 1) == (
        lax.broadcasted_iota(jnp.int32, (1, 8, part), 2) % 8
    )
    zero = jnp.zeros((part, 128), BF16)
    scale = jnp.asarray(0.125, BF16)

    def split(a):
        return jnp.concatenate([jnp.where(first, a, zero), jnp.where(first, zero, a)], axis=0)

    def attend_step(i, carry):
        t = i // (width // 128)
        hp = i % (width // 128)
        tok = pl.ds(pl.multiple_of(t * part, part), part)
        col = pl.multiple_of(hp * 128, 128)
        q = packed_s[tok, pl.ds(col, 128)]
        k = packed_s[tok, pl.ds(width + col, 128)]
        v = packed_s[tok, pl.ds(2 * width + col, 128)]
        da = datt_s[tok, pl.ds(col, 128)]
        k2 = split(k)
        v2 = split(v)
        scores = dot_nt(k2, q * scale).reshape(2, frames, 8, part)
        e = jnp.exp(scores - jnp.max(scores, axis=1, keepdims=True))
        probs = e * (1.0 / jnp.sum(e, axis=1, keepdims=True))
        probs = jnp.where(same[None], probs, 0.0)
        low = probs.astype(BF16).reshape(2, part, part)
        dp = dot_nt(v2, da * scale).reshape(2, frames, 8, part)
        inner = jnp.sum(dp * probs, axis=1, keepdims=True)
        ds = (probs * (dp - inner)).astype(BF16).reshape(2, part, part)
        attended = dot_tn(v2, low.reshape(2 * part, part)).astype(BF16)
        for b in range(2):
            left_s[1, pl.ds(block_row(hp * 2 + b, place), 64), tok] = attended[b * 64:(b + 1) * 64]
        right_s[tok, pl.ds(col, 128)] = dot_tn(ds.reshape(2 * part, part), k2).astype(BF16)
        right_s[tok, pl.ds(width + col, 128)] = dot_nn(
            jnp.concatenate([ds[0], ds[1]], axis=1), split(q)
        ).astype(BF16)
        right_s[tok, pl.ds(2 * width + col, 128)] = dot_nn(
            jnp.concatenate([low[0], low[1]], axis=1), split(da)
        ).astype(BF16)
        return carry

    lax.fori_loop(0, clips * halves * (width // 128), attend_step, 0, unroll=8)

    half = width // 2
    copies = []

    def write(src, dst):
        copies.append(pltpu.make_async_copy(src, dst, out_sems.at[len(copies)]))
        copies[-1].start()

    for k in range(4):
        block = (place[0] + k) % 4
        lanes = slice(k * 384, k * 384 + 128)
        rhs = right_s[:, pl.ds(pl.multiple_of(2560 + block * 128, 128), 128)]
        send_a_s[:, :, lanes] = dot_nn(left_s[0, half:, :], rhs).reshape(8, 64, 128).astype(BF16)
        keep_a_s[:, :, lanes] = dot_nn(left_s[0, :half, :], rhs).reshape(8, 64, 128)
        lanes = slice(k * 384 + 128, k * 384 + 384)
        rhs = right_s[:, pl.ds(pl.multiple_of(3072 + block * 256, 256), 256)]
        send_a_s[:, :, lanes] = dot_nn(left_s[1, half:, :], rhs).reshape(8, 64, 256).astype(BF16)
        keep_a_s[:, :, lanes] = dot_nn(left_s[1, :half, :], rhs).reshape(8, 64, 256)
    write(send_a_s, send_a_hbm)
    for k in range(4):
        block = (place[0] + k) % 4
        rhs = right_s[:, pl.ds(pl.multiple_of(block * 640, 128), 640)]
        send_b_s[k] = dot_nn(left_s[0, half:, :], rhs).reshape(8, 64, 640).astype(BF16)
        write(send_b_s.at[k], send_b_hbm.at[k])
        keep_b_s[k] = dot_nn(left_s[0, :half, :], rhs).reshape(8, 64, 640)
        write(keep_b_s.at[k], keep_b_hbm.at[k])
    write(keep_a_s, keep_a_hbm)

    for n in range(width // CHUNK):
        cols = slice(n * CHUNK, (n + 1) * CHUNK)
        dn_s[:, cols] = dot_nt(right_s[:, :3 * width], wqkv_s[cols, :])

    def back_step(i, carry):
        dgain, dbias = carry
        c = i // (frames // 2)
        q = i % (frames // 2)
        outs = []
        for hf in range(halves):
            at = pl.multiple_of((c * halves + hf) * part + q * 16, 16)
            dn = dn_s[pl.ds(at, 16), :]
            wh = wh_s[pl.ds(at, 16), :]
            inv = inv_s[pl.ds(at, 16), :][:, :1]
            dw = dn * wh
            dgain = dgain + dw[:8] + dw[8:]
            dbias = dbias + dn[:8] + dn[8:]
            scaled = dn * gain
            m1 = jnp.mean(scaled, axis=-1, keepdims=True)
            m2 = jnp.mean(scaled * wh, axis=-1, keepdims=True)
            g = right_s[pl.ds(at, 16), pl.ds(3 * width, width)].astype(F32)
            outs.append((g + inv * (scaled - m1 - wh * m2)).reshape(2, 8, width))
        grads = jnp.concatenate(outs, axis=1).astype(BF16)
        at = pl.ds(pl.multiple_of(c * positions, positions), positions)
        for f in range(2):
            back_ref[(f - place[1]) % 2, q, at, :width] = grads[f]
        return dgain, dbias

    zeros = jnp.zeros((8, width), F32)
    dgain, dbias = lax.fori_loop(0, clips * frames // 2, back_step, (zeros, zeros), unroll=2)
    dgain = jnp.sum(dgain, axis=0, keepdims=True)
    dbias = jnp.sum(dbias, axis=0, keepdims=True)
    lane = lax.broadcasted_iota(jnp.int32, (1, 128), 1)
    row = lax.broadcasted_iota(jnp.int32, (16, 128), 0)
    back_ref[:, :, 16:, width:] = jnp.zeros((2, 8, clips * positions - 16, 128), BF16)
    for f in range(frames):
        at = f // 2 * 128
        a = dgain[:, at:at + 128]
        b = dbias[:, at:at + 128]
        if f % 2 == 0:
            b = jnp.concatenate([b[:, 64:], b[:, :64]], axis=1)
        else:
            a = jnp.concatenate([a[:, 64:], a[:, :64]], axis=1)
        both = jnp.where(lane < 64, a, b)
        hi = both.astype(BF16).astype(F32)
        mid = (both - hi).astype(BF16).astype(F32)
        low = both - hi - mid
        terms = jnp.where(row == 0, hi, jnp.where(row == 1, mid, jnp.where(row == 2, low, 0.0)))
        back_ref[(f % 2 - place[1]) % 2, f // 2, :16, width:] = terms.astype(BF16)
    write(back_ref.at[1], theirs_hbm)
    write(back_ref.at[0], back_hbm)
    for copy in copies:
        copy.wait()


def run_main(place, tokens, gain, bias, wqkv, wout):
    frames, clips, positions, width = tokens.shape
    clips = clips // 2
    rows = clips * frames * positions
    vm = pl.BlockSpec(memory_space=pltpu.VMEM)
    hbm = pl.BlockSpec(memory_space=pl.ANY)
    a, b = (8, 64, 1536), (4, 8, 64, 640)
    back = (frames // 2, clips * positions, width + 128)
    return pl.pallas_call(
        main_kernel,
        out_shape=(
            jax.ShapeDtypeStruct(back, BF16),
            jax.ShapeDtypeStruct(back, BF16),
            jax.ShapeDtypeStruct(a, BF16),
            jax.ShapeDtypeStruct(b, BF16),
            jax.ShapeDtypeStruct(a, F32),
            jax.ShapeDtypeStruct(b, F32),
        ),
        in_specs=[pl.BlockSpec(memory_space=pltpu.SMEM), hbm, vm, vm, hbm, hbm],
        out_specs=(hbm,) * 6,
        scratch_shapes=[
            pltpu.VMEM(tokens.shape, BF16),
            pltpu.VMEM(wqkv.shape, BF16),
            pltpu.VMEM(wout.shape, BF16),
            pltpu.VMEM((2, width, rows), BF16),
            pltpu.VMEM((rows, 4 * width), BF16),
            pltpu.VMEM((rows, width), BF16),
            pltpu.VMEM((rows, 3 * width), BF16),
            pltpu.VMEM((rows, width), BF16),
            pltpu.VMEM((rows, width), F32),
            pltpu.VMEM((rows, 128), F32),
            pltpu.VMEM((rows, width), F32),
            pltpu.VMEM(a, BF16),
            pltpu.VMEM(b, BF16),
            pltpu.VMEM(a, F32),
            pltpu.VMEM(b, F32),
            pltpu.VMEM((2,) + back, BF16),
            pltpu.SemaphoreType.DMA((frames // 2,)),
            pltpu.SemaphoreType.DMA((3 * width // CHUNK + 1,)),
            pltpu.SemaphoreType.DMA((12,)),
        ],
        compiler_params=pltpu.CompilerParams(vmem_limit_bytes=63 * MIB),
        cost_estimate=pl.CostEstimate(flops=12 * 1024**3, bytes_accessed=20 * MIB, transcendentals=MIB),
        name="sublayer",
    )(place, tokens, gain, bias, wqkv, wout)


def message_kernel(place_ref, keep_ref, got_ref, back_ref, theirs_ref, own_ref, message_ref):
    message_ref[:, :32, 1536:] = back_ref[...]
    message_ref[:, 32:, 1536:] = theirs_ref[...]
    for i in range(4):
        g = keep_ref[i] + got_ref[i].astype(F32)
        message_ref[i, :, :1536] = g.astype(BF16)

        @pl.when(pl.program_id(0) * 4 + i == place_ref[2])
        def _():
            own_ref[...] = g


def step_call(kernel, name, in_blocks, outs):
    def spec(shape):
        if len(shape) == 2:
            return pl.BlockSpec(shape, lambda k, place: (0, 0))
        return pl.BlockSpec((4,) + shape[1:], lambda k, place: (k, 0, 0))

    return pl.pallas_call(
        kernel,
        grid_spec=pltpu.PrefetchScalarGridSpec(
            num_scalar_prefetch=1,
            grid=(2,),
            in_specs=[spec(shape) for shape in in_blocks],
            out_specs=tuple(spec(shape) for shape, _ in outs),
        ),
        out_shape=tuple(jax.ShapeDtypeStruct(shape, dtype) for shape, dtype in outs),
        compiler_params=pltpu.CompilerParams(vmem_limit_bytes=63 * MIB),
        cost_estimate=pl.CostEstimate(flops=MIB, bytes_accessed=9 * MIB, transcendentals=0),
        name=name,
    )


def run_message(place, keep, got, back, theirs):
    ins = [keep.shape, got.shape, back.shape, theirs.shape]
    outs = [((64, 1536), F32), ((8, 64, 1536 + back.shape[2]), BF16)]
    return step_call(message_kernel, "message", ins, outs)(place, keep, got, back, theirs)


def sum_kernel(place_ref, keep_ref, t1, t2, t3, own_ref, total_ref):
    for i in range(4):
        g = keep_ref[i] + t1[i].astype(F32) + t2[i].astype(F32) + t3[i].astype(F32)
        total_ref[i] = g.astype(BF16)

        @pl.when(pl.program_id(0) * 4 + i == place_ref[2])
        def _():
            own_ref[...] = g


def run_sum(place, keep, got):
    ins = [keep.shape] * 4
    outs = [(keep.shape[1:], F32), (keep.shape, BF16)]
    return step_call(sum_kernel, "sum_b", ins, outs)(place, keep, *got)


def unpack_kernel(place_ref, message_ref, out_ref):
    clips, rows, width = out_ref.shape
    for i in range(rows // 32):
        for which in range(2):
            at = pl.multiple_of(i * 32 + (which + place_ref[1]) % 2 * 16, 16)
            for c in range(clips):
                row = which * 32 + c * 16
                out_ref[c, pl.ds(at, 16), :] = message_ref[i, row:row + 16, 1536:1536 + width]


def run_unpack(place, message, clips, width):
    return pl.pallas_call(
        unpack_kernel,
        grid_spec=pltpu.PrefetchScalarGridSpec(
            num_scalar_prefetch=1,
            grid=(2,),
            in_specs=[pl.BlockSpec((4,) + message.shape[1:], lambda k, place: (k, 0, 0))],
            out_specs=pl.BlockSpec((clips, 128, width), lambda k, place: (0, k, 0)),
        ),
        out_shape=jax.ShapeDtypeStruct((clips, 256, width), BF16),
        compiler_params=pltpu.CompilerParams(vmem_limit_bytes=63 * MIB),
        name="unpack",
    )(place, message)


def pack_kernel(video_ref, cot_ref, out_ref, packed_s, sems):
    clips = video_ref.shape[0]
    loads = []
    for c in range(clips):
        loads.append(pltpu.make_async_copy(video_ref.at[c], packed_s.at[:, c], sems.at[2 * c]))
        loads.append(pltpu.make_async_copy(cot_ref.at[c], packed_s.at[:, clips + c], sems.at[2 * c + 1]))
    for load in loads:
        load.start()
    for load in loads:
        load.wait()
    store = pltpu.make_async_copy(packed_s, out_ref, sems.at[2 * clips])
    store.start()
    store.wait()


def run_pack(video, cotangent):
    clips, _, positions, width = video.shape
    shape = (clips, 16, positions // 16, width)
    packed = (16, 2 * clips, positions // 16, width)
    hbm = pl.BlockSpec(memory_space=pl.ANY)
    return pl.pallas_call(
        pack_kernel,
        in_specs=[hbm, hbm],
        out_specs=hbm,
        out_shape=jax.ShapeDtypeStruct(packed, BF16),
        scratch_shapes=[pltpu.VMEM(packed, BF16), pltpu.SemaphoreType.DMA((2 * clips + 1,))],
        compiler_params=pltpu.CompilerParams(vmem_limit_bytes=63 * MIB),
        name="pack",
    )(video.reshape(shape), cotangent.reshape(shape))


def terms_kernel(keep_ref, got_ref, own_ref, *term_refs):
    own_ref[...] = keep_ref[0] + got_ref[0].astype(F32)
    for i, term_ref in enumerate(term_refs):
        term_ref[...] = (keep_ref[i + 1] + got_ref[i + 1].astype(F32)).astype(BF16)


def run_terms(keep, got):
    shape = keep.shape[1:]
    ins = pl.BlockSpec((4, 4) + shape[1:], lambda k: (0, k, 0, 0))
    out = pl.BlockSpec((4,) + shape[1:], lambda k: (k, 0, 0))
    return pl.pallas_call(
        terms_kernel,
        grid=(2,),
        in_specs=[ins, ins],
        out_specs=(out,) * 4,
        out_shape=tuple(jax.ShapeDtypeStruct(shape, dtype) for dtype in (F32, BF16, BF16, BF16)),
        compiler_params=pltpu.CompilerParams(vmem_limit_bytes=63 * MIB),
        cost_estimate=pl.CostEstimate(flops=MIB, bytes_accessed=11 * MIB, transcendentals=0),
        name="terms_b",
    )(keep, got)


def place_kernel(scale, place_ref, d0, d1, d2, d3, qkv_ref, out_ref, gain_ref, bias_ref):
    small = jnp.zeros((8, 128), F32)
    for j, d in enumerate((d0, d1, d2, d3)):
        block = (place_ref[0] - j) % 4
        qkv_ref[:, pl.ds(pl.multiple_of(block * 640, 128), 640)] = d[:, :640] * scale
        qkv_ref[:, pl.ds(pl.multiple_of(2560 + block * 128, 128), 128)] = d[:, 640:768] * scale
        out_ref[:, pl.ds(pl.multiple_of(block * 256, 256), 256)] = d[:, 768:1024] * scale
        small = small + d[:8, 1024:]
    small = jnp.sum(small, axis=0, keepdims=True) * scale
    gain_ref[...] = small[:, :64]
    bias_ref[...] = small[:, 64:]


def run_place(place, scale, pieces):
    vm = pl.BlockSpec(memory_space=pltpu.VMEM)
    return pl.pallas_call(
        functools.partial(place_kernel, scale),
        out_shape=(
            jax.ShapeDtypeStruct((64, 3072), F32),
            jax.ShapeDtypeStruct((64, 1024), F32),
            jax.ShapeDtypeStruct((1, 64), F32),
            jax.ShapeDtypeStruct((1, 64), F32),
        ),
        in_specs=[pl.BlockSpec(memory_space=pltpu.SMEM)] + [vm] * 4,
        out_specs=(vm,) * 4,
        compiler_params=pltpu.CompilerParams(vmem_limit_bytes=8 * MIB),
        name="place_grads",
    )(place, *pieces)


def frame_pairs(move):
    pairs = []
    for i in range(16):
        y, z, core = move(i // 4, i // 2 % 2, i % 2)
        pairs.append((i, y % 4 * 4 + z % 2 * 2 + core % 2))
    return pairs


def dp_pairs(move):
    pairs = []
    for i in range(16):
        x, h = move(i // 4, i % 4)
        pairs.append((i, x % 4 * 4 + h % 4))
    return pairs


def go_core(a):
    return lax.ppermute(a, "frame", frame_pairs(lambda y, z, c: (y, z, c + 1)))


def trade_yz(a):
    groups = [[2 * i + core for i in range(8)] for core in range(2)]
    return lax.all_to_all(a, "frame", 0, 0, tiled=True, axis_index_groups=groups)


def go_x(a, k):
    return lax.ppermute(a, "dp", dp_pairs(lambda x, h: (x + k, h)))


def go_h(a, k):
    return lax.ppermute(a, "dp", dp_pairs(lambda x, h: (x, h + k)))


def combine(own, got):
    for part in got:
        own = own + part.astype(F32)
    return own


def exchange(pieces, go):
    return [go(pieces[k], k) for k in range(1, 4)]


def pick(array, index):
    return lax.dynamic_index_in_dim(array, index, 0, keepdims=False)


def reduce_yz(own, got, yz):
    mine = (jnp.arange(8) == yz).reshape((8,) + (1,) * own.ndim)
    return jnp.sum(jnp.where(mine, own[None], got.astype(F32)), axis=0)


def three_terms(value):
    hi = lax.reduce_precision(value, 8, 7)
    mid = lax.reduce_precision(value - hi, 8, 7)
    return jnp.pad(jnp.concatenate([hi, mid, value - hi - mid], axis=0), ((0, 61), (0, 0)))


def local(video, cotangent, norm_gain, norm_bias, qkv_weight, out_weight):
    clips, frames_here, positions, width = video.shape
    grad_scale = 1.0 / math.sqrt(clips * positions * 256)
    frame = lax.axis_index("frame")
    dp = lax.axis_index("dp")
    yz, core = frame // 2, frame % 2
    place = jnp.stack([dp // 4, core, yz]).astype(jnp.int32)
    gain = norm_gain.reshape(1, width)
    bias = norm_bias.reshape(1, width)
    tokens = lax.all_to_all(run_pack(video, cotangent), "frame", 0, 0, tiled=True)
    back, theirs, send_a, send_b, keep_a, keep_b = run_main(
        place, tokens, gain, bias, qkv_weight, out_weight
    )

    got_a = go_core(send_a)
    got_a, theirs, send_b = lax.optimization_barrier((got_a, go_core(theirs), send_b))
    got_b = go_core(send_b)
    own_a, message = run_message(place, keep_a, got_a, back, theirs)
    terms_b = run_terms(keep_b, got_b)
    message, terms_b = lax.optimization_barrier((message, terms_b))
    message = trade_yz(message)
    got_b = exchange(terms_b, go_x)
    message, got_b = lax.optimization_barrier((message, got_b))

    own_b, total_b = run_sum(place, terms_b[0], got_b)
    got_b = trade_yz(total_b)
    a = reduce_yz(own_a, message[:, :, :1536], yz)
    terms_a = [a[:, k * 384 : (k + 1) * 384] for k in range(4)]
    got_a = exchange([t.astype(BF16) for t in terms_a], go_x)
    small = jnp.sum(message[:, :, 1536 + width :].astype(F32), axis=(0, 1)).reshape(1, 128)
    terms = three_terms(small)
    message, terms, got_a, got_b = lax.optimization_barrier((message, terms, got_a, got_b))

    a = combine(terms_a[0], got_a)
    b = reduce_yz(own_b, got_b, yz)
    own = jnp.concatenate([b, a, terms], axis=1)
    own = combine(own, exchange([own.astype(BF16)] * 4, go_h))
    pieces = [own] + exchange([own] * 4, go_x)

    grad_video = run_unpack(place, message, clips, width).reshape(video.shape)
    pieces, grad_video = lax.optimization_barrier((pieces, grad_video))
    grad_qkv, grad_out, total_gain, total_bias = run_place(place, grad_scale, pieces)
    return grad_video, grad_qkv, grad_out, total_gain.reshape(64), total_bias.reshape(64)


def solution(mesh):
    in_specs = (P("dp", "frame", None, None), P("dp", "frame", None, None), P(), P(), P(), P())
    out_specs = (
        P("dp", "frame", None, None),
        P("frame", None),
        P("frame", None),
        P("frame"),
        P("frame"),
    )
    return jax.shard_map(local, mesh=mesh, in_specs=in_specs, out_specs=out_specs, check_vma=False)
```
